512 devices in a mesh: gx: 32 (over z, core), gy: 16 (over x, y).
Axes of the slice: x: 4, y: 4, z: 16, core: 2. Of those that a mesh axis runs over, the one named last changes fastest.
Arguments:
- right_side: float32 [512, 256, 128], P('gx', 'gy'), may hold values from -96 to 96
- alpha_cells: float32 [512, 256, 128], P('gx', 'gy'), may hold values from 0.05 to 0.5
- beta_x: float32 [512, 256, 128], P('gx', 'gy'), may hold values from 0.5 to 2
- beta_y: float32 [512, 256, 128], P('gx', 'gy'), may hold values from 0.5 to 2
- beta_z: float32 [512, 256, 128], P('gx', 'gy'), may hold values from 0.5 to 2
Outputs:
- smooth_fine: float32 [512, 256, 128], P('gx', 'gy')
- smooth_one: float32 [256, 128, 64], P('gx', 'gy')
- bottom: float32 [128, 64, 32], P('gx', 'gy')
The draws below stay inside these ranges and needn't reach their ends.
All inputs are finite; a program needn't handle non-finite values.
Results may differ from the reference program's by a relative error of at most 0.0003.
Values sent between devices are 32-bit elements; how exact they have to be, the bound alone decides.
A program may use at most 64 MiB of HBM per device.

```python
import math
import jax
import jax.numpy as jnp
from jax import lax

NZ = 128
BICG = 2
NX = 512
NY = 256


def block_levels(own_key, dims, shards, low, top_value):
    level = 1.0
    for position, parts in shards:
        draws = jax.random.uniform(jax.random.fold_in(jax.random.fold_in(own_key, 6), position), (parts,), jnp.float32, low / len(shards), top_value / len(shards))
        level = level * jnp.repeat(jnp.exp(draws), dims[position] // parts).reshape((-1,) + (1,) * (len(dims) - 1 - position))
    return level


def centred(key, extent, width, limit, shards=(), kind=jnp.bfloat16):
    drawn = jax.random.normal(key, extent, jnp.float32) * width
    if len(shards) > 0:
        drawn = block_levels(key, extent, shards, -0.22, 0.18) * drawn
    return jnp.clip(drawn, min=-limit, max=limit).astype(kind)


def setup_inputs(seed: int = 0) -> dict:
    arg_keys = jax.random.split(jax.random.key(seed), 6)
    return {
        "right_side": centred(arg_keys[0], (NX, NY, NZ), 16.0, 96.0, ((0, 32), (1, 16)), jnp.float32),
        "alpha_cells": jnp.clip(jnp.exp(math.log(0.5) - 2.3025851 * jax.random.uniform(arg_keys[1], (NX, NY, NZ), jnp.float32) ** block_levels(arg_keys[1], (NX, NY, NZ), ((0, 32), (1, 16)), -0.2, 0.2)), 0.05, 0.5),
        "beta_x": jnp.clip(jnp.exp(math.log(2.0) - 1.3862944 * jax.random.uniform(arg_keys[2], (NX, NY, NZ), jnp.float32) ** block_levels(arg_keys[2], (NX, NY, NZ), ((0, 32), (1, 16)), -0.2, 0.2)), 0.5, 2.0),
        "beta_y": jnp.clip(jnp.exp(math.log(2.0) - 1.3862944 * jax.random.uniform(arg_keys[3], (NX, NY, NZ), jnp.float32) ** block_levels(arg_keys[3], (NX, NY, NZ), ((0, 32), (1, 16)), -0.2, 0.2)), 0.5, 2.0),
        "beta_z": jnp.clip(jnp.exp(math.log(2.0) - 1.3862944 * jax.random.uniform(arg_keys[4], (NX, NY, NZ), jnp.float32) ** block_levels(arg_keys[4], (NX, NY, NZ), ((0, 32), (1, 16)), -0.2, 0.2)), 0.5, 2.0),
    }


LMAX = 2.0
LMIN = 0.25


def next_face(coeff, axis):
    count = coeff.shape[axis]
    head = lax.slice_in_dim(coeff, 1, count, axis=axis)
    tail = jnp.zeros_like(lax.slice_in_dim(coeff, 0, 1, axis=axis))
    return jnp.concatenate([head, tail], axis)


def combine(padded, alpha, faces, scale):
    bx, by, bz, bxu, byu, bzu = faces
    field = padded[1:-1, 1:-1, 1:-1]
    flux = bxu * (padded[2:, 1:-1, 1:-1] - field) - bx * (field - padded[:-2, 1:-1, 1:-1])
    flux = flux + byu * (padded[1:-1, 2:, 1:-1] - field) - by * (field - padded[1:-1, :-2, 1:-1])
    flux = flux + bzu * (padded[1:-1, 1:-1, 2:] - field) - bz * (field - padded[1:-1, 1:-1, :-2])
    return alpha * field - scale * flux


def chebyshev(rhs, alpha, faces, scale, apply):
    bx, by, bz, bxu, byu, bzu = faces
    inverse = 1.0 / (alpha + scale * (bx + bxu + by + byu + bz + bzu))
    theta = 0.5 * (LMAX + LMIN)
    delta = 0.5 * (LMAX - LMIN)
    sigma = theta / delta
    rho = 1.0 / sigma
    update = inverse * rhs / theta
    solved = update
    for sweep in range(3):
        resid = rhs - apply(solved)
        rho_next = 1.0 / (2.0 * sigma - rho)
        update = (rho_next * rho) * update + (2.0 * rho_next / delta) * (inverse * resid)
        solved = solved + update
        rho = rho_next
    resid = rhs - apply(solved)
    return solved, resid


def restrict_cells(values):
    a, b, c = values.shape
    return values.reshape(a // 2, 2, b // 2, 2, c // 2, 2).mean(axis=(1, 3, 5))


def restrict_faces(bx, by, bz):
    a, b, c = bx.shape
    coarse_x = bx[0::2].reshape(a // 2, b // 2, 2, c // 2, 2).mean(axis=(2, 4))
    coarse_y = by[:, 0::2].reshape(a // 2, 2, b // 2, c // 2, 2).mean(axis=(1, 4))
    coarse_z = bz[:, :, 0::2].reshape(a // 2, 2, b // 2, 2, c // 2).mean(axis=(1, 3))
    return coarse_x, coarse_y, coarse_z


def bicgstab(rhs, apply):
    solved = jnp.zeros_like(rhs)
    resid = rhs
    shadow = rhs
    direction = rhs
    rho = jnp.sum(shadow * resid)
    for sweep in range(BICG):
        image = apply(direction)
        step = rho / jnp.sum(shadow * image)
        half = resid - step * image
        turned = apply(half)
        omega = jnp.sum(turned * half) / jnp.sum(turned * turned)
        solved = solved + step * direction + omega * half
        resid = half - omega * turned
        rho_next = jnp.sum(shadow * resid)
        factor = (rho_next / rho) * (step / omega)
        direction = resid + factor * (direction - omega * image)
        rho = rho_next
    return solved


def level_faces(bx, by, bz):
    return (bx, by, bz, next_face(bx, 0), next_face(by, 1), next_face(bz, 2))


def partial_apply(alpha, faces, scale):
    def apply(field):
        return combine(jnp.pad(field, 1), alpha, faces, scale)
    return apply


def reference(right_side, alpha_cells, beta_x, beta_y, beta_z):
    rhs, alpha, bx, by, bz = right_side, alpha_cells, beta_x, beta_y, beta_z
    scale = 16.0
    smoothed = []
    for level in range(2):
        faces = level_faces(bx, by, bz)
        apply = partial_apply(alpha, faces, scale)
        solved, resid = chebyshev(rhs, alpha, faces, scale, apply)
        smoothed.append(solved)
        rhs = restrict_cells(resid)
        alpha = restrict_cells(alpha)
        bx, by, bz = restrict_faces(bx, by, bz)
        scale = scale * 0.25
    faces = level_faces(bx, by, bz)
    bottom = bicgstab(rhs, partial_apply(alpha, faces, scale))
    return smoothed[0], smoothed[1], bottom
```

```python
import jax
import jax.numpy as jnp
from jax import lax
from jax.experimental import pallas as pl
from jax.experimental.pallas import tpu as pltpu
from jax.sharding import PartitionSpec as P

MESH = pl.DeviceIdType.MESH
F32 = jnp.float32

BICG = 2
LMAX = 2.0
LMIN = 0.25
THETA = 0.5 * (LMAX + LMIN)
DELTA = 0.5 * (LMAX - LMIN)
SIGMA = THETA / DELTA

HALO = 4
LANES = 128
DIRECTIONS = ((1, 1), (1, -1), (-1, 1), (-1, -1), (0, 1), (0, -1), (1, 0), (-1, 0))
SHRINK = 0.125


def steps():
    rho = 1.0 / SIGMA
    out = []
    for _ in range(3):
        rho_next = 1.0 / (2.0 * SIGMA - rho)
        out.append((rho_next * rho, 2.0 * rho_next / DELTA))
        rho = rho_next
    return out


def lane_of(shape):
    return lax.broadcasted_iota(jnp.int32, shape, len(shape) - 1)


def roll(value, shift, axis):
    extent = value.shape[axis]
    return pltpu.roll(value, shift % extent, axis)


def spans(offset, own):
    if offset == 1:
        return pl.ds(own, HALO), pl.ds(0, HALO)
    if offset == -1:
        return pl.ds(HALO, HALO), pl.ds(own + HALO, HALO)
    return pl.ds(HALO, own), pl.ds(HALO, own)


def kernel(
    nx, ny,
    rhs_hbm, alpha_hbm, bx_hbm, by_hbm, bz_hbm,
    fine_hbm, one_ref, bottom_ref,
    raw, ext0, work0, pair0,
    raw1, packed1, coef1, work1, rhs1, pair1,
    packed2, coef2, basis,
    gather_y, gather_x,
    load_sem, out_sem, send_sem, recv_sem, ysend, yrecv, xsend, xrecv,
):
    gx = lax.axis_index("gx")
    gy = lax.axis_index("gy")
    n0, n1, n2 = raw.shape[1], raw1.shape[1], raw1.shape[1] // 2

    loads = [
        pltpu.make_async_copy(src, raw.at[i], load_sem.at[i])
        for i, src in enumerate((rhs_hbm, alpha_hbm, bx_hbm, by_hbm, bz_hbm))
    ]
    for copy in loads:
        copy.start()

    def has(dx, dy):
        ok = None
        for step, at, count in ((dx, gx, nx), (dy, gy, ny)):
            if step != 0:
                this = at < count - 1 if step > 0 else at > 0
                ok = this if ok is None else jnp.logical_and(ok, this)
        return ok

    barrier = pltpu.get_barrier_semaphore()
    greeted = jnp.int32(nx - 1 + ny - 1)
    for dx, dy in DIRECTIONS[:4]:
        there = has(dx, dy)
        greeted = greeted + there.astype(jnp.int32)

        @pl.when(there)
        def _(dx=dx, dy=dy):
            pl.semaphore_signal(barrier, inc=1, device_id=(gx + dx, gy + dy), device_id_type=MESH)

    def peer_y(o):
        return (gx, lax.rem(gy + o, ny))

    def peer_x(o):
        return (lax.rem(gx + o, nx), gy)

    for o in range(1, nx):
        pl.semaphore_signal(barrier, inc=1, device_id=peer_x(o), device_id_type=MESH)
    for o in range(1, ny):
        pl.semaphore_signal(barrier, inc=1, device_id=peer_y(o), device_id_type=MESH)

    def exchange(which, ref, own, lead):
        out = []
        for j, (dx, dy) in enumerate(DIRECTIONS):
            (sx, tx), (sy, ty) = spans(dx, own), spans(dy, own)
            src, dst = (ref.at[:, sx, sy], ref.at[:, tx, ty]) if lead else (ref.at[sx, sy], ref.at[tx, ty])
            copy = pltpu.make_async_remote_copy(
                src, dst, send_sem.at[which, j], recv_sem.at[which, j],
                device_id=(gx + dx, gy + dy), device_id_type=MESH,
            )
            out.append((copy, has(dx, dy), has(-dx, -dy)))
        return out

    def start(copies):
        for copy, to, _ in copies:
            pl.when(to)(copy.start)

    def arrive(copies):
        for copy, _, of in copies:
            pl.when(of)(copy.wait_recv)

    def leave(copies):
        for copy, to, _ in copies:
            pl.when(to)(copy.wait_send)

    x_inner = jnp.where(gx > 0, 1.0, 0.0).astype(F32)

    def own_coefs(alpha, bx, by, bz, scale, width):
        n = bx.shape[0]
        col = lax.broadcasted_iota(jnp.int32, bx.shape, 1)
        bz_in = jnp.where(lane_of(bx.shape) < width, 0.0, bz)
        bxu = jnp.concatenate([bx[1:], jnp.zeros_like(bx[:1])], 0)
        byu = jnp.where(col == n - 1, 0.0, roll(by, -1, 1))
        diag = alpha + scale * (bx + bxu + by + byu + bz + roll(bz_in, -width, 2))
        by_in = jnp.where(jnp.logical_and(col == 0, gy == 0), 0.0, by)
        bx_in = jnp.concatenate([bx[:1] * x_inner, bx[1:]], 0)
        return diag, bx_in, by_in, bz_in

    for copy in loads:
        copy.wait()

    own = pl.ds(HALO, n0)
    diag, bx_in, by_in, bz_in = own_coefs(raw[1], raw[2], raw[3], raw[4], 16.0, 1)
    for i, v in enumerate((raw[0], diag, bx_in, by_in, bz_in)):
        ext0[i, own, own, :] = v

    pl.semaphore_wait(barrier, greeted)
    sent0 = exchange(0, ext0, n0, True)
    start(sent0)

    def halves(ref, n):
        return ref[:, pl.ds(0, n, stride=2), :], ref[:, pl.ds(1, n, stride=2), :]

    def coarsen(alpha, bx, by, bz, pairs, width):
        n = bx.shape[0] // 2

        def xs(v):
            w = v.reshape((n, 2) + v.shape[1:])
            return w[:, 0], w[:, 1]

        def zsum(v):
            return v + roll(v, -width, 2)

        pairs[0, :, pl.ds(0, 2 * n)] = zsum(sum(xs(alpha)))
        pairs[1, :, pl.ds(0, 2 * n)] = zsum(xs(bx)[0])
        pairs[2, :, pl.ds(0, 2 * n)] = zsum(sum(xs(by)))
        pairs[3, :, pl.ds(0, 2 * n)] = sum(xs(bz))
        a0, a1 = halves(pairs.at[0], n)
        x0, x1 = halves(pairs.at[1], n)
        y0, _ = halves(pairs.at[2], n)
        z0, z1 = halves(pairs.at[3], n)
        return (a0 + a1) * 0.125, (x0 + x1) * 0.25, y0 * 0.25, (z0 + z1) * 0.25

    alpha1, bx1, by1, bz1 = coarsen(raw[1], raw[2], raw[3], raw[4], pair0, 1)
    diag, bx_in, by_in, bz_in = own_coefs(alpha1, bx1, by1, bz1, 4.0, 2)
    own = pl.ds(HALO, n1)
    lane = lane_of(diag.shape)
    packed1[0, own, own, :] = jnp.where(lane % 2 == 0, diag, roll(bx_in, 1, 2))
    packed1[1, own, own, :] = jnp.where(lane % 2 == 0, by_in, roll(bz_in, 1, 2))
    sent1 = exchange(1, packed1, n1, True)
    start(sent1)

    alpha2, bx2, by2, bz2 = coarsen(alpha1, bx1, by1, bz1, pair1, 2)
    diag, bx_in, by_in, bz_in = own_coefs(alpha2, bx2, by2, bz2, 1.0, 4)
    own = pl.ds(HALO, n2)
    lane = lane_of(diag.shape) % 4
    mixed = jnp.where(lane < 2, jnp.where(lane == 0, diag, roll(bx_in, 1, 2)), jnp.where(lane == 2, roll(by_in, 2, 2), roll(bz_in, 3, 2)))
    packed2[own, own, :] = mixed
    sent2 = exchange(2, packed2, n2, False)
    start(sent2)

    def border(ref, index, n, value):
        for flag, at in ((gx == 0, 0), (gx == nx - 1, n + HALO)):

            @pl.when(flag)
            def _(at=at):
                ref[index + (pl.ds(at, HALO),)] = value((HALO, n + 2 * HALO, LANES))

        for flag, at in ((gy == 0, 0), (gy == ny - 1, n + HALO)):

            @pl.when(flag)
            def _(at=at):
                ref[index + (slice(None), pl.ds(at, HALO))] = value((n + 2 * HALO, HALO, LANES))

    def zeros(shape):
        return jnp.zeros(shape, F32)

    def ones(every):
        return lambda shape: jnp.where(lane_of(shape) % every == 0, 1.0, 0.0).astype(F32)

    for i in (0, 2, 3, 4):
        border(ext0, (i,), n0, zeros)
    border(ext0, (1,), n0, ones(1))
    border(packed1, (0,), n1, ones(2))
    border(packed1, (1,), n1, zeros)
    border(rhs1, (), n1, zeros)

    def border2(ref, value):
        for flag, at in ((gx == 0, 0), (gx == nx - 1, n2 + HALO)):

            @pl.when(flag)
            def _(at=at):
                ref[pl.ds(at, HALO)] = value((HALO,) + ref.shape[1:])

        for flag, at in ((gy == 0, 0), (gy == ny - 1, n2 + HALO)):

            @pl.when(flag)
            def _(at=at):
                ref[:, pl.ds(at, HALO)] = value((ref.shape[0], HALO, LANES))

    border2(packed2, ones(4))
    border2(basis.at[0], zeros)

    def whole_diag(part, bx, by, n, scale):
        rows = part.shape[0]
        row = lax.broadcasted_iota(jnp.int32, part.shape, 0)
        col = lax.broadcasted_iota(jnp.int32, part.shape, 1)
        at_x = jnp.logical_or(row == HALO - 1, row == HALO + n - 1)
        at_y = jnp.logical_or(col == HALO - 1, col == HALO + n - 1)
        bxu = jnp.concatenate([bx[1:rows], jnp.zeros_like(bx[:1])], 0)
        return part + scale * (jnp.where(at_x, bxu, 0.0) + jnp.where(at_y, roll(by, -1, 1), 0.0))

    def sweep(number, faces, work, n, width, finish):
        coefs = steps()
        first, last = number + 1, n + 2 * HALO - number - 1
        rows = {22: 2, 20: 4, 18: 6, 16: 4, 14: 7, 12: 6, 10: 5, 8: 4}[last - first]
        source, target = 6 + number % 2, 7 - number % 2

        def body(i, carry):
            at = first + i * rows
            here = pl.ds(at, rows)
            x = work[source, here]
            total = faces[0, here] * work[source, pl.ds(at - 1, rows)]
            total = total + faces[0, pl.ds(at + 1, rows)] * work[source, pl.ds(at + 1, rows)]
            total = total + faces[1, here] * roll(x, 1, 1) + work[2, here] * roll(x, -1, 1)
            total = total + faces[2, here] * roll(x, width, 2) + work[3, here] * roll(x, -width, 2)
            scaled = work[1, here] - x + work[0, here] * total
            if number == 3:
                finish(at, rows, work[4, here] * scaled)
            else:
                a, b = coefs[number]
                update = a * (x if number == 0 else work[5, here]) + b * scaled
                work[5, here] = update
                work[target, here] = x + update
            return carry

        lax.fori_loop(0, (last - first) // rows, body, 0)

    def smooth(faces, work, n, width, finish):
        for number in range(4):
            sweep(number, faces, work, n, width, finish)

    def prepare(faces, work, diag, scale, width):
        inverse = 1.0 / diag
        work[0] = scale * inverse
        work[2] = roll(faces[1], -1, 1)
        work[3] = roll(faces[2], -width, 2)
        work[4] = diag

    def begin(work, rhs, scale):
        work[1] = work[0] * rhs * (1.0 / scale)
        work[6] = work[1] * (1.0 / THETA)

    arrive(sent0)
    faces0 = ext0.at[pl.ds(2, 3)]
    prepare(faces0, work0, whole_diag(ext0[1], ext0[2], ext0[3], n0, 16.0), 16.0, 1)
    begin(work0, ext0[0], 16.0)

    def halve(pairs, width):
        def finish(at, rows, resid):
            summed = resid.reshape((rows // 2, 2) + resid.shape[1:])
            summed = summed[:, 0] + summed[:, 1]
            half = lax.div(at - HALO, 2)
            pairs[pl.ds(half, rows // 2)] = summed + roll(summed, -width, 2)

        return finish

    def restrict(pairs, n):
        even = pairs[:, pl.ds(HALO, n, stride=2), :]
        odd = pairs[:, pl.ds(HALO + 1, n, stride=2), :]
        return (even + odd) * 0.125

    down0 = pair0.at[4]
    smooth(faces0, work0, n0, 1, halve(down0, 1))
    own = pl.ds(HALO, n1)
    rhs1[own, own, :] = restrict(down0, n1)
    sent3 = exchange(3, rhs1, n1, False)
    start(sent3)

    own = pl.ds(HALO, n0)
    store = pltpu.make_async_copy(work0.at[7, own, own], fine_hbm, out_sem)
    store.start()

    arrive(sent1)
    even = lane_of(packed1.shape[1:]) % 2 == 0
    part = jnp.where(even, packed1[0], 1.0)
    coef1[0] = roll(packed1[0], -1, 2)
    coef1[1] = packed1[1]
    coef1[2] = roll(packed1[1], -1, 2)
    prepare(coef1, work1, whole_diag(part, coef1[0], coef1[1], n1, 4.0), 4.0, 2)

    arrive(sent2)
    mixed = packed2[...] * SHRINK
    bx_in, by_in, bz_in = roll(mixed, -1, 2), roll(mixed, -2, 2), roll(mixed, -3, 2)
    coef2[0] = whole_diag(mixed, bx_in, by_in, n2, 1.0)
    coef2[1] = bx_in
    coef2[2] = by_in
    coef2[3] = roll(by_in, -1, 1)
    coef2[4] = bz_in
    coef2[5] = roll(bz_in, -4, 2)

    arrive(sent3)
    begin(work1, rhs1[...], 4.0)
    down1 = pair1.at[4]
    smooth(coef1, work1, n1, 2, halve(down1, 2))
    own = pl.ds(HALO, n2)
    basis[0, own, own, :] = restrict(down1, n2)
    sent4 = exchange(4, basis.at[0], n2, False)
    start(sent4)

    def compacted(value, width):
        rows = value.reshape((-1, LANES))
        count = LANES // width
        pick = lax.broadcasted_iota(jnp.int32, (LANES, count), 0) == width * lax.broadcasted_iota(jnp.int32, (LANES, count), 1)
        out = jnp.dot(rows, pick.astype(F32), precision=lax.Precision.HIGHEST, preferred_element_type=F32)
        return out.reshape(value.shape[:-1] + (count,))

    own = pl.ds(HALO, n1)
    one_ref[...] = compacted(work1[7, own, own, :], 2)

    arrive(sent4)
    for number in range(4):
        first, last = number + 1, n2 + 2 * HALO - number - 1
        here = pl.ds(first, last - first)
        x = basis[number, here]
        total = coef2[1, here] * basis[number, pl.ds(first - 1, last - first)]
        total = total + coef2[1, pl.ds(first + 1, last - first)] * basis[number, pl.ds(first + 1, last - first)]
        total = total + coef2[2, here] * roll(x, 1, 1) + coef2[3, here] * roll(x, -1, 1)
        total = total + coef2[4, here] * roll(x, 4, 2) + coef2[5, here] * roll(x, -4, 2)
        basis[number + 1, here] = coef2[0, here] * x - total

    own = pl.ds(HALO, n2)
    vectors = [basis[i, own, own, :] for i in range(5)]
    valid = lane_of((n2, LANES)) % 4 == 0
    lane = lane_of((1, LANES))
    row = jnp.zeros((1, LANES), F32)
    for k in range(9):
        product = jnp.sum(vectors[k // 2] * vectors[(k + 1) // 2], axis=0)
        product = jnp.where(valid, product, 0.0)
        moment = jnp.sum(jnp.sum(product, axis=0, keepdims=True), axis=1, keepdims=True)
        row = jnp.where(lane == k, moment, row)

    def all_sum(row, slots, ssem, rsem, peer):
        slots[0] = row
        copies = [
            pltpu.make_async_remote_copy(slots.at[0], slots.at[o], ssem.at[o], rsem.at[o], device_id=peer(o), device_id_type=MESH)
            for o in range(1, slots.shape[0])
        ]
        for copy in copies:
            copy.start()
        for copy in copies:
            copy.wait_recv()
        return jnp.sum(slots[...], axis=0), copies

    row, sent5 = all_sum(row, gather_y, ysend, yrecv, peer_y)
    row, sent6 = all_sum(row, gather_x, xsend, xrecv, peer_x)
    moments = [jnp.sum(jnp.where(lane == k, row, 0.0), axis=1, keepdims=True) for k in range(9)]

    def inner(u, w):
        total = None
        for i, a in enumerate(u):
            for j, b in enumerate(w):
                if a is not None and b is not None:
                    term = a * b * moments[i + j]
                    total = term if total is None else total + term
        return total

    def plus(u, c, w):
        out = []
        for a, b in zip(u, w):
            term = None if b is None else c * b
            out.append(a if term is None else term if a is None else a + term)
        return out

    def applied(u):
        return [None] + [None if a is None else a * (1.0 / SHRINK) for a in u[:-1]]

    shadow = [jnp.ones((1, 1), F32), None, None, None, None]
    solved = [None] * 5
    resid = direction = shadow
    rho = moments[0]
    for number in range(BICG):
        image = applied(direction)
        step = rho / inner(shadow, image)
        half = plus(resid, -step, image)
        turned = applied(half)
        omega = inner(turned, half) / inner(turned, turned)
        solved = plus(plus(solved, step, direction), omega, half)
        if number + 1 < BICG:
            resid = plus(half, -omega, turned)
            rho_next = inner(shadow, resid)
            factor = (rho_next / rho) * (step / omega)
            direction = plus(resid, factor, plus(direction, -omega, image))
            rho = rho_next

    total = None
    for i, c in enumerate(solved):
        if c is not None:
            term = c * basis[i, pl.ds(HALO, n2), pl.ds(0, 2 * HALO), :]
            total = term if total is None else total + term
    bottom_ref[...] = compacted(total, 4)[:, HALO:, :]

    for copies in (sent0, sent1, sent2, sent3, sent4):
        leave(copies)
    for copy in sent5 + sent6:
        copy.wait_send()
    store.wait()


def per_device(right_side, alpha_cells, beta_x, beta_y, beta_z):
    nx, ny = lax.axis_size("gx"), lax.axis_size("gy")
    n0, _, nz = right_side.shape
    n1, n2 = n0 // 2, n0 // 4
    e0, e1, e2 = n0 + 2 * HALO, n1 + 2 * HALO, n2 + 2 * HALO
    anywhere = pl.BlockSpec(memory_space=pl.ANY)
    vmem = pl.BlockSpec(memory_space=pltpu.VMEM)

    def body(*refs):
        kernel(nx, ny, *refs)

    return pl.pallas_call(
        body,
        out_shape=(
            jax.ShapeDtypeStruct((n0, n0, nz), F32),
            jax.ShapeDtypeStruct((n1, n1, nz // 2), F32),
            jax.ShapeDtypeStruct((n2, n2, nz // 4), F32),
        ),
        in_specs=[anywhere] * 5,
        out_specs=(anywhere, vmem, vmem),
        scratch_shapes=[
            pltpu.VMEM((5, n0, n0, nz), F32),
            pltpu.VMEM((5, e0, e0, nz), F32),
            pltpu.VMEM((8, e0, e0, nz), F32),
            pltpu.VMEM((5, n1, e0, nz), F32),
            pltpu.VMEM((4, n1, n1, nz), F32),
            pltpu.VMEM((2, e1, e1, nz), F32),
            pltpu.VMEM((3, e1, e1, nz), F32),
            pltpu.VMEM((8, e1, e1, nz), F32),
            pltpu.VMEM((e1, e1, nz), F32),
            pltpu.VMEM((5, n2, e1, nz), F32),
            pltpu.VMEM((e2, 16, nz), F32),
            pltpu.VMEM((6, e2, 16, nz), F32),
            pltpu.VMEM((5, e2, 16, nz), F32),
            pltpu.VMEM((ny, 1, nz), F32),
            pltpu.VMEM((nx, 1, nz), F32),
            pltpu.SemaphoreType.DMA((5,)),
            pltpu.SemaphoreType.DMA,
            pltpu.SemaphoreType.DMA((5, 8)),
            pltpu.SemaphoreType.DMA((5, 8)),
            pltpu.SemaphoreType.DMA((ny,)),
            pltpu.SemaphoreType.DMA((ny,)),
            pltpu.SemaphoreType.DMA((nx,)),
            pltpu.SemaphoreType.DMA((nx,)),
        ],
        compiler_params=pltpu.CompilerParams(collective_id=0, has_side_effects=True, vmem_limit_bytes=32 * 2**20),
        cost_estimate=pl.CostEstimate(flops=40_000_000, bytes_accessed=800_000, transcendentals=0),
        name="vcycle_down",
    )(right_side, alpha_cells, beta_x, beta_y, beta_z)


def solution(mesh):
    placed = P("gx", "gy", None)
    return jax.shard_map(per_device, mesh=mesh, in_specs=(placed,) * 5, out_specs=(placed,) * 3, check_vma=False)
```

```python
import jax
import jax.numpy as jnp
from jax import lax
from jax.experimental import pallas as pl
from jax.experimental.pallas import tpu as pltpu
from jax.sharding import PartitionSpec as P

MESH = pl.DeviceIdType.MESH
F32 = jnp.float32

BICG = 2
LMAX = 2.0
LMIN = 0.25
THETA = 0.5 * (LMAX + LMIN)
DELTA = 0.5 * (LMAX - LMIN)
SIGMA = THETA / DELTA

HALO = 4
LANES = 128
DIRECTIONS = ((1, 1), (1, -1), (-1, 1), (-1, -1), (0, 1), (0, -1), (1, 0), (-1, 0))
SHRINK = 0.125


def steps():
    rho = 1.0 / SIGMA
    out = []
    for _ in range(3):
        rho_next = 1.0 / (2.0 * SIGMA - rho)
        out.append((rho_next * rho, 2.0 * rho_next / DELTA))
        rho = rho_next
    return out


def lane_of(shape):
    return lax.broadcasted_iota(jnp.int32, shape, len(shape) - 1)


def roll(value, shift, axis):
    extent = value.shape[axis]
    return pltpu.roll(value, shift % extent, axis)


def spans(offset, own, depth=HALO, skip=0):
    if offset == 1:
        return pl.ds(own + HALO - skip - depth, depth), pl.ds(HALO - skip - depth, depth)
    if offset == -1:
        return pl.ds(HALO + skip, depth), pl.ds(own + HALO + skip, depth)
    return pl.ds(HALO, own), pl.ds(HALO, own)


def kernel(
    nx, ny,
    rhs_hbm, alpha_hbm, bx_hbm, by_hbm, bz_hbm,
    fine_hbm, one_hbm, bottom_hbm,
    raw, ext0, work0, pair0,
    raw1, packed1, coef1, work1, rhs1, pair1,
    packed2, coef2, basis,
    gather_y, gather_x, one_ref, bottom_ref,
    load_sem, out_sem, send_sem, recv_sem, more_send, more_recv, row_send, row_recv, known_x, known_y,
):
    gx = lax.axis_index("gx")
    gy = lax.axis_index("gy")
    n0, n1, n2 = raw.shape[1], raw1.shape[1], raw1.shape[1] // 2

    loads = [
        pltpu.make_async_copy(src, raw.at[i], load_sem.at[i])
        for i, src in enumerate((rhs_hbm, alpha_hbm, bx_hbm, by_hbm, bz_hbm))
    ]
    for copy in loads:
        copy.start()

    def has(dx, dy):
        ok = None
        for step, at, count in ((dx, gx, nx), (dy, gy, ny)):
            if step != 0:
                this = at < count - 1 if step > 0 else at > 0
                ok = this if ok is None else jnp.logical_and(ok, this)
        return ok

    barrier = pltpu.get_barrier_semaphore()
    greeted = jnp.int32(4)
    for dx, dy in DIRECTIONS[:4]:
        there = has(dx, dy)
        greeted = greeted + there.astype(jnp.int32)

        @pl.when(there)
        def _(dx=dx, dy=dy):
            pl.semaphore_signal(barrier, inc=1, device_id=(gx + dx, gy + dy), device_id_type=MESH)

    def peer_y(o):
        return (gx, lax.rem(gy + o + ny, ny))

    def peer_x(o):
        return (lax.rem(gx + o + nx, nx), gy)

    for o in (1, -1):
        pl.semaphore_signal(barrier, inc=1, device_id=peer_x(o), device_id_type=MESH)
        pl.semaphore_signal(barrier, inc=1, device_id=peer_y(o), device_id_type=MESH)

    def tell(number):
        for sems, peer, count in ((known_x, peer_x, nx), (known_y, peer_y, ny)):
            if 2**number < count // 2:
                for o in (2**number, -(2**number)):
                    pl.semaphore_signal(sems.at[number], inc=1, device_id=peer(o), device_id_type=MESH)

    def told(number):
        for sems, count in ((known_x, nx), (known_y, ny)):
            if 2**number < count // 2:
                pl.semaphore_wait(sems.at[number], 2)

    def remote(src, dst, ssem, rsem, dx, dy):
        copy = pltpu.make_async_remote_copy(src, dst, ssem, rsem, device_id=(gx + dx, gy + dy), device_id_type=MESH)
        return copy, has(dx, dy), has(-dx, -dy)

    def exchange(which, ref, own, lead, corner=HALO, skip=()):
        out = []
        for j, (dx, dy) in enumerate(DIRECTIONS):
            if (dx, dy) in skip:
                continue
            depth = corner if dx * dy != 0 else HALO
            (sx, tx), (sy, ty) = spans(dx, own, depth), spans(dy, own, depth)
            src, dst = (ref.at[:, sx, sy], ref.at[:, tx, ty]) if lead else (ref.at[sx, sy], ref.at[tx, ty])
            out.append(remote(src, dst, send_sem.at[which, j], recv_sem.at[which, j], dx, dy))
        return out

    def exchange_fine(ref, own):
        out = exchange(0, ref, own, True, HALO - 1, ((0, 1), (0, -1)))
        corners, sides = out[:4], out[4:]
        more = []

        def add(src, dst, dx, dy):
            k = len(more)
            more.append(remote(src, dst, more_send.at[k], more_recv.at[k], dx, dy))

        for dx, dy in DIRECTIONS[:4]:
            if dy == -1:
                (sx, tx), (sy, ty) = spans(dx, own, 1, HALO - 1), spans(dy, own, 1)
                add(ref.at[0, sx, sy], ref.at[0, tx, ty], dx, dy)
            if dx == -1:
                (sx, tx), (sy, ty) = spans(dx, own, 1), spans(dy, own, 1, HALO - 1)
                add(ref.at[3, sx, sy], ref.at[3, tx, ty], dx, dy)
        whole = pl.ds(HALO, own)
        for dy in (1, -1):
            sy, ty = spans(dy, own)
            add(ref.at[pl.ds(0, 3), whole, sy], ref.at[pl.ds(0, 3), whole, ty], 0, dy)
            sy, ty = spans(dy, own, HALO - 1)
            add(ref.at[pl.ds(3, 2), whole, sy], ref.at[pl.ds(3, 2), whole, ty], 0, dy)
        return corners + more + sides

    def start(copies):
        for copy, to, _ in copies:
            pl.when(to)(copy.start)

    def arrive(copies):
        for copy, _, of in copies:
            pl.when(of)(copy.wait_recv)

    def leave(copies):
        for copy, to, _ in copies:
            pl.when(to)(copy.wait_send)

    x_inner = jnp.where(gx > 0, 1.0, 0.0).astype(F32)

    def own_coefs(alpha, bx, by, bz, scale, width):
        n = bx.shape[0]
        col = lax.broadcasted_iota(jnp.int32, bx.shape, 1)
        bz_in = jnp.where(lane_of(bx.shape) < width, 0.0, bz)
        bxu = jnp.concatenate([bx[1:], jnp.zeros_like(bx[:1])], 0)
        byu = jnp.where(col == n - 1, 0.0, roll(by, -1, 1))
        diag = alpha + scale * (bx + bxu + by + byu + bz + roll(bz_in, -width, 2))
        by_in = jnp.where(jnp.logical_and(col == 0, gy == 0), 0.0, by)
        bx_in = jnp.concatenate([bx[:1] * x_inner, bx[1:]], 0)
        return diag, bx_in, by_in, bz_in

    for copy in loads:
        copy.wait()

    own = pl.ds(HALO, n0)
    diag, bx_in, by_in, bz_in = own_coefs(raw[1], raw[2], raw[3], raw[4], 16.0, 1)
    for i, v in enumerate((by_in, raw[0], diag, bx_in, bz_in)):
        ext0[i, own, own, :] = v

    pl.semaphore_wait(barrier, greeted)
    sent0 = exchange_fine(ext0, n0)
    start(sent0)
    tell(0)

    def halves(ref, n):
        return ref[:, pl.ds(0, n, stride=2), :], ref[:, pl.ds(1, n, stride=2), :]

    def coarsen(alpha, bx, by, bz, pairs, width):
        n = bx.shape[0] // 2

        def xs(v):
            w = v.reshape((n, 2) + v.shape[1:])
            return w[:, 0], w[:, 1]

        def zsum(v):
            return v + roll(v, -width, 2)

        pairs[0, :, pl.ds(0, 2 * n)] = zsum(sum(xs(alpha)))
        pairs[1, :, pl.ds(0, 2 * n)] = zsum(xs(bx)[0])
        pairs[2, :, pl.ds(0, 2 * n)] = zsum(sum(xs(by)))
        pairs[3, :, pl.ds(0, 2 * n)] = sum(xs(bz))
        a0, a1 = halves(pairs.at[0], n)
        x0, x1 = halves(pairs.at[1], n)
        y0, _ = halves(pairs.at[2], n)
        z0, z1 = halves(pairs.at[3], n)
        return (a0 + a1) * 0.125, (x0 + x1) * 0.25, y0 * 0.25, (z0 + z1) * 0.25

    alpha1, bx1, by1, bz1 = coarsen(raw[1], raw[2], raw[3], raw[4], pair0, 1)
    diag, bx_in, by_in, bz_in = own_coefs(alpha1, bx1, by1, bz1, 4.0, 2)
    own = pl.ds(HALO, n1)
    lane = lane_of(diag.shape)
    packed1[0, own, own, :] = jnp.where(lane % 2 == 0, diag, roll(bx_in, 1, 2))
    packed1[1, own, own, :] = jnp.where(lane % 2 == 0, by_in, roll(bz_in, 1, 2))
    sent1 = exchange(1, packed1, n1, True)
    start(sent1)

    alpha2, bx2, by2, bz2 = coarsen(alpha1, bx1, by1, bz1, pair1, 2)
    diag, bx_in, by_in, bz_in = own_coefs(alpha2, bx2, by2, bz2, 1.0, 4)
    own = pl.ds(HALO, n2)
    lane = lane_of(diag.shape) % 4
    mixed = jnp.where(lane < 2, jnp.where(lane == 0, diag, roll(bx_in, 1, 2)), jnp.where(lane == 2, roll(by_in, 2, 2), roll(bz_in, 3, 2)))
    packed2[own, own, :] = mixed
    sent2 = exchange(2, packed2, n2, False)
    start(sent2)

    def border(ref, index, n, value):
        for flag, at in ((gx == 0, 0), (gx == nx - 1, n + HALO)):

            @pl.when(flag)
            def _(at=at):
                ref[index + (pl.ds(at, HALO),)] = value((HALO, n + 2 * HALO, LANES))

        for flag, at in ((gy == 0, 0), (gy == ny - 1, n + HALO)):

            @pl.when(flag)
            def _(at=at):
                ref[index + (slice(None), pl.ds(at, HALO))] = value((n + 2 * HALO, HALO, LANES))

    def zeros(shape):
        return jnp.zeros(shape, F32)

    def ones(every):
        return lambda shape: jnp.where(lane_of(shape) % every == 0, 1.0, 0.0).astype(F32)

    for i in (0, 1, 3, 4):
        border(ext0, (i,), n0, zeros)
    border(ext0, (2,), n0, ones(1))
    border(packed1, (0,), n1, ones(2))
    border(packed1, (1,), n1, zeros)
    border(rhs1, (), n1, zeros)

    def border2(ref, value):
        for flag, at in ((gx == 0, 0), (gx == nx - 1, n2 + HALO)):

            @pl.when(flag)
            def _(at=at):
                ref[pl.ds(at, HALO)] = value((HALO,) + ref.shape[1:])

        for flag, at in ((gy == 0, 0), (gy == ny - 1, n2 + HALO)):

            @pl.when(flag)
            def _(at=at):
                ref[:, pl.ds(at, HALO)] = value((ref.shape[0], HALO, LANES))

    border2(packed2, ones(4))
    border2(basis.at[0], zeros)

    def whole_diag(part, bx, by, n, scale):
        rows = part.shape[0]
        row = lax.broadcasted_iota(jnp.int32, part.shape, 0)
        col = lax.broadcasted_iota(jnp.int32, part.shape, 1)
        at_x = jnp.logical_or(row == HALO - 1, row == HALO + n - 1)
        at_y = jnp.logical_or(col == HALO - 1, col == HALO + n - 1)
        bxu = jnp.concatenate([bx[1:rows], jnp.zeros_like(bx[:1])], 0)
        return part + scale * (jnp.where(at_x, bxu, 0.0) + jnp.where(at_y, roll(by, -1, 1), 0.0))

    def sweep(number, faces, work, n, width, finish):
        coefs = steps()
        first, last = number + 1, n + 2 * HALO - number - 1
        rows = {22: 2, 20: 4, 18: 6, 16: 4, 14: 7, 12: 6, 10: 5, 8: 4}[last - first]
        source, target = 6 + number % 2, 7 - number % 2

        def body(i, carry):
            at = first + i * rows
            here = pl.ds(at, rows)
            x = work[source, here]
            total = faces[0][here] * work[source, pl.ds(at - 1, rows)]
            total = total + faces[0][pl.ds(at + 1, rows)] * work[source, pl.ds(at + 1, rows)]
            total = total + faces[1][here] * roll(x, 1, 1) + work[2, here] * roll(x, -1, 1)
            total = total + faces[2][here] * roll(x, width, 2) + work[3, here] * roll(x, -width, 2)
            scaled = work[1, here] - x + work[0, here] * total
            if number == 3:
                finish(at, rows, work[4, here] * scaled)
            else:
                a, b = coefs[number]
                update = a * (x if number == 0 else work[5, here]) + b * scaled
                work[5, here] = update
                work[target, here] = x + update
            return carry

        lax.fori_loop(0, (last - first) // rows, body, 0, unroll=True)

    def smooth(faces, work, n, width, finish):
        for number in range(4):
            sweep(number, faces, work, n, width, finish)

    def prepare(faces, work, diag, scale, width):
        inverse = 1.0 / diag
        work[0] = scale * inverse
        work[2] = roll(faces[1][...], -1, 1)
        work[3] = roll(faces[2][...], -width, 2)
        work[4] = diag

    def begin(work, rhs, scale):
        work[1] = work[0] * rhs * (1.0 / scale)
        work[6] = work[1] * (1.0 / THETA)

    arrive(sent0)
    told(0)
    tell(1)
    faces0 = (ext0.at[3], ext0.at[0], ext0.at[4])
    prepare(faces0, work0, whole_diag(ext0[2], ext0[3], ext0[0], n0, 16.0), 16.0, 1)
    begin(work0, ext0[1], 16.0)

    def halve(pairs, width):
        def finish(at, rows, resid):
            summed = resid.reshape((rows // 2, 2) + resid.shape[1:])
            summed = summed[:, 0] + summed[:, 1]
            half = lax.div(at - HALO, 2)
            pairs[pl.ds(half, rows // 2)] = summed + roll(summed, -width, 2)

        return finish

    def restrict(pairs, n):
        even = pairs[:, pl.ds(HALO, n, stride=2), :]
        odd = pairs[:, pl.ds(HALO + 1, n, stride=2), :]
        return (even + odd) * 0.125

    down0 = pair0.at[4]
    smooth(faces0, work0, n0, 1, halve(down0, 1))
    own = pl.ds(HALO, n1)
    rhs1[own, own, :] = restrict(down0, n1)
    sent3 = exchange(3, rhs1, n1, False, HALO - 1)
    start(sent3)

    own = pl.ds(HALO, n0)
    store = pltpu.make_async_copy(work0.at[7, own, own], fine_hbm, out_sem.at[0])
    store.start()

    arrive(sent1)
    even = lane_of(packed1.shape[1:]) % 2 == 0
    part = jnp.where(even, packed1[0], 1.0)
    coef1[0] = roll(packed1[0], -1, 2)
    coef1[1] = packed1[1]
    coef1[2] = roll(packed1[1], -1, 2)
    faces1 = (coef1.at[0], coef1.at[1], coef1.at[2])
    prepare(faces1, work1, whole_diag(part, coef1[0], coef1[1], n1, 4.0), 4.0, 2)

    arrive(sent2)
    mixed = packed2[...] * SHRINK
    bx_in, by_in, bz_in = roll(mixed, -1, 2), roll(mixed, -2, 2), roll(mixed, -3, 2)
    coef2[0] = whole_diag(mixed, bx_in, by_in, n2, 1.0)
    coef2[1] = bx_in
    coef2[2] = by_in
    coef2[3] = roll(by_in, -1, 1)
    coef2[4] = bz_in
    coef2[5] = roll(bz_in, -4, 2)

    arrive(sent3)
    told(1)
    tell(2)
    begin(work1, rhs1[...], 4.0)
    down1 = pair1.at[4]
    smooth(faces1, work1, n1, 2, halve(down1, 2))
    own = pl.ds(HALO, n2)
    basis[0, own, own, :] = restrict(down1, n2)
    sent4 = exchange(4, basis.at[0], n2, False, HALO - 1)
    start(sent4)

    def compacted(value, width):
        rows = value.reshape((-1, LANES))
        count = LANES // width
        pick = lax.broadcasted_iota(jnp.int32, (LANES, count), 0) == width * lax.broadcasted_iota(jnp.int32, (LANES, count), 1)
        out = jnp.dot(rows, pick.astype(F32), precision=lax.Precision.HIGHEST, preferred_element_type=F32)
        return out.reshape(value.shape[:-1] + (count,))

    own = pl.ds(HALO, n1)
    one_ref[...] = compacted(work1[7, own, own, :], 2)
    store_one = pltpu.make_async_copy(one_ref, one_hbm, out_sem.at[1])
    store_one.start()

    arrive(sent4)
    told(2)
    tell(3)
    for number in range(4):
        first, last = number + 1, n2 + 2 * HALO - number - 1
        here = pl.ds(first, last - first)
        x = basis[number, here]
        total = coef2[1, here] * basis[number, pl.ds(first - 1, last - first)]
        total = total + coef2[1, pl.ds(first + 1, last - first)] * basis[number, pl.ds(first + 1, last - first)]
        total = total + coef2[2, here] * roll(x, 1, 1) + coef2[3, here] * roll(x, -1, 1)
        total = total + coef2[4, here] * roll(x, 4, 2) + coef2[5, here] * roll(x, -4, 2)
        basis[number + 1, here] = coef2[0, here] * x - total

    own = pl.ds(HALO, n2)
    vectors = [basis[i, own, own, :] for i in range(5)]
    valid = lane_of((n2, LANES)) % 4 == 0
    lane = lane_of((1, LANES))
    row = jnp.zeros((1, LANES), F32)
    for k in range(9):
        product = jnp.sum(vectors[k // 2] * vectors[(k + 1) // 2], axis=0)
        product = jnp.where(valid, product, 0.0)
        moment = jnp.sum(jnp.sum(product, axis=0, keepdims=True), axis=1, keepdims=True)
        row = jnp.where(lane == k, moment, row)

    def all_sum(row, slots, k, peer):
        slots[0] = row
        count = slots.shape[0] - 1
        for o in range(1, count + 1):
            pltpu.make_async_remote_copy(
                slots.at[0], slots.at[o], row_send.at[k], row_recv.at[k], device_id=peer(o), device_id_type=MESH
            ).start()
        others = slots.at[pl.ds(1, count)]
        pltpu.make_async_copy(others, others, row_recv.at[k]).wait()
        return jnp.sum(slots[...], axis=0), pltpu.make_async_copy(others, others, row_send.at[k])

    row, sent5 = all_sum(row, gather_y, 0, peer_y)
    told(3)
    row, sent6 = all_sum(row, gather_x, 1, peer_x)
    moments = [jnp.sum(jnp.where(lane == k, row, 0.0), axis=1, keepdims=True) for k in range(9)]

    def inner(u, w):
        total = None
        for i, a in enumerate(u):
            for j, b in enumerate(w):
                if a is not None and b is not None:
                    term = a * b * moments[i + j]
                    total = term if total is None else total + term
        return total

    def plus(u, c, w):
        out = []
        for a, b in zip(u, w):
            term = None if b is None else c * b
            out.append(a if term is None else term if a is None else a + term)
        return out

    def applied(u):
        return [None] + [None if a is None else a * (1.0 / SHRINK) for a in u[:-1]]

    shadow = [jnp.ones((1, 1), F32), None, None, None, None]
    solved = [None] * 5
    resid = direction = shadow
    rho = moments[0]
    for number in range(BICG):
        image = applied(direction)
        step = rho / inner(shadow, image)
        half = plus(resid, -step, image)
        turned = applied(half)
        omega = inner(turned, half) / inner(turned, turned)
        solved = plus(plus(solved, step, direction), omega, half)
        if number + 1 < BICG:
            resid = plus(half, -omega, turned)
            rho_next = inner(shadow, resid)
            factor = (rho_next / rho) * (step / omega)
            direction = plus(resid, factor, plus(direction, -omega, image))
            rho = rho_next

    total = None
    for i, c in enumerate(solved):
        if c is not None:
            term = c * basis[i, pl.ds(HALO, n2), pl.ds(0, 2 * HALO), :]
            total = term if total is None else total + term
    bottom_ref[...] = compacted(total, 4)[:, HALO:, :]
    store_bottom = pltpu.make_async_copy(bottom_ref, bottom_hbm, out_sem.at[2])
    store_bottom.start()

    for copies in (sent0, sent1, sent2, sent3, sent4):
        leave(copies)
    for copy in (sent5, sent6, store, store_one, store_bottom):
        copy.wait()


def per_device(right_side, alpha_cells, beta_x, beta_y, beta_z):
    nx, ny = lax.axis_size("gx"), lax.axis_size("gy")
    n0, _, nz = right_side.shape
    n1, n2 = n0 // 2, n0 // 4
    e0, e1, e2 = n0 + 2 * HALO, n1 + 2 * HALO, n2 + 2 * HALO
    anywhere = pl.BlockSpec(memory_space=pl.ANY)

    def body(*refs):
        kernel(nx, ny, *refs)

    return pl.pallas_call(
        body,
        out_shape=(
            jax.ShapeDtypeStruct((n0, n0, nz), F32),
            jax.ShapeDtypeStruct((n1, n1, nz // 2), F32),
            jax.ShapeDtypeStruct((n2, n2, nz // 4), F32),
        ),
        in_specs=[anywhere] * 5,
        out_specs=(anywhere,) * 3,
        scratch_shapes=[
            pltpu.VMEM((5, n0, n0, nz), F32),
            pltpu.VMEM((5, e0, e0, nz), F32),
            pltpu.VMEM((8, e0, e0, nz), F32),
            pltpu.VMEM((5, n1, e0, nz), F32),
            pltpu.VMEM((4, n1, n1, nz), F32),
            pltpu.VMEM((2, e1, e1, nz), F32),
            pltpu.VMEM((3, e1, e1, nz), F32),
            pltpu.VMEM((8, e1, e1, nz), F32),
            pltpu.VMEM((e1, e1, nz), F32),
            pltpu.VMEM((5, n2, e1, nz), F32),
            pltpu.VMEM((e2, 16, nz), F32),
            pltpu.VMEM((6, e2, 16, nz), F32),
            pltpu.VMEM((5, e2, 16, nz), F32),
            pltpu.VMEM((ny, 1, nz), F32),
            pltpu.VMEM((nx, 1, nz), F32),
            pltpu.VMEM((n1, n1, nz // 2), F32),
            pltpu.VMEM((n2, n2, nz // 4), F32),
            pltpu.SemaphoreType.DMA((5,)),
            pltpu.SemaphoreType.DMA((3,)),
            pltpu.SemaphoreType.DMA((5, 8)),
            pltpu.SemaphoreType.DMA((5, 8)),
            pltpu.SemaphoreType.DMA((8,)),
            pltpu.SemaphoreType.DMA((8,)),
            pltpu.SemaphoreType.DMA((2,)),
            pltpu.SemaphoreType.DMA((2,)),
            pltpu.SemaphoreType.REGULAR((4,)),
            pltpu.SemaphoreType.REGULAR((4,)),
        ],
        compiler_params=pltpu.CompilerParams(collective_id=0, has_side_effects=True, vmem_limit_bytes=60 * 2**20),
        cost_estimate=pl.CostEstimate(flops=40_000_000, bytes_accessed=800_000, transcendentals=0),
        name="vcycle_down",
    )(right_side, alpha_cells, beta_x, beta_y, beta_z)


def solution(mesh):
    placed = P("gx", "gy", None)
    return jax.shard_map(per_device, mesh=mesh, in_specs=(placed,) * 5, out_specs=(placed,) * 3, check_vma=False)
```

```python
import jax
import jax.numpy as jnp
from jax import lax
from jax.experimental import pallas as pl
from jax.experimental.pallas import tpu as pltpu
from jax.sharding import PartitionSpec as P

MESH = pl.DeviceIdType.MESH
F32 = jnp.float32

BICG = 2
LMAX = 2.0
LMIN = 0.25
THETA = 0.5 * (LMAX + LMIN)
DELTA = 0.5 * (LMAX - LMIN)
SIGMA = THETA / DELTA

HALO = 4
LANES = 128
DIRECTIONS = ((1, 1), (1, -1), (-1, 1), (-1, -1), (0, 1), (0, -1), (1, 0), (-1, 0))
SHRINK = 0.125


def steps():
    rho = 1.0 / SIGMA
    out = []
    for _ in range(3):
        rho_next = 1.0 / (2.0 * SIGMA - rho)
        out.append((rho_next * rho, 2.0 * rho_next / DELTA))
        rho = rho_next
    return out


def lane_of(shape):
    return lax.broadcasted_iota(jnp.int32, shape, len(shape) - 1)


def roll(value, shift, axis):
    extent = value.shape[axis]
    return pltpu.roll(value, shift % extent, axis)


def spans(offset, own, depth=HALO, skip=0):
    if offset == 1:
        return pl.ds(own + HALO - skip - depth, depth), pl.ds(HALO - skip - depth, depth)
    if offset == -1:
        return pl.ds(HALO + skip, depth), pl.ds(own + HALO + skip, depth)
    return pl.ds(HALO, own), pl.ds(HALO, own)


def kernel(
    nx, ny,
    rhs_hbm, alpha_hbm, bx_hbm, by_hbm, bz_hbm,
    fine_ref, one_ref, bottom_ref,
    raw, ext0, work0, pair0,
    raw1, packed1, coef1, work1, rhs1, pair1,
    packed2, coef2, basis,
    gather_y, gather_x,
    load_sem, out_sem, send_sem, recv_sem, more_send, more_recv, row_send, row_recv, known_x, known_y,
):
    gx = lax.axis_index("gx")
    gy = lax.axis_index("gy")
    n0, n1, n2 = raw.shape[1], raw1.shape[1], raw1.shape[1] // 2

    for i, src in enumerate((rhs_hbm, alpha_hbm, bx_hbm, by_hbm, bz_hbm)):
        pltpu.make_async_copy(src, raw.at[i], load_sem).start()

    def has(dx, dy):
        ok = None
        for step, at, count in ((dx, gx, nx), (dy, gy, ny)):
            if step != 0:
                this = at < count - 1 if step > 0 else at > 0
                ok = this if ok is None else jnp.logical_and(ok, this)
        return ok

    barrier = pltpu.get_barrier_semaphore()
    greeted = jnp.int32(4)
    for dx, dy in DIRECTIONS[:4]:
        there = has(dx, dy)
        greeted = greeted + there.astype(jnp.int32)

        @pl.when(there)
        def _(dx=dx, dy=dy):
            pl.semaphore_signal(barrier, inc=1, device_id=(gx + dx, gy + dy), device_id_type=MESH)

    def peer_y(o):
        return (gx, lax.rem(gy + o + ny, ny))

    def peer_x(o):
        return (lax.rem(gx + o + nx, nx), gy)

    for o in (1, -1):
        pl.semaphore_signal(barrier, inc=1, device_id=peer_x(o), device_id_type=MESH)
        pl.semaphore_signal(barrier, inc=1, device_id=peer_y(o), device_id_type=MESH)

    def tell(number):
        for sems, peer, count in ((known_x, peer_x, nx), (known_y, peer_y, ny)):
            if 2**number < count // 2:
                for o in (2**number, -(2**number)):
                    pl.semaphore_signal(sems.at[number], inc=1, device_id=peer(o), device_id_type=MESH)

    def told(number):
        for sems, count in ((known_x, nx), (known_y, ny)):
            if 2**number < count // 2:
                pl.semaphore_wait(sems.at[number], 2)

    def remote(src, dst, ssem, rsem, dx, dy):
        copy = pltpu.make_async_remote_copy(src, dst, ssem, rsem, device_id=(gx + dx, gy + dy), device_id_type=MESH)
        return copy, has(dx, dy), has(-dx, -dy)

    def exchange(which, ref, own, lead, corner=HALO, skip=()):
        out = []
        for j, (dx, dy) in enumerate(DIRECTIONS):
            if (dx, dy) in skip:
                continue
            depth = corner if dx * dy != 0 else HALO
            (sx, tx), (sy, ty) = spans(dx, own, depth), spans(dy, own, depth)
            src, dst = (ref.at[:, sx, sy], ref.at[:, tx, ty]) if lead else (ref.at[sx, sy], ref.at[tx, ty])
            out.append(remote(src, dst, send_sem.at[which, j], recv_sem.at[which, j], dx, dy))
        return out

    def exchange_fine(ref, own):
        out = exchange(0, ref, own, True, HALO - 1, ((0, 1), (0, -1)))
        corners, sides = out[:4], out[4:]
        more = []

        def add(src, dst, dx, dy):
            k = len(more)
            more.append(remote(src, dst, more_send.at[k], more_recv.at[k], dx, dy))

        for dx, dy in DIRECTIONS[:4]:
            if dy == -1:
                (sx, tx), (sy, ty) = spans(dx, own, 1, HALO - 1), spans(dy, own, 1)
                add(ref.at[0, sx, sy], ref.at[0, tx, ty], dx, dy)
            if dx == -1:
                (sx, tx), (sy, ty) = spans(dx, own, 1), spans(dy, own, 1, HALO - 1)
                add(ref.at[3, sx, sy], ref.at[3, tx, ty], dx, dy)
        whole = pl.ds(HALO, own)
        for dy in (1, -1):
            sy, ty = spans(dy, own)
            add(ref.at[pl.ds(0, 3), whole, sy], ref.at[pl.ds(0, 3), whole, ty], 0, dy)
            sy, ty = spans(dy, own, HALO - 1)
            add(ref.at[pl.ds(3, 2), whole, sy], ref.at[pl.ds(3, 2), whole, ty], 0, dy)
        return corners + more + sides

    def start(copies):
        for copy, to, _ in copies:
            pl.when(to)(copy.start)

    def arrive(copies):
        for copy, _, of in copies:
            pl.when(of)(copy.wait_recv)

    def leave(copies):
        for copy, to, _ in copies:
            pl.when(to)(copy.wait_send)

    x_inner = jnp.where(gx > 0, 1.0, 0.0).astype(F32)

    def own_coefs(alpha, bx, by, bz, scale, width):
        n = bx.shape[0]
        col = lax.broadcasted_iota(jnp.int32, bx.shape, 1)
        bz_in = jnp.where(lane_of(bx.shape) < width, 0.0, bz)
        bxu = jnp.concatenate([bx[1:], jnp.zeros_like(bx[:1])], 0)
        byu = jnp.where(col == n - 1, 0.0, roll(by, -1, 1))
        diag = alpha + scale * (bx + bxu + by + byu + bz + roll(bz_in, -width, 2))
        by_in = jnp.where(jnp.logical_and(col == 0, gy == 0), 0.0, by)
        bx_in = jnp.concatenate([bx[:1] * x_inner, bx[1:]], 0)
        return diag, bx_in, by_in, bz_in

    pltpu.make_async_copy(raw, raw, load_sem).wait()

    own = pl.ds(HALO, n0)
    diag, bx_in, by_in, bz_in = own_coefs(raw[1], raw[2], raw[3], raw[4], 16.0, 1)
    for i, v in enumerate((by_in, raw[0], diag, bx_in, bz_in)):
        ext0[i, own, own, :] = v

    pl.semaphore_wait(barrier, greeted)
    sent0 = exchange_fine(ext0, n0)
    start(sent0)
    tell(0)

    def halves(ref, n):
        return ref[:, pl.ds(0, n, stride=2), :], ref[:, pl.ds(1, n, stride=2), :]

    def coarsen(alpha, bx, by, bz, pairs, width):
        n = bx.shape[0] // 2

        def xs(v):
            w = v.reshape((n, 2) + v.shape[1:])
            return w[:, 0], w[:, 1]

        def zsum(v):
            return v + roll(v, -width, 2)

        pairs[0, :, pl.ds(0, 2 * n)] = zsum(sum(xs(alpha)))
        pairs[1, :, pl.ds(0, 2 * n)] = zsum(xs(bx)[0])
        pairs[2, :, pl.ds(0, 2 * n)] = zsum(sum(xs(by)))
        pairs[3, :, pl.ds(0, 2 * n)] = sum(xs(bz))
        a0, a1 = halves(pairs.at[0], n)
        x0, x1 = halves(pairs.at[1], n)
        y0, _ = halves(pairs.at[2], n)
        z0, z1 = halves(pairs.at[3], n)
        return (a0 + a1) * 0.125, (x0 + x1) * 0.25, y0 * 0.25, (z0 + z1) * 0.25

    alpha1, bx1, by1, bz1 = coarsen(raw[1], raw[2], raw[3], raw[4], pair0, 1)
    diag, bx_in, by_in, bz_in = own_coefs(alpha1, bx1, by1, bz1, 4.0, 2)
    own = pl.ds(HALO, n1)
    lane = lane_of(diag.shape)
    packed1[0, own, own, :] = jnp.where(lane % 2 == 0, diag, roll(bx_in, 1, 2))
    packed1[1, own, own, :] = jnp.where(lane % 2 == 0, by_in, roll(bz_in, 1, 2))
    sent1 = exchange(1, packed1, n1, True)
    start(sent1)

    alpha2, bx2, by2, bz2 = coarsen(alpha1, bx1, by1, bz1, pair1, 2)
    diag, bx_in, by_in, bz_in = own_coefs(alpha2, bx2, by2, bz2, 1.0, 4)
    own = pl.ds(HALO, n2)
    lane = lane_of(diag.shape) % 4
    mixed = jnp.where(lane < 2, jnp.where(lane == 0, diag, roll(bx_in, 1, 2)), jnp.where(lane == 2, roll(by_in, 2, 2), roll(bz_in, 3, 2)))
    packed2[own, own, :] = mixed
    sent2 = exchange(2, packed2, n2, False)
    start(sent2)

    def border(ref, index, n, value):
        for flag, at in ((gx == 0, 0), (gx == nx - 1, n + HALO)):

            @pl.when(flag)
            def _(at=at):
                ref[index + (pl.ds(at, HALO),)] = value((HALO, n + 2 * HALO, LANES))

        for flag, at in ((gy == 0, 0), (gy == ny - 1, n + HALO)):

            @pl.when(flag)
            def _(at=at):
                ref[index + (slice(None), pl.ds(at, HALO))] = value((n + 2 * HALO, HALO, LANES))

    def zeros(shape):
        return jnp.zeros(shape, F32)

    def ones(every):
        return lambda shape: jnp.where(lane_of(shape) % every == 0, 1.0, 0.0).astype(F32)

    for i in (0, 1, 3, 4):
        border(ext0, (i,), n0, zeros)
    border(ext0, (2,), n0, ones(1))
    border(packed1, (0,), n1, ones(2))
    border(packed1, (1,), n1, zeros)
    border(rhs1, (), n1, zeros)

    def border2(ref, value):
        for flag, at in ((gx == 0, 0), (gx == nx - 1, n2 + HALO)):

            @pl.when(flag)
            def _(at=at):
                ref[pl.ds(at, HALO)] = value((HALO,) + ref.shape[1:])

        for flag, at in ((gy == 0, 0), (gy == ny - 1, n2 + HALO)):

            @pl.when(flag)
            def _(at=at):
                ref[:, pl.ds(at, HALO)] = value((ref.shape[0], HALO, LANES))

    border2(packed2, ones(4))
    border2(basis.at[0], zeros)

    def whole_diag(part, bx, by, n, scale):
        rows = part.shape[0]
        row = lax.broadcasted_iota(jnp.int32, part.shape, 0)
        col = lax.broadcasted_iota(jnp.int32, part.shape, 1)
        at_x = jnp.logical_or(row == HALO - 1, row == HALO + n - 1)
        at_y = jnp.logical_or(col == HALO - 1, col == HALO + n - 1)
        bxu = jnp.concatenate([bx[1:rows], jnp.zeros_like(bx[:1])], 0)
        return part + scale * (jnp.where(at_x, bxu, 0.0) + jnp.where(at_y, roll(by, -1, 1), 0.0))

    def sweep(number, faces, work, n, width, finish):
        coefs = steps()
        first, last = number + 1, n + 2 * HALO - number - 1
        rows = {22: 2, 20: 4, 18: 6, 16: 4, 14: 7, 12: 6, 10: 5, 8: 4}[last - first]
        source, target = 6 + number % 2, 7 - number % 2

        def body(i, carry):
            at = first + i * rows
            here = pl.ds(at, rows)
            x = work[source, here]
            total = faces[0][here] * work[source, pl.ds(at - 1, rows)]
            total = total + faces[0][pl.ds(at + 1, rows)] * work[source, pl.ds(at + 1, rows)]
            total = total + faces[1][here] * roll(x, 1, 1) + work[2, here] * roll(x, -1, 1)
            total = total + faces[2][here] * roll(x, width, 2) + work[3, here] * roll(x, -width, 2)
            scaled = work[1, here] - x + work[0, here] * total
            if number == 3:
                finish(at, rows, work[4, here] * scaled)
            else:
                a, b = coefs[number]
                update = a * (x if number == 0 else work[5, here]) + b * scaled
                work[5, here] = update
                work[target, here] = x + update
            return carry

        lax.fori_loop(0, (last - first) // rows, body, 0, unroll=True)

    def smooth(faces, work, n, width, finish):
        for number in range(4):
            sweep(number, faces, work, n, width, finish)

    def prepare(faces, work, diag, scale, width):
        inverse = 1.0 / diag
        work[0] = scale * inverse
        work[2] = roll(faces[1][...], -1, 1)
        work[3] = roll(faces[2][...], -width, 2)
        work[4] = diag

    def begin(work, rhs, scale):
        work[1] = work[0] * rhs * (1.0 / scale)
        work[6] = work[1] * (1.0 / THETA)

    arrive(sent0)
    told(0)
    tell(1)
    faces0 = (ext0.at[3], ext0.at[0], ext0.at[4])
    prepare(faces0, work0, whole_diag(ext0[2], ext0[3], ext0[0], n0, 16.0), 16.0, 1)
    begin(work0, ext0[1], 16.0)

    def halve(pairs, width):
        def finish(at, rows, resid):
            summed = resid.reshape((rows // 2, 2) + resid.shape[1:])
            summed = summed[:, 0] + summed[:, 1]
            half = lax.div(at - HALO, 2)
            pairs[pl.ds(half, rows // 2)] = summed + roll(summed, -width, 2)

        return finish

    def restrict(pairs, n):
        even = pairs[:, pl.ds(HALO, n, stride=2), :]
        odd = pairs[:, pl.ds(HALO + 1, n, stride=2), :]
        return (even + odd) * 0.125

    down0 = pair0.at[4]
    smooth(faces0, work0, n0, 1, halve(down0, 1))
    own = pl.ds(HALO, n1)
    rhs1[own, own, :] = restrict(down0, n1)
    sent3 = exchange(3, rhs1, n1, False, HALO - 1)
    start(sent3)

    own = pl.ds(HALO, n0)
    store = pltpu.make_async_copy(work0.at[7, own, own], fine_ref, out_sem)
    store.start()

    arrive(sent1)
    even = lane_of(packed1.shape[1:]) % 2 == 0
    part = jnp.where(even, packed1[0], 1.0)
    coef1[0] = roll(packed1[0], -1, 2)
    coef1[1] = packed1[1]
    coef1[2] = roll(packed1[1], -1, 2)
    faces1 = (coef1.at[0], coef1.at[1], coef1.at[2])
    prepare(faces1, work1, whole_diag(part, coef1[0], coef1[1], n1, 4.0), 4.0, 2)

    arrive(sent2)
    mixed = packed2[...] * SHRINK
    bx_in, by_in, bz_in = roll(mixed, -1, 2), roll(mixed, -2, 2), roll(mixed, -3, 2)
    coef2[0] = whole_diag(mixed, bx_in, by_in, n2, 1.0)
    coef2[1] = bx_in
    coef2[2] = by_in
    coef2[3] = roll(by_in, -1, 1)
    coef2[4] = bz_in
    coef2[5] = roll(bz_in, -4, 2)

    arrive(sent3)
    told(1)
    tell(2)
    begin(work1, rhs1[...], 4.0)
    down1 = pair1.at[4]
    smooth(faces1, work1, n1, 2, halve(down1, 2))
    own = pl.ds(HALO, n2)
    basis[0, own, own, :] = restrict(down1, n2)
    sent4 = exchange(4, basis.at[0], n2, False, HALO - 1)
    start(sent4)

    def compacted(value, width):
        rows = value.reshape((-1, LANES))
        count = LANES // width
        pick = lax.broadcasted_iota(jnp.int32, (LANES, count), 0) == width * lax.broadcasted_iota(jnp.int32, (LANES, count), 1)
        out = jnp.dot(rows, pick.astype(F32), precision=lax.Precision.HIGHEST, preferred_element_type=F32)
        return out.reshape(value.shape[:-1] + (count,))

    own = pl.ds(HALO, n1)
    one_ref[...] = compacted(work1[7, own, own, :], 2)

    arrive(sent4)
    told(2)
    tell(3)
    for number in range(4):
        first, last = number + 1, n2 + 2 * HALO - number - 1
        here = pl.ds(first, last - first)
        x = basis[number, here]
        total = coef2[1, here] * basis[number, pl.ds(first - 1, last - first)]
        total = total + coef2[1, pl.ds(first + 1, last - first)] * basis[number, pl.ds(first + 1, last - first)]
        total = total + coef2[2, here] * roll(x, 1, 1) + coef2[3, here] * roll(x, -1, 1)
        total = total + coef2[4, here] * roll(x, 4, 2) + coef2[5, here] * roll(x, -4, 2)
        basis[number + 1, here] = coef2[0, here] * x - total

    own = pl.ds(HALO, n2)
    vectors = [basis[i, own, own, :] for i in range(5)]
    valid = lane_of((n2, LANES)) % 4 == 0
    lane = lane_of((1, LANES))
    row = jnp.zeros((1, LANES), F32)
    for k in range(9):
        product = jnp.sum(vectors[k // 2] * vectors[(k + 1) // 2], axis=0)
        product = jnp.where(valid, product, 0.0)
        moment = jnp.sum(jnp.sum(product, axis=0, keepdims=True), axis=1, keepdims=True)
        row = jnp.where(lane == k, moment, row)

    def all_sum(row, slots, k, peer):
        slots[0] = row
        count = slots.shape[0] - 1
        for o in sorted(range(1, count + 1), key=lambda o: -min(o, count + 1 - o)):
            pltpu.make_async_remote_copy(
                slots.at[0], slots.at[o], row_send.at[k], row_recv.at[k], device_id=peer(o), device_id_type=MESH
            ).start()
        others = slots.at[pl.ds(1, count)]
        pltpu.make_async_copy(others, others, row_recv.at[k]).wait()
        return jnp.sum(slots[...], axis=0), pltpu.make_async_copy(others, others, row_send.at[k])

    row, sent5 = all_sum(row, gather_y, 0, peer_y)
    told(3)
    row, sent6 = all_sum(row, gather_x, 1, peer_x)
    moments = [jnp.sum(jnp.where(lane == k, row, 0.0), axis=1, keepdims=True) for k in range(9)]

    def inner(u, w):
        total = None
        for i, a in enumerate(u):
            for j, b in enumerate(w):
                if a is not None and b is not None:
                    term = a * b * moments[i + j]
                    total = term if total is None else total + term
        return total

    def plus(u, c, w):
        out = []
        for a, b in zip(u, w):
            term = None if b is None else c * b
            out.append(a if term is None else term if a is None else a + term)
        return out

    def applied(u):
        return [None] + [None if a is None else a * (1.0 / SHRINK) for a in u[:-1]]

    shadow = [jnp.ones((1, 1), F32), None, None, None, None]
    solved = [None] * 5
    resid = direction = shadow
    rho = moments[0]
    for number in range(BICG):
        image = applied(direction)
        step = rho / inner(shadow, image)
        half = plus(resid, -step, image)
        turned = applied(half)
        omega = inner(turned, half) / inner(turned, turned)
        solved = plus(plus(solved, step, direction), omega, half)
        if number + 1 < BICG:
            resid = plus(half, -omega, turned)
            rho_next = inner(shadow, resid)
            factor = (rho_next / rho) * (step / omega)
            direction = plus(resid, factor, plus(direction, -omega, image))
            rho = rho_next

    total = None
    for i, c in enumerate(solved):
        if c is not None:
            term = c * basis[i, pl.ds(HALO, n2), pl.ds(0, 2 * HALO), :]
            total = term if total is None else total + term
    bottom_ref[...] = compacted(total, 4)[:, HALO:, :]

    for copies in (sent0, sent1, sent2, sent3, sent4):
        leave(copies)
    for copy in (sent5, sent6, store):
        copy.wait()


def per_device(right_side, alpha_cells, beta_x, beta_y, beta_z):
    nx, ny = lax.axis_size("gx"), lax.axis_size("gy")
    n0, _, nz = right_side.shape
    n1, n2 = n0 // 2, n0 // 4
    e0, e1, e2 = n0 + 2 * HALO, n1 + 2 * HALO, n2 + 2 * HALO
    anywhere = pl.BlockSpec(memory_space=pl.ANY)
    vmem = pl.BlockSpec(memory_space=pltpu.VMEM)

    def body(*refs):
        kernel(nx, ny, *refs)

    return pl.pallas_call(
        body,
        out_shape=(
            pltpu.VMEM((n0, n0, nz), F32),
            pltpu.VMEM((n1, n1, nz // 2), F32),
            pltpu.VMEM((n2, n2, nz // 4), F32),
        ),
        in_specs=[anywhere] * 5,
        out_specs=(vmem,) * 3,
        scratch_shapes=[
            pltpu.VMEM((5, n0, n0, nz), F32),
            pltpu.VMEM((5, e0, e0, nz), F32),
            pltpu.VMEM((8, e0, e0, nz), F32),
            pltpu.VMEM((5, n1, e0, nz), F32),
            pltpu.VMEM((4, n1, n1, nz), F32),
            pltpu.VMEM((2, e1, e1, nz), F32),
            pltpu.VMEM((3, e1, e1, nz), F32),
            pltpu.VMEM((8, e1, e1, nz), F32),
            pltpu.VMEM((e1, e1, nz), F32),
            pltpu.VMEM((5, n2, e1, nz), F32),
            pltpu.VMEM((e2, 16, nz), F32),
            pltpu.VMEM((6, e2, 16, nz), F32),
            pltpu.VMEM((5, e2, 16, nz), F32),
            pltpu.VMEM((ny, 1, nz), F32),
            pltpu.VMEM((nx, 1, nz), F32),
            pltpu.SemaphoreType.DMA,
            pltpu.SemaphoreType.DMA,
            pltpu.SemaphoreType.DMA((5, 8)),
            pltpu.SemaphoreType.DMA((5, 8)),
            pltpu.SemaphoreType.DMA((8,)),
            pltpu.SemaphoreType.DMA((8,)),
            pltpu.SemaphoreType.DMA((2,)),
            pltpu.SemaphoreType.DMA((2,)),
            pltpu.SemaphoreType.REGULAR((4,)),
            pltpu.SemaphoreType.REGULAR((4,)),
        ],
        compiler_params=pltpu.CompilerParams(collective_id=0, has_side_effects=True, vmem_limit_bytes=60 * 2**20),
        cost_estimate=pl.CostEstimate(flops=40_000_000, bytes_accessed=800_000, transcendentals=0),
        name="vcycle_down",
    )(right_side, alpha_cells, beta_x, beta_y, beta_z)


def solution(mesh):
    placed = P("gx", "gy", None)
    return jax.shard_map(per_device, mesh=mesh, in_specs=(placed,) * 5, out_specs=(placed,) * 3, check_vma=False)
```

```python
import jax
import jax.numpy as jnp
from jax import lax
from jax.experimental import pallas as pl
from jax.experimental.pallas import tpu as pltpu
from jax.sharding import PartitionSpec as P

MESH = pl.DeviceIdType.MESH
F32 = jnp.float32

BICG = 2
LMAX = 2.0
LMIN = 0.25
THETA = 0.5 * (LMAX + LMIN)
DELTA = 0.5 * (LMAX - LMIN)
SIGMA = THETA / DELTA

HALO = 4
LANES = 128
DIRECTIONS = ((1, 1), (1, -1), (-1, 1), (-1, -1), (0, 1), (0, -1), (1, 0), (-1, 0))
SHRINK = 0.125


def steps():
    rho = 1.0 / SIGMA
    out = []
    for _ in range(3):
        rho_next = 1.0 / (2.0 * SIGMA - rho)
        out.append((rho_next * rho, 2.0 * rho_next / DELTA))
        rho = rho_next
    return out


def lane_of(shape):
    return lax.broadcasted_iota(jnp.int32, shape, len(shape) - 1)


def roll(value, shift, axis):
    extent = value.shape[axis]
    return pltpu.roll(value, shift % extent, axis)


def spans(offset, own, depth=HALO, skip=0):
    if offset == 1:
        return pl.ds(own + HALO - skip - depth, depth), pl.ds(HALO - skip - depth, depth)
    if offset == -1:
        return pl.ds(HALO + skip, depth), pl.ds(own + HALO + skip, depth)
    return pl.ds(HALO, own), pl.ds(HALO, own)


def kernel(
    nx, ny,
    rhs_hbm, alpha_hbm, bx_hbm, by_hbm, bz_hbm,
    fine_ref, one_ref, bottom_ref,
    raw, ext0, work0, pair0,
    packed1, coef1, work1, rhs1, part1, send1, land1, pair1,
    packed2, coef2, land2, basis,
    gather_y, gather_x,
    load_sem, out_sem, send_sem, recv_sem, more_send, more_recv, row_send, row_recv, known_x, known_y,
):
    gx = lax.axis_index("gx")
    gy = lax.axis_index("gy")
    n0, n1, n2 = raw.shape[1], raw.shape[1] // 2, raw.shape[1] // 4

    for i, src in enumerate((rhs_hbm, alpha_hbm, bx_hbm, by_hbm, bz_hbm)):
        pltpu.make_async_copy(src, raw.at[i], load_sem).start()

    def has(dx, dy):
        ok = None
        for step, at, count in ((dx, gx, nx), (dy, gy, ny)):
            if step != 0:
                this = at < count - 1 if step > 0 else at > 0
                ok = this if ok is None else jnp.logical_and(ok, this)
        return ok

    barrier = pltpu.get_barrier_semaphore()
    greeted = jnp.int32(4)
    for dx, dy in DIRECTIONS[:4]:
        there = has(dx, dy)
        greeted = greeted + there.astype(jnp.int32)

        @pl.when(there)
        def _(dx=dx, dy=dy):
            pl.semaphore_signal(barrier, inc=1, device_id=(gx + dx, gy + dy), device_id_type=MESH)

    def peer_y(o):
        return (gx, lax.rem(gy + o + ny, ny))

    def peer_x(o):
        return (lax.rem(gx + o + nx, nx), gy)

    for o in (1, -1):
        pl.semaphore_signal(barrier, inc=1, device_id=peer_x(o), device_id_type=MESH)
        pl.semaphore_signal(barrier, inc=1, device_id=peer_y(o), device_id_type=MESH)

    def tell(number):
        for sems, peer, count in ((known_x, peer_x, nx), (known_y, peer_y, ny)):
            if 2**number < count // 2:
                for o in (2**number, -(2**number)):
                    pl.semaphore_signal(sems.at[number], inc=1, device_id=peer(o), device_id_type=MESH)

    def told(number):
        for sems, count in ((known_x, nx), (known_y, ny)):
            if 2**number < count // 2:
                pl.semaphore_wait(sems.at[number], 2)

    def remote(src, dst, ssem, rsem, dx, dy):
        copy = pltpu.make_async_remote_copy(src, dst, ssem, rsem, device_id=(gx + dx, gy + dy), device_id_type=MESH)
        return copy, has(dx, dy), has(-dx, -dy)

    def exchange(which, part):
        return [
            remote(*part(dx, dy), send_sem.at[which, j], recv_sem.at[which, j], dx, dy)
            for j, (dx, dy) in enumerate(DIRECTIONS)
        ]

    def exchange_fine(ref, own):
        out = []
        deep = HALO - 1

        def add(src, dst, dx, dy):
            k = len(out)
            ssem, rsem = (send_sem.at[0, k], recv_sem.at[0, k]) if k < 8 else (more_send.at[k - 8], more_recv.at[k - 8])
            out.append(remote(src, dst, ssem, rsem, dx, dy))

        for dx, dy in DIRECTIONS[:4]:
            (sx, tx), (sy, ty) = spans(dx, own, deep - 1), spans(dy, own, deep - 1)
            add(ref.at[:, sx, sy], ref.at[:, tx, ty], dx, dy)
            if dy == -1:
                (sx, tx), (sy, ty) = spans(dx, own, 1, deep - 1), spans(dy, own, 1)
                add(ref.at[0, sx, sy], ref.at[0, tx, ty], dx, dy)
            if dx == -1:
                (sx, tx), (sy, ty) = spans(dx, own, 1), spans(dy, own, 1, deep - 1)
                add(ref.at[3, sx, sy], ref.at[3, tx, ty], dx, dy)
        whole = pl.ds(HALO, own)
        for dy in (1, -1):
            sy, ty = spans(dy, own, deep)
            add(ref.at[pl.ds(0, 3), whole, sy], ref.at[pl.ds(0, 3), whole, ty], 0, dy)
            sy, ty = spans(dy, own, deep - 1)
            add(ref.at[pl.ds(3, 2), whole, sy], ref.at[pl.ds(3, 2), whole, ty], 0, dy)
        for dx in (1, -1):
            sx, tx = spans(dx, own, deep)
            add(ref.at[:, sx, whole], ref.at[:, tx, whole], dx, 0)
        return out

    def start(copies):
        for copy, to, _ in copies:
            pl.when(to)(copy.start)

    def arrive(copies):
        for copy, _, of in copies:
            pl.when(of)(copy.wait_recv)

    def leave(copies):
        for copy, to, _ in copies:
            pl.when(to)(copy.wait_send)

    x_inner = jnp.where(gx > 0, 1.0, 0.0).astype(F32)

    def own_coefs(alpha, bx, by, bz, scale, width):
        n = bx.shape[0]
        col = lax.broadcasted_iota(jnp.int32, bx.shape, 1)
        bz_in = jnp.where(lane_of(bx.shape) < width, 0.0, bz)
        bxu = jnp.concatenate([bx[1:], jnp.zeros_like(bx[:1])], 0)
        byu = jnp.where(col == n - 1, 0.0, roll(by, -1, 1))
        diag = alpha + scale * (bx + bxu + by + byu + bz + roll(bz_in, -width, 2))
        by_in = jnp.where(jnp.logical_and(col == 0, gy == 0), 0.0, by)
        bx_in = jnp.concatenate([bx[:1] * x_inner, bx[1:]], 0)
        return diag, bx_in, by_in, bz_in

    for ref in (part1, land1, land2):
        ref[...] = jnp.zeros(ref.shape, F32)

    pltpu.make_async_copy(raw, raw, load_sem).wait()

    own = pl.ds(HALO, n0)
    diag, bx_in, by_in, bz_in = own_coefs(raw[1], raw[2], raw[3], raw[4], 16.0, 1)
    for i, v in enumerate((by_in, raw[0], diag, bx_in, bz_in)):
        ext0[i, own, own, :] = v

    pl.semaphore_wait(barrier, greeted)
    sent0 = exchange_fine(ext0, n0)
    start(sent0)
    tell(0)

    def halves(ref, n):
        return ref[pl.ds(0, n), pl.ds(0, n, stride=2), :], ref[pl.ds(0, n), pl.ds(1, n, stride=2), :]

    def coarsen(alpha, bx, by, bz, pairs, width):
        n = bx.shape[0] // 2

        def xs(v):
            w = v.reshape((n, 2) + v.shape[1:])
            return w[:, 0], w[:, 1]

        def zsum(v):
            return v + roll(v, -width, 2)

        pairs[0, pl.ds(0, n), pl.ds(0, 2 * n)] = zsum(sum(xs(alpha)))
        pairs[1, pl.ds(0, n), pl.ds(0, 2 * n)] = zsum(xs(bx)[0])
        pairs[2, pl.ds(0, n), pl.ds(0, 2 * n)] = zsum(sum(xs(by)))
        pairs[3, pl.ds(0, n), pl.ds(0, 2 * n)] = sum(xs(bz))
        a0, a1 = halves(pairs.at[0], n)
        x0, x1 = halves(pairs.at[1], n)
        y0, _ = halves(pairs.at[2], n)
        z0, z1 = halves(pairs.at[3], n)
        return (a0 + a1) * 0.125, (x0 + x1) * 0.25, y0 * 0.25, (z0 + z1) * 0.25

    alpha1, bx1, by1, bz1 = coarsen(raw[1], raw[2], raw[3], raw[4], pair0, 1)
    diag, bx_in, by_in, bz_in = own_coefs(alpha1, bx1, by1, bz1, 4.0, 2)
    own = pl.ds(HALO, n1)
    lane = lane_of(diag.shape)
    packed1[0, own, own, :] = jnp.where(lane % 2 == 0, diag, roll(bx_in, 1, 2))
    packed1[1, own, own, :] = jnp.where(lane % 2 == 0, by_in, roll(bz_in, 1, 2))

    alpha2, bx2, by2, bz2 = coarsen(alpha1, bx1, by1, bz1, pair1, 2)
    diag, bx_in, by_in, bz_in = own_coefs(alpha2, bx2, by2, bz2, 1.0, 4)
    lane = lane_of(diag.shape) % 4
    mixed = jnp.where(lane < 2, jnp.where(lane == 0, diag, roll(bx_in, 1, 2)), jnp.where(lane == 2, roll(by_in, 2, 2), roll(bz_in, 3, 2)))
    for i in range(2):
        for j in range(2):
            packed1[2, pl.ds(HALO + n2 * i, n2), pl.ds(HALO + n2 * j, n2), :] = mixed

    def edges(dx, dy):
        (sx, tx), (sy, ty) = spans(dx, n1), spans(dy, n1)
        return packed1.at[:, sx, sy], packed1.at[:, tx, ty]

    sent1 = exchange(1, edges)
    start(sent1)

    def border(ref, index, n, value):
        for flag, at in ((gx == 0, 0), (gx == nx - 1, n + HALO)):

            @pl.when(flag)
            def _(at=at):
                ref[index + (pl.ds(at, HALO),)] = value((HALO, n + 2 * HALO, LANES))

        for flag, at in ((gy == 0, 0), (gy == ny - 1, n + HALO)):

            @pl.when(flag)
            def _(at=at):
                ref[index + (slice(None), pl.ds(at, HALO))] = value((n + 2 * HALO, HALO, LANES))

    def zeros(shape):
        return jnp.zeros(shape, F32)

    def ones(every):
        return lambda shape: jnp.where(lane_of(shape) % every == 0, 1.0, 0.0).astype(F32)

    for i in (0, 1, 3, 4):
        border(ext0, (i,), n0, zeros)
    border(ext0, (2,), n0, ones(1))
    border(packed1, (0,), n1, ones(2))
    border(packed1, (1,), n1, zeros)
    border(packed1, (2,), n1, ones(4))

    def whole_diag(part, bx, by, n, scale):
        rows = part.shape[0]
        row = lax.broadcasted_iota(jnp.int32, part.shape, 0)
        col = lax.broadcasted_iota(jnp.int32, part.shape, 1)
        at_x = jnp.logical_or(row == HALO - 1, row == HALO + n - 1)
        at_y = jnp.logical_or(col == HALO - 1, col == HALO + n - 1)
        bxu = jnp.concatenate([bx[1:rows], jnp.zeros_like(bx[:1])], 0)
        return part + scale * (jnp.where(at_x, bxu, 0.0) + jnp.where(at_y, roll(by, -1, 1), 0.0))

    def sweep(number, first, rows, faces, work, width, finish, clip=None):
        coefs = steps()
        source, target = 6 + number % 2, 7 - number % 2

        def body(i, carry):
            at = first + i * rows[1]
            here = pl.ds(at, rows[1])
            x = work[source, here]
            total = faces[0][here] * work[source, pl.ds(at - 1, rows[1])]
            total = total + faces[0][pl.ds(at + 1, rows[1])] * work[source, pl.ds(at + 1, rows[1])]
            total = total + faces[1][here] * roll(x, 1, 1) + work[2, here] * roll(x, -1, 1)
            total = total + faces[2][here] * roll(x, width, 2) + work[3, here] * roll(x, -width, 2)
            if number == 3:
                finish(at, rows[1], work[4, here], work[1, here] - x, work[0, here], total)
            else:
                a, b = coefs[number]
                scaled = work[1, here] - x + work[0, here] * total
                update = a * (x if number == 0 else work[5, here]) + b * scaled
                x = x + update
                if clip is not None:
                    col = lax.broadcasted_iota(jnp.int32, x.shape, 1)
                    x = jnp.where(jnp.logical_and(col >= HALO, col < HALO + clip), x, 0.0)
                work[5, here] = update
                work[target, here] = x
            return carry

        lax.fori_loop(0, rows[0], body, 0, unroll=True)

    def prepare(faces, work, diag, scale, width):
        inverse = 1.0 / diag
        work[0] = scale * inverse
        work[2] = roll(faces[1][...], -1, 1)
        work[3] = roll(faces[2][...], -width, 2)
        work[4] = diag

    def begin(work, rhs, scale):
        work[1] = work[0] * rhs * (1.0 / scale)
        work[6] = work[1] * (1.0 / THETA)

    arrive(sent0)
    told(0)
    tell(1)
    faces0 = (ext0.at[3], ext0.at[0], ext0.at[4])
    prepare(faces0, work0, whole_diag(ext0[2], ext0[3], ext0[0], n0, 16.0), 16.0, 1)
    begin(work0, ext0[1], 16.0)

    def halve(pairs, first, width):
        def finish(at, resid):
            rows = resid.shape[0] // 2
            summed = resid.reshape((rows, 2) + resid.shape[1:])
            summed = summed[:, 0] + summed[:, 1]
            pairs[pl.ds(lax.div(at - first, 2), rows)] = summed + roll(summed, -width, 2)

        return finish

    down0 = pair0.at[4]
    keep0 = halve(down0, 2, 1)

    def partial(at, rows, diag, gap, scaled, total):
        row = at + lax.broadcasted_iota(jnp.int32, gap.shape, 0)
        col = lax.broadcasted_iota(jnp.int32, gap.shape, 1)
        in_x = jnp.logical_and(row >= HALO, row < HALO + n0)
        in_y = jnp.logical_and(col >= HALO, col < HALO + n0)
        near_y = jnp.logical_and(col >= HALO - 2, col < HALO + n0 + 2)
        mine = jnp.where(jnp.logical_and(in_x, in_y), diag * gap, 0.0)
        keep0(at, mine + jnp.where(jnp.logical_or(in_y, jnp.logical_and(in_x, near_y)), 16.0 * total, 0.0))

    sweep(0, 2, (5, 4), faces0, work0, 1, None)
    sweep(1, 3, (3, 6), faces0, work0, 1, None)
    sweep(2, 4, (4, 4), faces0, work0, 1, None, n0)
    for at in (1, HALO + n0):
        work0[7, pl.ds(at, 3)] = jnp.zeros((3,) + work0.shape[2:], F32)
    sweep(3, 2, (5, 4), faces0, work0, 1, partial)
    count = n1 + HALO
    terms = (down0[:, pl.ds(0, count, stride=2), :] + down0[:, pl.ds(1, count, stride=2), :]) * 0.125
    part1[pl.ds(HALO - 1, n1 + 2), pl.ds(HALO - 2, count), :] = terms
    halved = part1[...].reshape(rhs1.shape)
    even = lane_of(send1.shape) % 2 == 0
    send1[...] = jnp.where(even, halved[:, 0], roll(halved[:, 1], 1, 2))

    def outer(dx, dy):
        half = n1 // 2
        sx, tx = {
            0: (pl.ds(1, half + 2), pl.ds(1, half + 2)),
            1: (pl.ds(half, 3), pl.ds(0, 3)),
            -1: (pl.ds(1, 3), pl.ds(half + 1, 3)),
        }[dx]
        wide = HALO + 1
        sy, ty = {
            0: (pl.ds(HALO - 1, n1 + 2), pl.ds(HALO - 1, n1 + 2)),
            1: (pl.ds(n1 + HALO + 1 - wide, wide), pl.ds(HALO + 1 - wide, wide)),
            -1: (pl.ds(HALO - 1, wide), pl.ds(HALO - 1 + n1, wide)),
        }[dy]
        land = land1.at[2 if dx * dy != 0 else 1 if dx != 0 else 0]
        return send1.at[sx, sy], land.at[tx, ty]

    sent2 = exchange(2, outer)
    start(sent2)

    own = pl.ds(HALO, n0)
    store = pltpu.make_async_copy(work0.at[7, own, own], fine_ref, out_sem)
    store.start()

    arrive(sent1)
    even = lane_of(packed1.shape[1:]) % 2 == 0
    part = jnp.where(even, packed1[0], 1.0)
    coef1[0] = roll(packed1[0], -1, 2)
    coef1[1] = packed1[1]
    coef1[2] = roll(packed1[1], -1, 2)
    faces1 = (coef1.at[0], coef1.at[1], coef1.at[2])
    prepare(faces1, work1, whole_diag(part, coef1[0], coef1[1], n1, 4.0), 4.0, 2)

    outer_at = HALO + n1
    low, high = pl.ds(0, 2 * HALO), pl.ds(outer_at, HALO)
    packed2[low, low] = packed1[2, low, low]
    packed2[low, pl.ds(2 * HALO, HALO)] = packed1[2, low, high]
    packed2[pl.ds(2 * HALO, HALO), low] = packed1[2, high, low]
    packed2[pl.ds(2 * HALO, HALO), pl.ds(2 * HALO, HALO)] = packed1[2, high, high]
    mixed = packed2[...] * SHRINK
    bx_in, by_in, bz_in = roll(mixed, -1, 2), roll(mixed, -2, 2), roll(mixed, -3, 2)
    coef2[0] = whole_diag(mixed, bx_in, by_in, n2, 1.0)
    coef2[1] = bx_in
    coef2[2] = by_in
    coef2[3] = roll(by_in, -1, 1)
    coef2[4] = bz_in
    coef2[5] = roll(bz_in, -4, 2)

    arrive(sent2)
    told(1)
    tell(2)
    summed = send1[...] + land1[0] + land1[1] + land1[2]
    rhs1[:, 0] = summed
    rhs1[:, 1] = roll(summed, -1, 2)
    begin(work1, rhs1[...].reshape(part1.shape), 4.0)
    down1 = pair1.at[4]
    keep1 = halve(down1, HALO, 2)

    def whole(at, rows, diag, gap, scaled, total):
        keep1(at, diag * (gap + scaled * total))

    for number, rows in enumerate(((2, 7), (2, 6), (2, 5), (2, 4))):
        sweep(number, number + 1, rows, faces1, work1, 2, whole)
    rhs2 = (down1[:, pl.ds(HALO, n2, stride=2), :] + down1[:, pl.ds(HALO + 1, n2, stride=2), :]) * 0.125
    lane = lane_of(rhs2.shape[1:]) % 4
    mixed = rhs2[0]
    for i in range(1, n2):
        mixed = jnp.where(lane == i, roll(rhs2[i], i, 1), mixed)
    land2[1, pl.ds(HALO, n2), :] = mixed

    def block(dx, dy):
        return land2.at[1, pl.ds(HALO, n2)], land2.at[1 - dx, pl.ds(HALO - n2 * dy, n2)]

    sent3 = exchange(3, block)
    start(sent3)

    def compacted(value, width):
        rows = value.reshape((-1, LANES))
        count = LANES // width
        pick = lax.broadcasted_iota(jnp.int32, (LANES, count), 0) == width * lax.broadcasted_iota(jnp.int32, (LANES, count), 1)
        out = jnp.dot(rows, pick.astype(F32), precision=lax.Precision.HIGHEST, preferred_element_type=F32)
        return out.reshape(value.shape[:-1] + (count,))

    own = pl.ds(HALO, n1)
    one_ref[...] = compacted(work1[7, own, own, :], 2)

    arrive(sent3)
    told(2)
    tell(3)
    for i in range(3):
        for j in range(n2):
            basis[0, n2 * i + j] = land2[i] if j == 0 else roll(land2[i], -j, 1)
    for number in range(4):
        first, last = number + 1, n2 + 2 * HALO - number - 1
        here = pl.ds(first, last - first)
        x = basis[number, here]
        total = coef2[1, here] * basis[number, pl.ds(first - 1, last - first)]
        total = total + coef2[1, pl.ds(first + 1, last - first)] * basis[number, pl.ds(first + 1, last - first)]
        total = total + coef2[2, here] * roll(x, 1, 1) + coef2[3, here] * roll(x, -1, 1)
        total = total + coef2[4, here] * roll(x, 4, 2) + coef2[5, here] * roll(x, -4, 2)
        basis[number + 1, here] = coef2[0, here] * x - total

    own = pl.ds(HALO, n2)
    vectors = [basis[i, own, own, :] for i in range(5)]
    valid = lane_of((n2, LANES)) % 4 == 0
    lane = lane_of((1, LANES))
    row = jnp.zeros((1, LANES), F32)
    for k in range(9):
        product = jnp.sum(vectors[k // 2] * vectors[(k + 1) // 2], axis=0)
        product = jnp.where(valid, product, 0.0)
        moment = jnp.sum(jnp.sum(product, axis=0, keepdims=True), axis=1, keepdims=True)
        row = jnp.where(lane == k, moment, row)

    def all_sum(row, slots, k, peer):
        slots[0] = row
        count = slots.shape[0] - 1
        for o in sorted(range(1, count + 1), key=lambda o: -min(o, count + 1 - o)):
            pltpu.make_async_remote_copy(
                slots.at[0], slots.at[o], row_send.at[k], row_recv.at[k], device_id=peer(o), device_id_type=MESH
            ).start()
        others = slots.at[pl.ds(1, count)]
        pltpu.make_async_copy(others, others, row_recv.at[k]).wait()
        return jnp.sum(slots[...], axis=0), pltpu.make_async_copy(others, others, row_send.at[k])

    row, sent5 = all_sum(row, gather_y, 0, peer_y)
    told(3)
    row, sent6 = all_sum(row, gather_x, 1, peer_x)
    moments = [jnp.sum(jnp.where(lane == k, row, 0.0), axis=1, keepdims=True) for k in range(9)]

    def inner(u, w):
        total = None
        for i, a in enumerate(u):
            for j, b in enumerate(w):
                if a is not None and b is not None:
                    term = a * b * moments[i + j]
                    total = term if total is None else total + term
        return total

    def plus(u, c, w):
        out = []
        for a, b in zip(u, w):
            term = None if b is None else c * b
            out.append(a if term is None else term if a is None else a + term)
        return out

    def applied(u):
        return [None] + [None if a is None else a * (1.0 / SHRINK) for a in u[:-1]]

    shadow = [jnp.ones((1, 1), F32), None, None, None, None]
    solved = [None] * 5
    resid = direction = shadow
    rho = moments[0]
    for number in range(BICG):
        image = applied(direction)
        step = rho / inner(shadow, image)
        half = plus(resid, -step, image)
        turned = applied(half)
        omega = inner(turned, half) / inner(turned, turned)
        solved = plus(plus(solved, step, direction), omega, half)
        if number + 1 < BICG:
            resid = plus(half, -omega, turned)
            rho_next = inner(shadow, resid)
            factor = (rho_next / rho) * (step / omega)
            direction = plus(resid, factor, plus(direction, -omega, image))
            rho = rho_next

    total = None
    for i, c in enumerate(solved):
        if c is not None:
            term = c * basis[i, pl.ds(HALO, n2), pl.ds(0, 2 * HALO), :]
            total = term if total is None else total + term
    bottom_ref[...] = compacted(total, 4)[:, HALO:, :]

    for copies in (sent0, sent1, sent2, sent3):
        leave(copies)
    for copy in (sent5, sent6, store):
        copy.wait()


def per_device(right_side, alpha_cells, beta_x, beta_y, beta_z):
    nx, ny = lax.axis_size("gx"), lax.axis_size("gy")
    n0, _, nz = right_side.shape
    n1, n2 = n0 // 2, n0 // 4
    e0, e1, e2 = n0 + 2 * HALO, n1 + 2 * HALO, n2 + 2 * HALO
    anywhere = pl.BlockSpec(memory_space=pl.ANY)
    vmem = pl.BlockSpec(memory_space=pltpu.VMEM)

    def body(*refs):
        kernel(nx, ny, *refs)

    return pl.pallas_call(
        body,
        out_shape=(
            pltpu.VMEM((n0, n0, nz), F32),
            pltpu.VMEM((n1, n1, nz // 2), F32),
            pltpu.VMEM((n2, n2, nz // 4), F32),
        ),
        in_specs=[anywhere] * 5,
        out_specs=(vmem,) * 3,
        scratch_shapes=[
            pltpu.VMEM((5, n0, n0, nz), F32),
            pltpu.VMEM((5, e0, e0, nz), F32),
            pltpu.VMEM((8, e0, e0, nz), F32),
            pltpu.VMEM((5, n1 + 2, e0, nz), F32),
            pltpu.VMEM((3, e1, e1, nz), F32),
            pltpu.VMEM((3, e1, e1, nz), F32),
            pltpu.VMEM((8, e1, e1, nz), F32),
            pltpu.VMEM((e1 // 2, 2, e1, nz), F32),
            pltpu.VMEM((e1, e1, nz), F32),
            pltpu.VMEM((e1 // 2, e1, nz), F32),
            pltpu.VMEM((3, e1 // 2, e1, nz), F32),
            pltpu.VMEM((5, n2, e1, nz), F32),
            pltpu.VMEM((e2, 16, nz), F32),
            pltpu.VMEM((6, e2, 16, nz), F32),
            pltpu.VMEM((3, 16, nz), F32),
            pltpu.VMEM((5, e2, 16, nz), F32),
            pltpu.VMEM((ny, 1, nz), F32),
            pltpu.VMEM((nx, 1, nz), F32),
            pltpu.SemaphoreType.DMA,
            pltpu.SemaphoreType.DMA,
            pltpu.SemaphoreType.DMA((4, 8)),
            pltpu.SemaphoreType.DMA((4, 8)),
            pltpu.SemaphoreType.DMA((6,)),
            pltpu.SemaphoreType.DMA((6,)),
            pltpu.SemaphoreType.DMA((2,)),
            pltpu.SemaphoreType.DMA((2,)),
            pltpu.SemaphoreType.REGULAR((4,)),
            pltpu.SemaphoreType.REGULAR((4,)),
        ],
        compiler_params=pltpu.CompilerParams(collective_id=0, has_side_effects=True, vmem_limit_bytes=60 * 2**20),
        cost_estimate=pl.CostEstimate(flops=40_000_000, bytes_accessed=800_000, transcendentals=0),
        name="vcycle_down",
    )(right_side, alpha_cells, beta_x, beta_y, beta_z)


def solution(mesh):
    placed = P("gx", "gy", None)
    return jax.shard_map(per_device, mesh=mesh, in_specs=(placed,) * 5, out_specs=(placed,) * 3, check_vma=False)
```

```python
import jax
import jax.numpy as jnp
from jax import lax
from jax.experimental import pallas as pl
from jax.experimental.pallas import tpu as pltpu
from jax.sharding import PartitionSpec as P

MESH = pl.DeviceIdType.MESH
F32 = jnp.float32

BICG = 2
LMAX = 2.0
LMIN = 0.25
THETA = 0.5 * (LMAX + LMIN)
DELTA = 0.5 * (LMAX - LMIN)
SIGMA = THETA / DELTA

HALO = 4
LANES = 128
DIRECTIONS = ((1, 1), (1, -1), (-1, 1), (-1, -1), (0, 1), (0, -1), (1, 0), (-1, 0))
SHRINK = 0.125


def steps():
    rho = 1.0 / SIGMA
    out = []
    for _ in range(3):
        rho_next = 1.0 / (2.0 * SIGMA - rho)
        out.append((rho_next * rho, 2.0 * rho_next / DELTA))
        rho = rho_next
    return out


def lane_of(shape):
    return lax.broadcasted_iota(jnp.int32, shape, len(shape) - 1)


def roll(value, shift, axis):
    extent = value.shape[axis]
    return pltpu.roll(value, shift % extent, axis)


def spans(offset, own, depth=HALO, skip=0):
    if offset == 1:
        return pl.ds(own + HALO - skip - depth, depth), pl.ds(HALO - skip - depth, depth)
    if offset == -1:
        return pl.ds(HALO + skip, depth), pl.ds(own + HALO + skip, depth)
    return pl.ds(HALO, own), pl.ds(HALO, own)


def kernel(
    nx, ny,
    rhs_hbm, alpha_hbm, bx_hbm, by_hbm, bz_hbm,
    fine_ref, one_ref, bottom_ref,
    raw, ext0, work0, pair0,
    packed1, coef1, work1, rhs1, part1, send1, land1, pair1,
    coef_blocks, coef_cols, coef2, rhs_blocks, rhs_cols, basis,
    gather_x,
    load_sem, out_sem, send_sem, recv_sem, more_send, more_recv, line_send, line_recv, row_send, row_recv, known_x, known_y,
):
    gx = lax.axis_index("gx")
    gy = lax.axis_index("gy")
    n0, n1, n2 = raw.shape[1], raw.shape[1] // 2, raw.shape[1] // 4

    for i, src in enumerate((rhs_hbm, alpha_hbm, bx_hbm, by_hbm, bz_hbm)):
        pltpu.make_async_copy(src, raw.at[i], load_sem).start()

    def has(dx, dy):
        ok = None
        for step, at, count in ((dx, gx, nx), (dy, gy, ny)):
            if step != 0:
                this = at < count - 1 if step > 0 else at > 0
                ok = this if ok is None else jnp.logical_and(ok, this)
        return ok

    barrier = pltpu.get_barrier_semaphore()
    greeted = jnp.int32(4)
    for dx, dy in DIRECTIONS[:4]:
        there = has(dx, dy)
        greeted = greeted + there.astype(jnp.int32)

        @pl.when(there)
        def _(dx=dx, dy=dy):
            pl.semaphore_signal(barrier, inc=1, device_id=(gx + dx, gy + dy), device_id_type=MESH)

    def peer_y(o):
        return (gx, lax.rem(gy + o + ny, ny))

    def peer_x(o):
        return (lax.rem(gx + o + nx, nx), gy)

    for o in (1, -1):
        pl.semaphore_signal(barrier, inc=1, device_id=peer_x(o), device_id_type=MESH)
        pl.semaphore_signal(barrier, inc=1, device_id=peer_y(o), device_id_type=MESH)

    def tell(number, sems, peer, count):
        if 2**number < count // 2:
            for o in (2**number, -(2**number)):
                pl.semaphore_signal(sems.at[number], inc=1, device_id=peer(o), device_id_type=MESH)

    def told(number, sems, peer, count):
        if 2**number < count // 2:
            pl.semaphore_wait(sems.at[number], 2)

    along_x, along_y = (known_x, peer_x, nx), (known_y, peer_y, ny)

    def remote(src, dst, ssem, rsem, dx, dy):
        copy = pltpu.make_async_remote_copy(src, dst, ssem, rsem, device_id=(gx + dx, gy + dy), device_id_type=MESH)
        return copy, has(dx, dy), has(-dx, -dy)

    def exchange(which, part):
        return [
            remote(*part(dx, dy), send_sem.at[which, j], recv_sem.at[which, j], dx, dy)
            for j, (dx, dy) in enumerate(DIRECTIONS)
        ]

    def exchange_fine(ref, own):
        out = []
        deep = HALO - 1

        def add(src, dst, dx, dy):
            k = len(out)
            ssem, rsem = (send_sem.at[0, k], recv_sem.at[0, k]) if k < 8 else (more_send.at[k - 8], more_recv.at[k - 8])
            out.append(remote(src, dst, ssem, rsem, dx, dy))

        for dx, dy in DIRECTIONS[:4]:
            (sx, tx), (sy, ty) = spans(dx, own, deep - 1), spans(dy, own, deep - 1)
            add(ref.at[:, sx, sy], ref.at[:, tx, ty], dx, dy)
            if dy == -1:
                (sx, tx), (sy, ty) = spans(dx, own, 1, deep - 1), spans(dy, own, 1)
                add(ref.at[0, sx, sy], ref.at[0, tx, ty], dx, dy)
            if dx == -1:
                (sx, tx), (sy, ty) = spans(dx, own, 1), spans(dy, own, 1, deep - 1)
                add(ref.at[3, sx, sy], ref.at[3, tx, ty], dx, dy)
        whole = pl.ds(HALO, own)
        for dy in (1, -1):
            sy, ty = spans(dy, own, deep)
            add(ref.at[pl.ds(0, 3), whole, sy], ref.at[pl.ds(0, 3), whole, ty], 0, dy)
            sy, ty = spans(dy, own, deep - 1)
            add(ref.at[pl.ds(3, 2), whole, sy], ref.at[pl.ds(3, 2), whole, ty], 0, dy)
        for dx in (1, -1):
            sx, tx = spans(dx, own, deep)
            add(ref.at[:, sx, whole], ref.at[:, tx, whole], dx, 0)
        return out

    def start(copies):
        for copy, to, _ in copies:
            pl.when(to)(copy.start)

    def arrive(copies):
        for copy, _, of in copies:
            pl.when(of)(copy.wait_recv)

    def leave(copies):
        for copy, to, _ in copies:
            pl.when(to)(copy.wait_send)

    x_inner = jnp.where(gx > 0, 1.0, 0.0).astype(F32)

    def own_coefs(alpha, bx, by, bz, scale, width):
        n = bx.shape[0]
        col = lax.broadcasted_iota(jnp.int32, bx.shape, 1)
        bz_in = jnp.where(lane_of(bx.shape) < width, 0.0, bz)
        bxu = jnp.concatenate([bx[1:], jnp.zeros_like(bx[:1])], 0)
        byu = jnp.where(col == n - 1, 0.0, roll(by, -1, 1))
        diag = alpha + scale * (bx + bxu + by + byu + bz + roll(bz_in, -width, 2))
        by_in = jnp.where(jnp.logical_and(col == 0, gy == 0), 0.0, by)
        bx_in = jnp.concatenate([bx[:1] * x_inner, bx[1:]], 0)
        return diag, bx_in, by_in, bz_in

    for ref in (part1, land1):
        ref[...] = jnp.zeros(ref.shape, F32)

    pltpu.make_async_copy(raw, raw, load_sem).wait()

    own = pl.ds(HALO, n0)
    diag, bx_in, by_in, bz_in = own_coefs(raw[1], raw[2], raw[3], raw[4], 16.0, 1)
    for i, v in enumerate((by_in, raw[0], diag, bx_in, bz_in)):
        ext0[i, own, own, :] = v

    pl.semaphore_wait(barrier, greeted)
    sent0 = exchange_fine(ext0, n0)
    start(sent0)
    tell(0, *along_x)
    tell(0, *along_y)

    def halves(ref, n):
        return ref[pl.ds(0, n), pl.ds(0, n, stride=2), :], ref[pl.ds(0, n), pl.ds(1, n, stride=2), :]

    def coarsen(alpha, bx, by, bz, pairs, width):
        n = bx.shape[0] // 2

        def xs(v):
            w = v.reshape((n, 2) + v.shape[1:])
            return w[:, 0], w[:, 1]

        def zsum(v):
            return v + roll(v, -width, 2)

        pairs[0, pl.ds(0, n), pl.ds(0, 2 * n)] = zsum(sum(xs(alpha)))
        pairs[1, pl.ds(0, n), pl.ds(0, 2 * n)] = zsum(xs(bx)[0])
        pairs[2, pl.ds(0, n), pl.ds(0, 2 * n)] = zsum(sum(xs(by)))
        pairs[3, pl.ds(0, n), pl.ds(0, 2 * n)] = sum(xs(bz))
        a0, a1 = halves(pairs.at[0], n)
        x0, x1 = halves(pairs.at[1], n)
        y0, _ = halves(pairs.at[2], n)
        z0, z1 = halves(pairs.at[3], n)
        return (a0 + a1) * 0.125, (x0 + x1) * 0.25, y0 * 0.25, (z0 + z1) * 0.25

    alpha1, bx1, by1, bz1 = coarsen(raw[1], raw[2], raw[3], raw[4], pair0, 1)
    diag, bx_in, by_in, bz_in = own_coefs(alpha1, bx1, by1, bz1, 4.0, 2)
    own = pl.ds(HALO, n1)
    lane = lane_of(diag.shape)
    packed1[0, own, own, :] = jnp.where(lane % 2 == 0, diag, roll(bx_in, 1, 2))
    packed1[1, own, own, :] = jnp.where(lane % 2 == 0, by_in, roll(bz_in, 1, 2))

    alpha2, bx2, by2, bz2 = coarsen(alpha1, bx1, by1, bz1, pair1, 2)
    diag, bx_in, by_in, bz_in = own_coefs(alpha2, bx2, by2, bz2, 1.0, 4)
    lane = lane_of(diag.shape) % 4
    mixed = jnp.where(lane < 2, jnp.where(lane == 0, diag, roll(bx_in, 1, 2)), jnp.where(lane == 2, roll(by_in, 2, 2), roll(bz_in, 3, 2)))
    first4 = pl.ds(0, n2)
    coef_blocks[1, gy, :, first4] = mixed

    def edges(dx, dy):
        (sx, tx), (sy, ty) = spans(dx, n1), spans(dy, n1)
        return packed1.at[:, sx, sy], packed1.at[:, tx, ty]

    sent1 = exchange(1, edges)
    start(sent1)

    def border(ref, index, n, value):
        for flag, at in ((gx == 0, 0), (gx == nx - 1, n + HALO)):

            @pl.when(flag)
            def _(at=at):
                ref[index + (pl.ds(at, HALO),)] = value((HALO, n + 2 * HALO, LANES))

        for flag, at in ((gy == 0, 0), (gy == ny - 1, n + HALO)):

            @pl.when(flag)
            def _(at=at):
                ref[index + (slice(None), pl.ds(at, HALO))] = value((n + 2 * HALO, HALO, LANES))

    def zeros(shape):
        return jnp.zeros(shape, F32)

    def ones(every):
        return lambda shape: jnp.where(lane_of(shape) % every == 0, 1.0, 0.0).astype(F32)

    for i in (0, 1, 3, 4):
        border(ext0, (i,), n0, zeros)
    border(ext0, (2,), n0, ones(1))
    border(packed1, (0,), n1, ones(2))
    border(packed1, (1,), n1, zeros)
    for flag, at in ((gx == 0, 0), (gx == nx - 1, 2)):

        @pl.when(flag)
        def _(at=at):
            coef_blocks[at] = zeros(coef_blocks.shape[1:])
            rhs_blocks[at] = zeros(rhs_blocks.shape[1:])

    wide = n2 * (ny // 4)
    line, head, tail = pl.ds(HALO, wide), pl.ds(0, HALO), pl.ds(HALO + wide, HALO)
    for ref in (coef_cols, rhs_cols):
        for part in (head, tail):
            at = (slice(None),) * (len(ref.shape) - 2) + (part,)
            ref[at] = zeros(ref.shape[:-2] + (HALO, LANES))

    told(0, *along_y)
    tell(1, *along_y)

    def whole_diag(part, bx, by, n, scale):
        rows = part.shape[0]
        row = lax.broadcasted_iota(jnp.int32, part.shape, 0)
        col = lax.broadcasted_iota(jnp.int32, part.shape, 1)
        at_x = jnp.logical_or(row == HALO - 1, row == HALO + n - 1)
        at_y = jnp.logical_or(col == HALO - 1, col == HALO + n - 1)
        bxu = jnp.concatenate([bx[1:rows], jnp.zeros_like(bx[:1])], 0)
        return part + scale * (jnp.where(at_x, bxu, 0.0) + jnp.where(at_y, roll(by, -1, 1), 0.0))

    def sweep(number, first, rows, faces, work, width, finish, clip=None):
        coefs = steps()
        source, target = 6 + number % 2, 7 - number % 2

        def body(i, carry):
            at = first + i * rows[1]
            here = pl.ds(at, rows[1])
            x = work[source, here]
            total = faces[0][here] * work[source, pl.ds(at - 1, rows[1])]
            total = total + faces[0][pl.ds(at + 1, rows[1])] * work[source, pl.ds(at + 1, rows[1])]
            total = total + faces[1][here] * roll(x, 1, 1) + work[2, here] * roll(x, -1, 1)
            total = total + faces[2][here] * roll(x, width, 2) + work[3, here] * roll(x, -width, 2)
            if number == 3:
                finish(at, rows[1], work[4, here], work[1, here] - x, work[0, here], total)
            else:
                a, b = coefs[number]
                scaled = work[1, here] - x + work[0, here] * total
                update = a * (x if number == 0 else work[5, here]) + b * scaled
                x = x + update
                if clip is not None:
                    col = lax.broadcasted_iota(jnp.int32, x.shape, 1)
                    x = jnp.where(jnp.logical_and(col >= HALO, col < HALO + clip), x, 0.0)
                work[5, here] = update
                work[target, here] = x
            return carry

        lax.fori_loop(0, rows[0], body, 0, unroll=True)

    def prepare(faces, work, diag, scale, width):
        inverse = 1.0 / diag
        work[0] = scale * inverse
        work[2] = roll(faces[1][...], -1, 1)
        work[3] = roll(faces[2][...], -width, 2)
        work[4] = diag

    def begin(work, rhs, scale):
        work[1] = work[0] * rhs * (1.0 / scale)
        work[6] = work[1] * (1.0 / THETA)

    arrive(sent0)
    told(0, *along_x)
    tell(1, *along_x)
    told(1, *along_y)
    tell(2, *along_y)
    faces0 = (ext0.at[3], ext0.at[0], ext0.at[4])
    prepare(faces0, work0, whole_diag(ext0[2], ext0[3], ext0[0], n0, 16.0), 16.0, 1)
    begin(work0, ext0[1], 16.0)

    def halve(pairs, first, width):
        def finish(at, resid):
            rows = resid.shape[0] // 2
            summed = resid.reshape((rows, 2) + resid.shape[1:])
            summed = summed[:, 0] + summed[:, 1]
            pairs[pl.ds(lax.div(at - first, 2), rows)] = summed + roll(summed, -width, 2)

        return finish

    down0 = pair0.at[4]
    keep0 = halve(down0, 2, 1)

    def partial(at, rows, diag, gap, scaled, total):
        row = at + lax.broadcasted_iota(jnp.int32, gap.shape, 0)
        col = lax.broadcasted_iota(jnp.int32, gap.shape, 1)
        in_x = jnp.logical_and(row >= HALO, row < HALO + n0)
        in_y = jnp.logical_and(col >= HALO, col < HALO + n0)
        near_y = jnp.logical_and(col >= HALO - 2, col < HALO + n0 + 2)
        mine = jnp.where(jnp.logical_and(in_x, in_y), diag * gap, 0.0)
        keep0(at, mine + jnp.where(jnp.logical_or(in_y, jnp.logical_and(in_x, near_y)), 16.0 * total, 0.0))

    sweep(0, 2, (5, 4), faces0, work0, 1, None)
    sweep(1, 3, (3, 6), faces0, work0, 1, None)
    sweep(2, 4, (4, 4), faces0, work0, 1, None, n0)
    for at in (1, HALO + n0):
        work0[7, pl.ds(at, 3)] = jnp.zeros((3,) + work0.shape[2:], F32)
    sweep(3, 2, (5, 4), faces0, work0, 1, partial)
    count = n1 + HALO
    terms = (down0[:, pl.ds(0, count, stride=2), :] + down0[:, pl.ds(1, count, stride=2), :]) * 0.125
    part1[pl.ds(HALO - 1, n1 + 2), pl.ds(HALO - 2, count), :] = terms
    halved = part1[...].reshape(rhs1.shape)
    even = lane_of(send1.shape) % 2 == 0
    send1[...] = jnp.where(even, halved[:, 0], roll(halved[:, 1], 1, 2))

    def outer(dx, dy):
        half = n1 // 2
        sx, tx = {
            0: (pl.ds(1, half + 2), pl.ds(1, half + 2)),
            1: (pl.ds(half, 3), pl.ds(0, 3)),
            -1: (pl.ds(1, 3), pl.ds(half + 1, 3)),
        }[dx]
        wide = HALO + 1
        sy, ty = {
            0: (pl.ds(HALO - 1, n1 + 2), pl.ds(HALO - 1, n1 + 2)),
            1: (pl.ds(n1 + HALO + 1 - wide, wide), pl.ds(HALO + 1 - wide, wide)),
            -1: (pl.ds(HALO - 1, wide), pl.ds(HALO - 1 + n1, wide)),
        }[dy]
        land = land1.at[2 if dx * dy != 0 else 1 if dx != 0 else 0]
        return send1.at[sx, sy], land.at[tx, ty]

    sent2 = exchange(2, outer)
    start(sent2)

    told(2, *along_y)
    mine = coef_blocks.at[1, gy, :, first4]
    for o in range(1, ny):
        pltpu.make_async_remote_copy(
            mine, mine, line_send.at[0], line_recv.at[0], device_id=peer_y(o), device_id_type=MESH
        ).start()

    own = pl.ds(HALO, n0)
    store = pltpu.make_async_copy(work0.at[7, own, own], fine_ref, out_sem)
    store.start()

    arrive(sent1)
    even = lane_of(packed1.shape[1:]) % 2 == 0
    part = jnp.where(even, packed1[0], 1.0)
    coef1[0] = roll(packed1[0], -1, 2)
    coef1[1] = packed1[1]
    coef1[2] = roll(packed1[1], -1, 2)
    faces1 = (coef1.at[0], coef1.at[1], coef1.at[2])
    prepare(faces1, work1, whole_diag(part, coef1[0], coef1[1], n1, 4.0), 4.0, 2)

    arrive(sent2)
    told(1, *along_x)
    tell(2, *along_x)
    summed = send1[...] + land1[0] + land1[1] + land1[2]
    rhs1[:, 0] = summed
    rhs1[:, 1] = roll(summed, -1, 2)
    begin(work1, rhs1[...].reshape(part1.shape), 4.0)
    down1 = pair1.at[4]
    keep1 = halve(down1, HALO, 2)

    def whole(at, rows, diag, gap, scaled, total):
        keep1(at, diag * (gap + scaled * total))

    for number, rows in enumerate(((2, 7), (2, 6), (2, 5), (2, 4))):
        sweep(number, number + 1, rows, faces1, work1, 2, whole)
    rhs2 = (down1[:, pl.ds(HALO, n2, stride=2), :] + down1[:, pl.ds(HALO + 1, n2, stride=2), :]) * 0.125
    lane = lane_of(rhs2.shape[1:]) % 4
    mixed = rhs2[0]
    for i in range(1, n2):
        mixed = jnp.where(lane == i, roll(rhs2[i], i, 1), mixed)
    rhs_blocks[1, gy, first4] = mixed

    mine = rhs_blocks.at[1, gy, first4]
    for dx in (1, -1, 0):

        def spread(dx=dx):
            for o in sorted(range(1 if dx == 0 else 0, ny), key=lambda o: -min(o, ny - o)):
                pltpu.make_async_remote_copy(
                    mine, rhs_blocks.at[1 - dx, gy, first4], line_send.at[3 + dx], line_recv.at[3 + dx],
                    device_id=(gx + dx, lax.rem(gy + o, ny)), device_id_type=MESH,
                ).start()

        if dx == 0:
            spread()
        else:
            pl.when(has(dx, 0))(spread)

    told(2, *along_x)
    tell(3, *along_x)

    def bytes_of(ref, sem):
        return pltpu.make_async_copy(ref, ref, sem)

    others = pl.ds(0, ny - 1)
    bytes_of(coef_blocks.at[1, others, :, first4], line_recv.at[0]).wait()
    passed = []
    for dx in (1, -1):
        src, dst = coef_blocks.at[1, :, :, first4], coef_blocks.at[1 - dx, :, :, first4]
        passed.append(remote(src, dst, line_send.at[(dx + 1) // 2 * 4 + 1], line_recv.at[(dx + 1) // 2 * 4 + 1], dx, 0))
    start(passed)

    def compacted(value, width, shift=0):
        rows = value.reshape((-1, LANES))
        count = LANES // width
        pick = lax.broadcasted_iota(jnp.int32, (LANES, count), 0) == shift + width * lax.broadcasted_iota(jnp.int32, (LANES, count), 1)
        out = jnp.dot(rows, pick.astype(F32), precision=lax.Precision.HIGHEST, preferred_element_type=F32)
        return out.reshape(value.shape[:-1] + (count,))

    own = pl.ds(HALO, n1)
    one_ref[...] = compacted(work1[7, own, own, :], 2)

    residue = lane_of(basis.shape[2:]) % 4

    def grouped(blocks, shift):
        out = None
        for q in range(4):
            moved = roll(blocks[q], q - shift, 1) if q != shift else blocks[q]
            out = moved if out is None else jnp.where(residue == q, moved, out)
        return out

    def joined(ref):
        side = lane_of((ref.shape[0], HALO, LANES)) % 4
        ref[:, head] = jnp.where(side != 0, roll(ref[:, pl.ds(wide, HALO)], 1, 2), 0.0)
        ref[:, tail] = jnp.where(side != 3, roll(ref[:, pl.ds(HALO, HALO)], -1, 2), 0.0)

    arrive(passed)
    for s in range(3):
        for b in range(ny):
            q, p = divmod(b, ny // 4)
            for i in range(n2):
                coef_cols[s, i, q, pl.ds(HALO + n2 * p, n2)] = coef_blocks[s, b, i, first4]
    for s in range(3):
        for i in range(n2):
            blocks = [coef_cols[s, i, q] * SHRINK for q in range(4)]
            for a, at in enumerate((0, 1, 2, 4)):
                coef2[at, n2 * s + i] = grouped(blocks, a)
    for at in (0, 1, 2, 4):
        joined(coef2.at[at])
    diag, bx_in, by_in = coef2[0], coef2[1], coef2[2]
    row = lax.broadcasted_iota(jnp.int32, diag.shape, 0)
    col = lax.broadcasted_iota(jnp.int32, diag.shape, 1)
    bxu = jnp.concatenate([bx_in[1:], jnp.zeros_like(bx_in[:1])], 0)
    byu = roll(by_in, -1, 1)
    coef2[0] = diag + jnp.where(row % n2 == n2 - 1, bxu, 0.0) + jnp.where(col % n2 == n2 - 1, byu, 0.0)
    coef2[3] = byu
    coef2[5] = roll(coef2[4], -4, 2)

    bytes_of(rhs_blocks.at[1, others, first4], line_recv.at[3]).wait()
    for dx in (1, -1):
        arriving = bytes_of(rhs_blocks.at[1 - dx, :, first4], line_recv.at[3 + dx])
        pl.when(has(-dx, 0))(arriving.wait)
    for s in range(3):
        for b in range(ny):
            q, p = divmod(b, ny // 4)
            rhs_cols[s, q, pl.ds(HALO + n2 * p, n2)] = rhs_blocks[s, b, first4]
        blocks = [rhs_cols[s, q] for q in range(4)]
        for i in range(n2):
            basis[0, n2 * s + i] = grouped(blocks, i)
    joined(basis.at[0])
    for number in range(4):
        first, last = number + 1, n2 + 2 * HALO - number - 1
        here = pl.ds(first, last - first)
        x = basis[number, here]
        total = coef2[1, here] * basis[number, pl.ds(first - 1, last - first)]
        total = total + coef2[1, pl.ds(first + 1, last - first)] * basis[number, pl.ds(first + 1, last - first)]
        total = total + coef2[2, here] * roll(x, 1, 1) + coef2[3, here] * roll(x, -1, 1)
        total = total + coef2[4, here] * roll(x, 4, 2) + coef2[5, here] * roll(x, -4, 2)
        basis[number + 1, here] = coef2[0, here] * x - total

    own = pl.ds(HALO, n2)
    vectors = [basis[i, own, line, :] for i in range(5)]
    lane = lane_of((1, LANES))
    row = jnp.zeros((1, LANES), F32)
    for k in range(9):
        product = jnp.sum(vectors[k // 2] * vectors[(k + 1) // 2], axis=0)
        moment = jnp.sum(jnp.sum(product, axis=0, keepdims=True), axis=1, keepdims=True)
        row = jnp.where(lane == k, moment, row)

    def all_sum(row, slots, k, peer):
        slots[0] = row
        count = slots.shape[0] - 1
        for o in sorted(range(1, count + 1), key=lambda o: -min(o, count + 1 - o)):
            pltpu.make_async_remote_copy(
                slots.at[0], slots.at[o], row_send.at[k], row_recv.at[k], device_id=peer(o), device_id_type=MESH
            ).start()
        others = slots.at[pl.ds(1, count)]
        pltpu.make_async_copy(others, others, row_recv.at[k]).wait()
        return jnp.sum(slots[...], axis=0), pltpu.make_async_copy(others, others, row_send.at[k])

    told(3, *along_x)
    row, sent5 = all_sum(row, gather_x, 0, peer_x)
    moments = [jnp.sum(jnp.where(lane == k, row, 0.0), axis=1, keepdims=True) for k in range(9)]

    def inner(u, w):
        total = None
        for i, a in enumerate(u):
            for j, b in enumerate(w):
                if a is not None and b is not None:
                    term = a * b * moments[i + j]
                    total = term if total is None else total + term
        return total

    def plus(u, c, w):
        out = []
        for a, b in zip(u, w):
            term = None if b is None else c * b
            out.append(a if term is None else term if a is None else a + term)
        return out

    def applied(u):
        return [None] + [None if a is None else a * (1.0 / SHRINK) for a in u[:-1]]

    shadow = [jnp.ones((1, 1), F32), None, None, None, None]
    solved = [None] * 5
    resid = direction = shadow
    rho = moments[0]
    for number in range(BICG):
        image = applied(direction)
        step = rho / inner(shadow, image)
        half = plus(resid, -step, image)
        turned = applied(half)
        omega = inner(turned, half) / inner(turned, turned)
        solved = plus(plus(solved, step, direction), omega, half)
        if number + 1 < BICG:
            resid = plus(half, -omega, turned)
            rho_next = inner(shadow, resid)
            factor = (rho_next / rho) * (step / omega)
            direction = plus(resid, factor, plus(direction, -omega, image))
            rho = rho_next

    total = None
    for i, c in enumerate(solved):
        if c is not None:
            term = c * vectors[i]
            total = term if total is None else total + term
    group, place = lax.div(gy, ny // 4), lax.rem(gy, ny // 4)
    mine = compacted(total, 4, group)
    bottom = mine[:, :n2]
    for p in range(1, ny // 4):
        bottom = jnp.where(place == p, mine[:, n2 * p : n2 * (p + 1)], bottom)
    bottom_ref[...] = bottom

    for copies in (sent0, sent1, sent2, passed):
        leave(copies)
    for copy in (sent5, store, bytes_of(coef_blocks.at[1, others, :, first4], line_send.at[0]), bytes_of(rhs_blocks.at[1, others, first4], line_send.at[3])):
        copy.wait()
    for dx in (1, -1):
        pl.when(has(dx, 0))(bytes_of(rhs_blocks.at[1, :, first4], line_send.at[3 + dx]).wait)


def per_device(right_side, alpha_cells, beta_x, beta_y, beta_z):
    nx, ny = lax.axis_size("gx"), lax.axis_size("gy")
    n0, _, nz = right_side.shape
    n1, n2 = n0 // 2, n0 // 4
    e0, e1, e2 = n0 + 2 * HALO, n1 + 2 * HALO, n2 + 2 * HALO
    anywhere = pl.BlockSpec(memory_space=pl.ANY)
    vmem = pl.BlockSpec(memory_space=pltpu.VMEM)

    def body(*refs):
        kernel(nx, ny, *refs)

    return pl.pallas_call(
        body,
        out_shape=(
            pltpu.VMEM((n0, n0, nz), F32),
            pltpu.VMEM((n1, n1, nz // 2), F32),
            pltpu.VMEM((n2, n2, nz // 4), F32),
        ),
        in_specs=[anywhere] * 5,
        out_specs=(vmem,) * 3,
        scratch_shapes=[
            pltpu.VMEM((5, n0, n0, nz), F32),
            pltpu.VMEM((5, e0, e0, nz), F32),
            pltpu.VMEM((8, e0, e0, nz), F32),
            pltpu.VMEM((5, n1 + 2, e0, nz), F32),
            pltpu.VMEM((2, e1, e1, nz), F32),
            pltpu.VMEM((3, e1, e1, nz), F32),
            pltpu.VMEM((8, e1, e1, nz), F32),
            pltpu.VMEM((e1 // 2, 2, e1, nz), F32),
            pltpu.VMEM((e1, e1, nz), F32),
            pltpu.VMEM((e1 // 2, e1, nz), F32),
            pltpu.VMEM((3, e1 // 2, e1, nz), F32),
            pltpu.VMEM((5, n2, e1, nz), F32),
            pltpu.VMEM((3, ny, n2, 8, nz), F32),
            pltpu.VMEM((3, n2, 4, 24, nz), F32),
            pltpu.VMEM((6, e2, 24, nz), F32),
            pltpu.VMEM((3, ny, 8, nz), F32),
            pltpu.VMEM((3, 4, 24, nz), F32),
            pltpu.VMEM((5, e2, 24, nz), F32),
            pltpu.VMEM((nx, 1, nz), F32),
            pltpu.SemaphoreType.DMA,
            pltpu.SemaphoreType.DMA,
            pltpu.SemaphoreType.DMA((3, 8)),
            pltpu.SemaphoreType.DMA((3, 8)),
            pltpu.SemaphoreType.DMA((6,)),
            pltpu.SemaphoreType.DMA((6,)),
            pltpu.SemaphoreType.DMA((6,)),
            pltpu.SemaphoreType.DMA((6,)),
            pltpu.SemaphoreType.DMA((1,)),
            pltpu.SemaphoreType.DMA((1,)),
            pltpu.SemaphoreType.REGULAR((4,)),
            pltpu.SemaphoreType.REGULAR((4,)),
        ],
        compiler_params=pltpu.CompilerParams(collective_id=0, has_side_effects=True, vmem_limit_bytes=60 * 2**20),
        cost_estimate=pl.CostEstimate(flops=40_000_000, bytes_accessed=800_000, transcendentals=0),
        name="vcycle_down",
    )(right_side, alpha_cells, beta_x, beta_y, beta_z)


def solution(mesh):
    placed = P("gx", "gy", None)
    return jax.shard_map(per_device, mesh=mesh, in_specs=(placed,) * 5, out_specs=(placed,) * 3, check_vma=False)
```

```python
import jax
import jax.numpy as jnp
from jax import lax
from jax.experimental import pallas as pl
from jax.experimental.pallas import tpu as pltpu
from jax.sharding import PartitionSpec as P

MESH = pl.DeviceIdType.MESH
F32 = jnp.float32

BICG = 2
LMAX = 2.0
LMIN = 0.25
THETA = 0.5 * (LMAX + LMIN)
DELTA = 0.5 * (LMAX - LMIN)
SIGMA = THETA / DELTA

HALO = 4
LANES = 128
DIRECTIONS = ((1, 1), (1, -1), (-1, 1), (-1, -1), (0, 1), (0, -1), (1, 0), (-1, 0))
SHRINK = 0.125


def steps():
    rho = 1.0 / SIGMA
    out = []
    for _ in range(3):
        rho_next = 1.0 / (2.0 * SIGMA - rho)
        out.append((rho_next * rho, 2.0 * rho_next / DELTA))
        rho = rho_next
    return out


def lane_of(shape):
    return lax.broadcasted_iota(jnp.int32, shape, len(shape) - 1)


def roll(value, shift, axis):
    extent = value.shape[axis]
    return pltpu.roll(value, shift % extent, axis)


def spans(offset, own, depth=HALO, skip=0):
    if offset == 1:
        return pl.ds(own + HALO - skip - depth, depth), pl.ds(HALO - skip - depth, depth)
    if offset == -1:
        return pl.ds(HALO + skip, depth), pl.ds(own + HALO + skip, depth)
    return pl.ds(HALO, own), pl.ds(HALO, own)


def kernel(
    nx, ny,
    rhs_hbm, alpha_hbm, bx_hbm, by_hbm, bz_hbm,
    fine_ref, one_ref, bottom_ref,
    raw, ext0, work0, pair0,
    packed1, coef1, work1, rhs1, part1, send1, land1, pair1,
    coef_blocks, coef_cols, coef2, rhs_blocks, rhs_cols, basis,
    gather_x, tally,
    load_sem, out_sem, send_sem, recv_sem, line_send, line_recv, row_send, row_recv, known_x, known_y,
):
    gx = lax.axis_index("gx")
    gy = lax.axis_index("gy")
    n0, n1, n2 = raw.shape[1], raw.shape[1] // 2, raw.shape[1] // 4

    for i, src in enumerate((rhs_hbm, alpha_hbm, bx_hbm, by_hbm, bz_hbm)):
        pltpu.make_async_copy(src, raw.at[i], load_sem).start()

    def has(dx, dy):
        ok = None
        for step, at, count in ((dx, gx, nx), (dy, gy, ny)):
            if step != 0:
                this = at < count - 1 if step > 0 else at > 0
                ok = this if ok is None else jnp.logical_and(ok, this)
        return ok

    barrier = pltpu.get_barrier_semaphore()
    greeted = jnp.int32(4)
    for dx, dy in DIRECTIONS[:4]:
        there = has(dx, dy)
        greeted = greeted + there.astype(jnp.int32)

        @pl.when(there)
        def _(dx=dx, dy=dy):
            pl.semaphore_signal(barrier, inc=1, device_id=(gx + dx, gy + dy), device_id_type=MESH)

    def peer_y(o):
        return (gx, lax.rem(gy + o + ny, ny))

    def peer_x(o):
        return (lax.rem(gx + o + nx, nx), gy)

    for o in (1, -1):
        pl.semaphore_signal(barrier, inc=1, device_id=peer_x(o), device_id_type=MESH)
        pl.semaphore_signal(barrier, inc=1, device_id=peer_y(o), device_id_type=MESH)

    def tell(number, sems, peer, count):
        if 2**number < count // 2:
            for o in (2**number, -(2**number)):
                pl.semaphore_signal(sems.at[number], inc=1, device_id=peer(o), device_id_type=MESH)

    def told(number, sems, peer, count):
        if 2**number < count // 2:
            pl.semaphore_wait(sems.at[number], 2)

    along_x, along_y = (known_x, peer_x, nx), (known_y, peer_y, ny)

    def remote(src, dst, ssem, rsem, dx, dy):
        copy = pltpu.make_async_remote_copy(src, dst, ssem, rsem, device_id=(gx + dx, gy + dy), device_id_type=MESH)
        rows = 1
        for extent in dst.shape[:-1]:
            rows *= extent
        return copy, dx, dy, rows

    def exchange(which, part):
        return [remote(*part(dx, dy), send_sem.at[which], recv_sem.at[which], dx, dy) for dx, dy in DIRECTIONS]

    def exchange_fine(ref, own):
        out = []
        deep = HALO - 1

        def add(src, dst, dx, dy):
            out.append(remote(src, dst, send_sem.at[0], recv_sem.at[0], dx, dy))

        for dx, dy in DIRECTIONS[:4]:
            (sx, tx), (sy, ty) = spans(dx, own, deep - 1), spans(dy, own, deep - 1)
            add(ref.at[:, sx, sy], ref.at[:, tx, ty], dx, dy)
            if dy == -1:
                (sx, tx), (sy, ty) = spans(dx, own, 1, deep - 1), spans(dy, own, 1)
                add(ref.at[0, sx, sy], ref.at[0, tx, ty], dx, dy)
            if dx == -1:
                (sx, tx), (sy, ty) = spans(dx, own, 1), spans(dy, own, 1, deep - 1)
                add(ref.at[3, sx, sy], ref.at[3, tx, ty], dx, dy)
        whole = pl.ds(HALO, own)
        for dy in (1, -1):
            sy, ty = spans(dy, own, deep)
            add(ref.at[pl.ds(0, 3), whole, sy], ref.at[pl.ds(0, 3), whole, ty], 0, dy)
            sy, ty = spans(dy, own, deep - 1)
            add(ref.at[pl.ds(3, 2), whole, sy], ref.at[pl.ds(3, 2), whole, ty], 0, dy)
        for dx in (1, -1):
            sx, tx = spans(dx, own, deep)
            add(ref.at[:, sx, whole], ref.at[:, tx, whole], dx, 0)
        return out

    def start(copies):
        for copy, dx, dy, _ in copies:
            pl.when(has(dx, dy))(copy.start)

    def bytes_of(ref, sem):
        return pltpu.make_async_copy(ref, ref, sem)

    def settle(copies, sem, way):
        def waits(ex, ey):
            rows = sum(r for _, dx, dy, r in copies if (ex == 0 or way * dx != ex) and (ey == 0 or way * dy != ey))
            bytes_of(tally.at[pl.ds(0, rows)], sem).wait()

        def where(at, count):
            return {-1: at == 0, 0: jnp.logical_and(at > 0, at < count - 1), 1: at == count - 1}

        at_x, at_y = where(gx, nx), where(gy, ny)
        inside = jnp.logical_and(at_x[0], at_y[0])
        pl.when(inside)(lambda: waits(0, 0))

        @pl.when(jnp.logical_not(inside))
        def _():
            for ex in (-1, 0, 1):
                for ey in (-1, 0, 1):
                    if (ex, ey) != (0, 0):
                        pl.when(jnp.logical_and(at_x[ex], at_y[ey]))(lambda ex=ex, ey=ey: waits(ex, ey))

    def arrive(copies, which):
        settle(copies, recv_sem.at[which], -1)

    def leave(copies, which):
        settle(copies, send_sem.at[which], 1)

    x_inner = jnp.where(gx > 0, 1.0, 0.0).astype(F32)

    def own_coefs(alpha, bx, by, bz, scale, width):
        n = bx.shape[0]
        col = lax.broadcasted_iota(jnp.int32, bx.shape, 1)
        bz_in = jnp.where(lane_of(bx.shape) < width, 0.0, bz)
        bxu = jnp.concatenate([bx[1:], jnp.zeros_like(bx[:1])], 0)
        byu = jnp.where(col == n - 1, 0.0, roll(by, -1, 1))
        diag = alpha + scale * (bx + bxu + by + byu + bz + roll(bz_in, -width, 2))
        by_in = jnp.where(jnp.logical_and(col == 0, gy == 0), 0.0, by)
        bx_in = jnp.concatenate([bx[:1] * x_inner, bx[1:]], 0)
        return diag, bx_in, by_in, bz_in

    for ref in (part1, land1):
        ref[...] = jnp.zeros(ref.shape, F32)

    pltpu.make_async_copy(raw, raw, load_sem).wait()

    own = pl.ds(HALO, n0)
    diag, bx_in, by_in, bz_in = own_coefs(raw[1], raw[2], raw[3], raw[4], 16.0, 1)
    for i, v in enumerate((by_in, raw[0], diag, bx_in, bz_in)):
        ext0[i, own, own, :] = v

    pl.semaphore_wait(barrier, greeted)
    sent0 = exchange_fine(ext0, n0)
    start(sent0)
    tell(0, *along_x)
    tell(0, *along_y)

    def halves(ref, n):
        return ref[pl.ds(0, n), pl.ds(0, n, stride=2), :], ref[pl.ds(0, n), pl.ds(1, n, stride=2), :]

    def coarsen(alpha, bx, by, bz, pairs, width):
        n = bx.shape[0] // 2

        def xs(v):
            w = v.reshape((n, 2) + v.shape[1:])
            return w[:, 0], w[:, 1]

        def zsum(v):
            return v + roll(v, -width, 2)

        pairs[0, pl.ds(0, n), pl.ds(0, 2 * n)] = zsum(sum(xs(alpha)))
        pairs[1, pl.ds(0, n), pl.ds(0, 2 * n)] = zsum(xs(bx)[0])
        pairs[2, pl.ds(0, n), pl.ds(0, 2 * n)] = zsum(sum(xs(by)))
        pairs[3, pl.ds(0, n), pl.ds(0, 2 * n)] = sum(xs(bz))
        a0, a1 = halves(pairs.at[0], n)
        x0, x1 = halves(pairs.at[1], n)
        y0, _ = halves(pairs.at[2], n)
        z0, z1 = halves(pairs.at[3], n)
        return (a0 + a1) * 0.125, (x0 + x1) * 0.25, y0 * 0.25, (z0 + z1) * 0.25

    alpha1, bx1, by1, bz1 = coarsen(raw[1], raw[2], raw[3], raw[4], pair0, 1)
    diag, bx_in, by_in, bz_in = own_coefs(alpha1, bx1, by1, bz1, 4.0, 2)
    own = pl.ds(HALO, n1)
    lane = lane_of(diag.shape)
    packed1[0, own, own, :] = jnp.where(lane % 2 == 0, diag, roll(bx_in, 1, 2))
    packed1[1, own, own, :] = jnp.where(lane % 2 == 0, by_in, roll(bz_in, 1, 2))

    alpha2, bx2, by2, bz2 = coarsen(alpha1, bx1, by1, bz1, pair1, 2)
    diag, bx_in, by_in, bz_in = own_coefs(alpha2, bx2, by2, bz2, 1.0, 4)
    lane = lane_of(diag.shape) % 4
    mixed = jnp.where(lane < 2, jnp.where(lane == 0, diag, roll(bx_in, 1, 2)), jnp.where(lane == 2, roll(by_in, 2, 2), roll(bz_in, 3, 2)))
    first4 = pl.ds(0, n2)
    coef_blocks[1, gy, :, first4] = mixed

    def edges(dx, dy):
        (sx, tx), (sy, ty) = spans(dx, n1), spans(dy, n1)
        return packed1.at[:, sx, sy], packed1.at[:, tx, ty]

    sent1 = exchange(1, edges)
    start(sent1)

    def border(ref, index, n, value):
        for flag, at in ((gx == 0, 0), (gx == nx - 1, n + HALO)):

            @pl.when(flag)
            def _(at=at):
                ref[index + (pl.ds(at, HALO),)] = value((HALO, n + 2 * HALO, LANES))

        for flag, at in ((gy == 0, 0), (gy == ny - 1, n + HALO)):

            @pl.when(flag)
            def _(at=at):
                ref[index + (slice(None), pl.ds(at, HALO))] = value((n + 2 * HALO, HALO, LANES))

    def zeros(shape):
        return jnp.zeros(shape, F32)

    def ones(every):
        return lambda shape: jnp.where(lane_of(shape) % every == 0, 1.0, 0.0).astype(F32)

    for i in (0, 1, 3, 4):
        border(ext0, (i,), n0, zeros)
    border(ext0, (2,), n0, ones(1))
    border(packed1, (0,), n1, ones(2))
    border(packed1, (1,), n1, zeros)
    for flag, at in ((gx == 0, 0), (gx == nx - 1, 2)):

        @pl.when(flag)
        def _(at=at):
            coef_blocks[at] = zeros(coef_blocks.shape[1:])
            rhs_blocks[at] = zeros(rhs_blocks.shape[1:])

    wide = n2 * (ny // 4)
    line, head, tail = pl.ds(HALO, wide), pl.ds(0, HALO), pl.ds(HALO + wide, HALO)
    for ref in (coef_cols, rhs_cols):
        for part in (head, tail):
            at = (slice(None),) * (len(ref.shape) - 2) + (part,)
            ref[at] = zeros(ref.shape[:-2] + (HALO, LANES))

    told(0, *along_y)
    tell(1, *along_y)

    def whole_diag(part, bx, by, n, scale):
        rows = part.shape[0]
        row = lax.broadcasted_iota(jnp.int32, part.shape, 0)
        col = lax.broadcasted_iota(jnp.int32, part.shape, 1)
        at_x = jnp.logical_or(row == HALO - 1, row == HALO + n - 1)
        at_y = jnp.logical_or(col == HALO - 1, col == HALO + n - 1)
        bxu = jnp.concatenate([bx[1:rows], jnp.zeros_like(bx[:1])], 0)
        return part + scale * (jnp.where(at_x, bxu, 0.0) + jnp.where(at_y, roll(by, -1, 1), 0.0))

    def sweep(number, first, rows, faces, work, width, finish, clip=None):
        coefs = steps()
        source, target = 6 + number % 2, 7 - number % 2

        def body(i, carry):
            at = first + i * rows[1]
            here = pl.ds(at, rows[1])
            x = work[source, here]
            total = faces[0][here] * work[source, pl.ds(at - 1, rows[1])]
            total = total + faces[0][pl.ds(at + 1, rows[1])] * work[source, pl.ds(at + 1, rows[1])]
            total = total + faces[1][here] * roll(x, 1, 1) + work[2, here] * roll(x, -1, 1)
            total = total + faces[2][here] * roll(x, width, 2) + work[3, here] * roll(x, -width, 2)
            if number == 3:
                finish(at, rows[1], work[4, here], work[1, here] - x, work[0, here], total)
            else:
                a, b = coefs[number]
                scaled = work[1, here] - x + work[0, here] * total
                update = a * (x if number == 0 else work[5, here]) + b * scaled
                x = x + update
                if clip is not None:
                    col = lax.broadcasted_iota(jnp.int32, x.shape, 1)
                    x = jnp.where(jnp.logical_and(col >= HALO, col < HALO + clip), x, 0.0)
                work[5, here] = update
                work[target, here] = x
            return carry

        lax.fori_loop(0, rows[0], body, 0, unroll=True)

    def prepare(faces, work, diag, scale, width):
        inverse = 1.0 / diag
        work[0] = scale * inverse
        work[2] = roll(faces[1][...], -1, 1)
        work[3] = roll(faces[2][...], -width, 2)
        work[4] = diag

    def begin(work, rhs, scale):
        work[1] = work[0] * rhs * (1.0 / scale)
        work[6] = work[1] * (1.0 / THETA)

    arrive(sent0, 0)
    told(0, *along_x)
    tell(1, *along_x)
    told(1, *along_y)
    tell(2, *along_y)
    faces0 = (ext0.at[3], ext0.at[0], ext0.at[4])
    prepare(faces0, work0, whole_diag(ext0[2], ext0[3], ext0[0], n0, 16.0), 16.0, 1)
    begin(work0, ext0[1], 16.0)

    def halve(pairs, first, width):
        def finish(at, resid):
            rows = resid.shape[0] // 2
            summed = resid.reshape((rows, 2) + resid.shape[1:])
            summed = summed[:, 0] + summed[:, 1]
            pairs[pl.ds(lax.div(at - first, 2), rows)] = summed + roll(summed, -width, 2)

        return finish

    down0 = pair0.at[4]
    keep0 = halve(down0, 2, 1)

    def partial(at, rows, diag, gap, scaled, total):
        row = at + lax.broadcasted_iota(jnp.int32, gap.shape, 0)
        col = lax.broadcasted_iota(jnp.int32, gap.shape, 1)
        in_x = jnp.logical_and(row >= HALO, row < HALO + n0)
        in_y = jnp.logical_and(col >= HALO, col < HALO + n0)
        near_y = jnp.logical_and(col >= HALO - 2, col < HALO + n0 + 2)
        mine = jnp.where(jnp.logical_and(in_x, in_y), diag * gap, 0.0)
        keep0(at, mine + jnp.where(jnp.logical_or(in_y, jnp.logical_and(in_x, near_y)), 16.0 * total, 0.0))

    sweep(0, 2, (5, 4), faces0, work0, 1, None)
    sweep(1, 3, (3, 6), faces0, work0, 1, None)
    sweep(2, 4, (4, 4), faces0, work0, 1, None, n0)
    for at in (1, HALO + n0):
        work0[7, pl.ds(at, 3)] = jnp.zeros((3,) + work0.shape[2:], F32)
    sweep(3, 2, (5, 4), faces0, work0, 1, partial)
    count = n1 + HALO
    terms = (down0[:, pl.ds(0, count, stride=2), :] + down0[:, pl.ds(1, count, stride=2), :]) * 0.125
    part1[pl.ds(HALO - 1, n1 + 2), pl.ds(HALO - 2, count), :] = terms
    halved = part1[...].reshape(rhs1.shape)
    even = lane_of(send1.shape) % 2 == 0
    send1[...] = jnp.where(even, halved[:, 0], roll(halved[:, 1], 1, 2))

    def outer(dx, dy):
        half = n1 // 2
        sx, tx = {
            0: (pl.ds(1, half + 2), pl.ds(1, half + 2)),
            1: (pl.ds(half, 3), pl.ds(0, 3)),
            -1: (pl.ds(1, 3), pl.ds(half + 1, 3)),
        }[dx]
        wide = HALO + 1
        sy, ty = {
            0: (pl.ds(HALO - 1, n1 + 2), pl.ds(HALO - 1, n1 + 2)),
            1: (pl.ds(n1 + HALO + 1 - wide, wide), pl.ds(HALO + 1 - wide, wide)),
            -1: (pl.ds(HALO - 1, wide), pl.ds(HALO - 1 + n1, wide)),
        }[dy]
        land = land1.at[2 if dx * dy != 0 else 1 if dx != 0 else 0]
        return send1.at[sx, sy], land.at[tx, ty]

    sent2 = exchange(2, outer)
    start(sent2)

    told(2, *along_y)
    mine = coef_blocks.at[1, gy, :, first4]
    for o in range(1, ny):
        pltpu.make_async_remote_copy(
            mine, mine, line_send.at[0], line_recv.at[0], device_id=peer_y(o), device_id_type=MESH
        ).start()

    own = pl.ds(HALO, n0)
    store = pltpu.make_async_copy(work0.at[7, own, own], fine_ref, out_sem)
    store.start()

    arrive(sent1, 1)
    even = lane_of(packed1.shape[1:]) % 2 == 0
    part = jnp.where(even, packed1[0], 1.0)
    coef1[0] = roll(packed1[0], -1, 2)
    coef1[1] = packed1[1]
    coef1[2] = roll(packed1[1], -1, 2)
    faces1 = (coef1.at[0], coef1.at[1], coef1.at[2])
    prepare(faces1, work1, whole_diag(part, coef1[0], coef1[1], n1, 4.0), 4.0, 2)

    arrive(sent2, 2)
    told(1, *along_x)
    tell(2, *along_x)
    summed = send1[...] + land1[0] + land1[1] + land1[2]
    rhs1[:, 0] = summed
    rhs1[:, 1] = roll(summed, -1, 2)
    begin(work1, rhs1[...].reshape(part1.shape), 4.0)
    down1 = pair1.at[4]
    keep1 = halve(down1, HALO, 2)

    def whole(at, rows, diag, gap, scaled, total):
        keep1(at, diag * (gap + scaled * total))

    for number, rows in enumerate(((2, 7), (2, 6), (2, 5), (2, 4))):
        sweep(number, number + 1, rows, faces1, work1, 2, whole)
    rhs2 = (down1[:, pl.ds(HALO, n2, stride=2), :] + down1[:, pl.ds(HALO + 1, n2, stride=2), :]) * 0.125
    lane = lane_of(rhs2.shape[1:]) % 4
    mixed = rhs2[0]
    for i in range(1, n2):
        mixed = jnp.where(lane == i, roll(rhs2[i], i, 1), mixed)
    rhs_blocks[1, gy, first4] = mixed

    mine = rhs_blocks.at[1, gy, first4]
    for dx in (1, -1, 0):

        def spread(dx=dx):
            for o in sorted(range(1 if dx == 0 else 0, ny), key=lambda o: -min(o, ny - o)):
                pltpu.make_async_remote_copy(
                    mine, rhs_blocks.at[1 - dx, gy, first4], line_send.at[3 + dx], line_recv.at[3 + dx],
                    device_id=(gx + dx, lax.rem(gy + o, ny)), device_id_type=MESH,
                ).start()

        if dx == 0:
            spread()
        else:
            pl.when(has(dx, 0))(spread)

    told(2, *along_x)
    tell(3, *along_x)

    others = pl.ds(0, ny - 1)
    bytes_of(coef_blocks.at[1, others, :, first4], line_recv.at[0]).wait()
    passed = []
    for dx in (1, -1):
        src, dst = coef_blocks.at[1, :, :, first4], coef_blocks.at[1 - dx, :, :, first4]
        passed.append(remote(src, dst, line_send.at[(dx + 1) // 2 * 4 + 1], line_recv.at[(dx + 1) // 2 * 4 + 1], dx, 0))
    start(passed)

    def compacted(value, width, shift=0):
        rows = value.reshape((-1, LANES))
        count = LANES // width
        pick = lax.broadcasted_iota(jnp.int32, (LANES, count), 0) == shift + width * lax.broadcasted_iota(jnp.int32, (LANES, count), 1)
        out = jnp.dot(rows, pick.astype(F32), precision=lax.Precision.HIGHEST, preferred_element_type=F32)
        return out.reshape(value.shape[:-1] + (count,))

    own = pl.ds(HALO, n1)
    one_ref[...] = compacted(work1[7, own, own, :], 2)

    residue = lane_of(basis.shape[2:]) % 4

    def grouped(blocks, shift):
        out = None
        for q in range(4):
            moved = roll(blocks[q], q - shift, 1) if q != shift else blocks[q]
            out = moved if out is None else jnp.where(residue == q, moved, out)
        return out

    def joined(ref):
        side = lane_of((ref.shape[0], HALO, LANES)) % 4
        ref[:, head] = jnp.where(side != 0, roll(ref[:, pl.ds(wide, HALO)], 1, 2), 0.0)
        ref[:, tail] = jnp.where(side != 3, roll(ref[:, pl.ds(HALO, HALO)], -1, 2), 0.0)

    for copy, dx, _, _ in passed:
        pl.when(has(-dx, 0))(copy.wait_recv)
    for s in range(3):
        for b in range(ny):
            q, p = divmod(b, ny // 4)
            for i in range(n2):
                coef_cols[s, i, q, pl.ds(HALO + n2 * p, n2)] = coef_blocks[s, b, i, first4]
    for s in range(3):
        for i in range(n2):
            blocks = [coef_cols[s, i, q] * SHRINK for q in range(4)]
            for a, at in enumerate((0, 1, 2, 4)):
                coef2[at, n2 * s + i] = grouped(blocks, a)
    for at in (0, 1, 2, 4):
        joined(coef2.at[at])
    diag, bx_in, by_in = coef2[0], coef2[1], coef2[2]
    row = lax.broadcasted_iota(jnp.int32, diag.shape, 0)
    col = lax.broadcasted_iota(jnp.int32, diag.shape, 1)
    bxu = jnp.concatenate([bx_in[1:], jnp.zeros_like(bx_in[:1])], 0)
    byu = roll(by_in, -1, 1)
    coef2[0] = diag + jnp.where(row % n2 == n2 - 1, bxu, 0.0) + jnp.where(col % n2 == n2 - 1, byu, 0.0)
    coef2[3] = byu
    coef2[5] = roll(coef2[4], -4, 2)

    bytes_of(rhs_blocks.at[1, others, first4], line_recv.at[3]).wait()
    for s in (1, 0, 2):
        if s != 1:
            arriving = bytes_of(rhs_blocks.at[s, :, first4], line_recv.at[4 - s])
            pl.when(has(s - 1, 0))(arriving.wait)
        for b in range(ny):
            q, p = divmod(b, ny // 4)
            rhs_cols[s, q, pl.ds(HALO + n2 * p, n2)] = rhs_blocks[s, b, first4]
        blocks = [rhs_cols[s, q] for q in range(4)]
        for i in range(n2):
            basis[0, n2 * s + i] = grouped(blocks, i)
    joined(basis.at[0])
    for number in range(4):
        first, last = number + 1, n2 + 2 * HALO - number - 1
        here = pl.ds(first, last - first)
        x = basis[number, here]
        total = coef2[1, here] * basis[number, pl.ds(first - 1, last - first)]
        total = total + coef2[1, pl.ds(first + 1, last - first)] * basis[number, pl.ds(first + 1, last - first)]
        total = total + coef2[2, here] * roll(x, 1, 1) + coef2[3, here] * roll(x, -1, 1)
        total = total + coef2[4, here] * roll(x, 4, 2) + coef2[5, here] * roll(x, -4, 2)
        basis[number + 1, here] = coef2[0, here] * x - total

    own = pl.ds(HALO, n2)
    vectors = [basis[i, own, line, :] for i in range(5)]
    lane = lane_of((1, LANES))
    row = jnp.zeros((1, LANES), F32)
    for k in range(9):
        product = jnp.sum(vectors[k // 2] * vectors[(k + 1) // 2], axis=0)
        moment = jnp.sum(jnp.sum(product, axis=0, keepdims=True), axis=1, keepdims=True)
        row = jnp.where(lane == k, moment, row)

    def all_sum(row, slots, k, peer):
        slots[0] = row
        count = slots.shape[0] - 1
        for o in sorted(range(1, count + 1), key=lambda o: -min(o, count + 1 - o)):
            pltpu.make_async_remote_copy(
                slots.at[0], slots.at[o], row_send.at[k], row_recv.at[k], device_id=peer(o), device_id_type=MESH
            ).start()
        meanwhile()
        others = slots.at[pl.ds(1, count)]
        bytes_of(others, row_recv.at[k]).wait()
        return jnp.sum(slots[...], axis=0), bytes_of(others, row_send.at[k])

    def meanwhile():
        for which, copies in enumerate((sent0, sent1, sent2)):
            leave(copies, which)
        for copy, dx, _, _ in passed:
            pl.when(has(dx, 0))(copy.wait_send)
        for dx in (1, -1):
            pl.when(has(dx, 0))(bytes_of(rhs_blocks.at[1, :, first4], line_send.at[3 + dx]).wait)
        bytes_of(rhs_blocks.at[1, others, first4], line_send.at[3]).wait()
        bytes_of(coef_blocks.at[1, others, :, first4], line_send.at[0]).wait()
        store.wait()

    told(3, *along_x)
    row, sent5 = all_sum(row, gather_x, 0, peer_x)
    moments = [jnp.sum(jnp.where(lane == k, row, 0.0), axis=1, keepdims=True) for k in range(9)]

    def inner(u, w):
        total = None
        for i, a in enumerate(u):
            for j, b in enumerate(w):
                if a is not None and b is not None:
                    term = a * b * moments[i + j]
                    total = term if total is None else total + term
        return total

    def plus(u, c, w):
        out = []
        for a, b in zip(u, w):
            term = None if b is None else c * b
            out.append(a if term is None else term if a is None else a + term)
        return out

    def applied(u):
        return [None] + [None if a is None else a * (1.0 / SHRINK) for a in u[:-1]]

    shadow = [jnp.ones((1, 1), F32), None, None, None, None]
    solved = [None] * 5
    resid = direction = shadow
    rho = moments[0]
    for number in range(BICG):
        image = applied(direction)
        step = rho / inner(shadow, image)
        half = plus(resid, -step, image)
        turned = applied(half)
        omega = inner(turned, half) / inner(turned, turned)
        solved = plus(plus(solved, step, direction), omega, half)
        if number + 1 < BICG:
            resid = plus(half, -omega, turned)
            rho_next = inner(shadow, resid)
            factor = (rho_next / rho) * (step / omega)
            direction = plus(resid, factor, plus(direction, -omega, image))
            rho = rho_next

    total = None
    for i, c in enumerate(solved):
        if c is not None:
            term = c * vectors[i]
            total = term if total is None else total + term
    group, place = lax.div(gy, ny // 4), lax.rem(gy, ny // 4)
    mine = compacted(total, 4, group)
    bottom = mine[:, :n2]
    for p in range(1, ny // 4):
        bottom = jnp.where(place == p, mine[:, n2 * p : n2 * (p + 1)], bottom)
    bottom_ref[...] = bottom
    sent5.wait()


def per_device(right_side, alpha_cells, beta_x, beta_y, beta_z):
    nx, ny = lax.axis_size("gx"), lax.axis_size("gy")
    n0, _, nz = right_side.shape
    n1, n2 = n0 // 2, n0 // 4
    e0, e1, e2 = n0 + 2 * HALO, n1 + 2 * HALO, n2 + 2 * HALO
    anywhere = pl.BlockSpec(memory_space=pl.ANY)
    vmem = pl.BlockSpec(memory_space=pltpu.VMEM)

    def body(*refs):
        kernel(nx, ny, *refs)

    return pl.pallas_call(
        body,
        out_shape=(
            pltpu.VMEM((n0, n0, nz), F32),
            pltpu.VMEM((n1, n1, nz // 2), F32),
            pltpu.VMEM((n2, n2, nz // 4), F32),
        ),
        in_specs=[anywhere] * 5,
        out_specs=(vmem,) * 3,
        scratch_shapes=[
            pltpu.VMEM((5, n0, n0, nz), F32),
            pltpu.VMEM((5, e0, e0, nz), F32),
            pltpu.VMEM((8, e0, e0, nz), F32),
            pltpu.VMEM((5, n1 + 2, e0, nz), F32),
            pltpu.VMEM((2, e1, e1, nz), F32),
            pltpu.VMEM((3, e1, e1, nz), F32),
            pltpu.VMEM((8, e1, e1, nz), F32),
            pltpu.VMEM((e1 // 2, 2, e1, nz), F32),
            pltpu.VMEM((e1, e1, nz), F32),
            pltpu.VMEM((e1 // 2, e1, nz), F32),
            pltpu.VMEM((3, e1 // 2, e1, nz), F32),
            pltpu.VMEM((5, n2, e1, nz), F32),
            pltpu.VMEM((3, ny, n2, 8, nz), F32),
            pltpu.VMEM((3, n2, 4, 24, nz), F32),
            pltpu.VMEM((6, e2, 24, nz), F32),
            pltpu.VMEM((3, ny, 8, nz), F32),
            pltpu.VMEM((3, 4, 24, nz), F32),
            pltpu.VMEM((5, e2, 24, nz), F32),
            pltpu.VMEM((nx, 1, nz), F32),
            pltpu.VMEM((1024, nz), F32),
            pltpu.SemaphoreType.DMA,
            pltpu.SemaphoreType.DMA,
            pltpu.SemaphoreType.DMA((3,)),
            pltpu.SemaphoreType.DMA((3,)),
            pltpu.SemaphoreType.DMA((6,)),
            pltpu.SemaphoreType.DMA((6,)),
            pltpu.SemaphoreType.DMA((1,)),
            pltpu.SemaphoreType.DMA((1,)),
            pltpu.SemaphoreType.REGULAR((4,)),
            pltpu.SemaphoreType.REGULAR((4,)),
        ],
        compiler_params=pltpu.CompilerParams(collective_id=0, has_side_effects=True, vmem_limit_bytes=60 * 2**20),
        cost_estimate=pl.CostEstimate(flops=40_000_000, bytes_accessed=800_000, transcendentals=0),
        name="vcycle_down",
    )(right_side, alpha_cells, beta_x, beta_y, beta_z)


def solution(mesh):
    placed = P("gx", "gy", None)
    return jax.shard_map(per_device, mesh=mesh, in_specs=(placed,) * 5, out_specs=(placed,) * 3, check_vma=False)
```

```python
import jax
import jax.numpy as jnp
from jax import lax
from jax.experimental import pallas as pl
from jax.experimental.pallas import tpu as pltpu
from jax.sharding import PartitionSpec as P

MESH = pl.DeviceIdType.MESH
F32 = jnp.float32

BICG = 2
LMAX = 2.0
LMIN = 0.25
THETA = 0.5 * (LMAX + LMIN)
DELTA = 0.5 * (LMAX - LMIN)
SIGMA = THETA / DELTA

HALO = 4
LANES = 128
DIRECTIONS = ((1, 1), (1, -1), (-1, 1), (-1, -1), (0, 1), (0, -1), (1, 0), (-1, 0))
SHRINK = 0.125


def steps():
    rho = 1.0 / SIGMA
    out = []
    for _ in range(3):
        rho_next = 1.0 / (2.0 * SIGMA - rho)
        out.append((rho_next * rho, 2.0 * rho_next / DELTA))
        rho = rho_next
    return out


def lane_of(shape):
    return lax.broadcasted_iota(jnp.int32, shape, len(shape) - 1)


def roll(value, shift, axis):
    extent = value.shape[axis]
    return pltpu.roll(value, shift % extent, axis)


def spans(offset, own, depth=HALO, skip=0):
    if offset == 1:
        return pl.ds(own + HALO - skip - depth, depth), pl.ds(HALO - skip - depth, depth)
    if offset == -1:
        return pl.ds(HALO + skip, depth), pl.ds(own + HALO + skip, depth)
    return pl.ds(HALO, own), pl.ds(HALO, own)


def kernel(
    nx, ny,
    rhs_hbm, alpha_hbm, bx_hbm, by_hbm, bz_hbm,
    fine_ref, one_ref, bottom_ref,
    raw, ext0, work0, pair0,
    packed1, coef1, work1, rhs1, part1, send1, land1, pair1,
    coef_blocks, coef_cols, coef2, rhs_blocks, rhs_cols, basis,
    gather_x, tally,
    load_sem, out_sem, send_sem, recv_sem, line_send, line_recv, row_send, row_recv, known_x, known_y,
):
    gx = lax.axis_index("gx")
    gy = lax.axis_index("gy")
    n0, n1, n2 = raw.shape[1], raw.shape[1] // 2, raw.shape[1] // 4

    for i, src in enumerate((rhs_hbm, alpha_hbm, bx_hbm, by_hbm, bz_hbm)):
        pltpu.make_async_copy(src, raw.at[i], load_sem).start()

    def has(dx, dy):
        ok = None
        for step, at, count in ((dx, gx, nx), (dy, gy, ny)):
            if step != 0:
                this = at < count - 1 if step > 0 else at > 0
                ok = this if ok is None else jnp.logical_and(ok, this)
        return ok

    barrier = pltpu.get_barrier_semaphore()
    greeted = jnp.int32(4)
    for dx, dy in DIRECTIONS[:4]:
        there = has(dx, dy)
        greeted = greeted + there.astype(jnp.int32)

        @pl.when(there)
        def _(dx=dx, dy=dy):
            pl.semaphore_signal(barrier, inc=1, device_id=(gx + dx, gy + dy), device_id_type=MESH)

    def peer_y(o):
        return (gx, lax.rem(gy + o + ny, ny))

    def peer_x(o):
        return (lax.rem(gx + o + nx, nx), gy)

    for o in (1, -1):
        pl.semaphore_signal(barrier, inc=1, device_id=peer_x(o), device_id_type=MESH)
        pl.semaphore_signal(barrier, inc=1, device_id=peer_y(o), device_id_type=MESH)

    def tell(number, sems, peer, count):
        if 2**number < count // 2:
            for o in (2**number, -(2**number)):
                pl.semaphore_signal(sems.at[number], inc=1, device_id=peer(o), device_id_type=MESH)

    def told(number, sems, peer, count):
        if 2**number < count // 2:
            pl.semaphore_wait(sems.at[number], 2)

    along_x, along_y = (known_x, peer_x, nx), (known_y, peer_y, ny)

    def remote(src, dst, ssem, rsem, dx, dy):
        copy = pltpu.make_async_remote_copy(src, dst, ssem, rsem, device_id=(gx + dx, gy + dy), device_id_type=MESH)
        rows = 1
        for extent in dst.shape[:-1]:
            rows *= extent
        return copy, dx, dy, rows

    def exchange(which, part):
        return [remote(*part(dx, dy), send_sem.at[which], recv_sem.at[which], dx, dy) for dx, dy in DIRECTIONS]

    def exchange_fine(ref, own):
        out = []
        deep = HALO - 1

        def add(src, dst, dx, dy):
            out.append(remote(src, dst, send_sem.at[0], recv_sem.at[0], dx, dy))

        for dx, dy in DIRECTIONS[:4]:
            (sx, tx), (sy, ty) = spans(dx, own, deep - 1), spans(dy, own, deep - 1)
            add(ref.at[:, sx, sy], ref.at[:, tx, ty], dx, dy)
            if dy == -1:
                (sx, tx), (sy, ty) = spans(dx, own, 1, deep - 1), spans(dy, own, 1)
                add(ref.at[0, sx, sy], ref.at[0, tx, ty], dx, dy)
            if dx == -1:
                (sx, tx), (sy, ty) = spans(dx, own, 1), spans(dy, own, 1, deep - 1)
                add(ref.at[3, sx, sy], ref.at[3, tx, ty], dx, dy)
        whole = pl.ds(HALO, own)
        for dy in (1, -1):
            sy, ty = spans(dy, own, deep)
            add(ref.at[pl.ds(0, 3), whole, sy], ref.at[pl.ds(0, 3), whole, ty], 0, dy)
            sy, ty = spans(dy, own, deep - 1)
            add(ref.at[pl.ds(3, 2), whole, sy], ref.at[pl.ds(3, 2), whole, ty], 0, dy)
        for dx in (1, -1):
            sx, tx = spans(dx, own, deep)
            add(ref.at[:, sx, whole], ref.at[:, tx, whole], dx, 0)
        return out

    def start(copies):
        for copy, dx, dy, _ in copies:
            pl.when(has(dx, dy))(copy.start)

    def bytes_of(ref, sem):
        return pltpu.make_async_copy(ref, ref, sem)

    def settle(copies, sem, way):
        def waits(ex, ey):
            rows = sum(r for _, dx, dy, r in copies if (ex == 0 or way * dx != ex) and (ey == 0 or way * dy != ey))
            bytes_of(tally.at[pl.ds(0, rows)], sem).wait()

        def where(at, count):
            return {-1: at == 0, 0: jnp.logical_and(at > 0, at < count - 1), 1: at == count - 1}

        at_x, at_y = where(gx, nx), where(gy, ny)
        inside = jnp.logical_and(at_x[0], at_y[0])
        pl.when(inside)(lambda: waits(0, 0))

        @pl.when(jnp.logical_not(inside))
        def _():
            for ex in (-1, 0, 1):
                for ey in (-1, 0, 1):
                    if (ex, ey) != (0, 0):
                        pl.when(jnp.logical_and(at_x[ex], at_y[ey]))(lambda ex=ex, ey=ey: waits(ex, ey))

    def arrive(copies, which):
        settle(copies, recv_sem.at[which], -1)

    def leave(copies, which):
        settle(copies, send_sem.at[which], 1)

    x_inner = jnp.where(gx > 0, 1.0, 0.0).astype(F32)

    def own_coefs(alpha, bx, by, bz, scale, width):
        n = bx.shape[0]
        col = lax.broadcasted_iota(jnp.int32, bx.shape, 1)
        bz_in = jnp.where(lane_of(bx.shape) < width, 0.0, bz)
        bxu = jnp.concatenate([bx[1:], jnp.zeros_like(bx[:1])], 0)
        byu = jnp.where(col == n - 1, 0.0, roll(by, -1, 1))
        diag = alpha + scale * (bx + bxu + by + byu + bz + roll(bz_in, -width, 2))
        by_in = jnp.where(jnp.logical_and(col == 0, gy == 0), 0.0, by)
        bx_in = jnp.concatenate([bx[:1] * x_inner, bx[1:]], 0)
        return diag, bx_in, by_in, bz_in

    for ref in (part1, land1):
        ref[...] = jnp.zeros(ref.shape, F32)

    pltpu.make_async_copy(raw, raw, load_sem).wait()

    own = pl.ds(HALO, n0)
    diag, bx_in, by_in, bz_in = own_coefs(raw[1], raw[2], raw[3], raw[4], 16.0, 1)
    for i, v in enumerate((by_in, raw[0], diag, bx_in, bz_in)):
        ext0[i, own, own, :] = v

    pl.semaphore_wait(barrier, greeted)
    sent0 = exchange_fine(ext0, n0)
    start(sent0)
    tell(0, *along_x)
    tell(0, *along_y)

    def halves(ref, n):
        return ref[pl.ds(0, n), pl.ds(0, n, stride=2), :], ref[pl.ds(0, n), pl.ds(1, n, stride=2), :]

    def coarsen(alpha, bx, by, bz, pairs, width):
        n = bx.shape[0] // 2

        def xs(v):
            w = v.reshape((n, 2) + v.shape[1:])
            return w[:, 0], w[:, 1]

        def zsum(v):
            return v + roll(v, -width, 2)

        pairs[0, pl.ds(0, n), pl.ds(0, 2 * n)] = zsum(sum(xs(alpha)))
        pairs[1, pl.ds(0, n), pl.ds(0, 2 * n)] = zsum(xs(bx)[0])
        pairs[2, pl.ds(0, n), pl.ds(0, 2 * n)] = zsum(sum(xs(by)))
        pairs[3, pl.ds(0, n), pl.ds(0, 2 * n)] = sum(xs(bz))
        a0, a1 = halves(pairs.at[0], n)
        x0, x1 = halves(pairs.at[1], n)
        y0, _ = halves(pairs.at[2], n)
        z0, z1 = halves(pairs.at[3], n)
        return (a0 + a1) * 0.125, (x0 + x1) * 0.25, y0 * 0.25, (z0 + z1) * 0.25

    alpha1, bx1, by1, bz1 = coarsen(raw[1], raw[2], raw[3], raw[4], pair0, 1)
    diag, bx_in, by_in, bz_in = own_coefs(alpha1, bx1, by1, bz1, 4.0, 2)
    own = pl.ds(HALO, n1)
    lane = lane_of(diag.shape)
    packed1[0, own, own, :] = jnp.where(lane % 2 == 0, diag, roll(bx_in, 1, 2))
    packed1[1, own, own, :] = jnp.where(lane % 2 == 0, by_in, roll(bz_in, 1, 2))

    alpha2, bx2, by2, bz2 = coarsen(alpha1, bx1, by1, bz1, pair1, 2)
    diag, bx_in, by_in, bz_in = own_coefs(alpha2, bx2, by2, bz2, 1.0, 4)
    lane = lane_of(diag.shape) % 4
    mixed = jnp.where(lane < 2, jnp.where(lane == 0, diag, roll(bx_in, 1, 2)), jnp.where(lane == 2, roll(by_in, 2, 2), roll(bz_in, 3, 2)))
    first4 = pl.ds(0, n2)
    coef_blocks[1, gy, :, first4] = mixed

    def edges(dx, dy):
        (sx, tx), (sy, ty) = spans(dx, n1), spans(dy, n1)
        return packed1.at[:, sx, sy], packed1.at[:, tx, ty]

    sent1 = exchange(1, edges)
    start(sent1)

    def border(ref, index, n, value):
        for flag, at in ((gx == 0, 0), (gx == nx - 1, n + HALO)):

            @pl.when(flag)
            def _(at=at):
                ref[index + (pl.ds(at, HALO),)] = value((HALO, n + 2 * HALO, LANES))

        for flag, at in ((gy == 0, 0), (gy == ny - 1, n + HALO)):

            @pl.when(flag)
            def _(at=at):
                ref[index + (slice(None), pl.ds(at, HALO))] = value((n + 2 * HALO, HALO, LANES))

    def zeros(shape):
        return jnp.zeros(shape, F32)

    def ones(every):
        return lambda shape: jnp.where(lane_of(shape) % every == 0, 1.0, 0.0).astype(F32)

    for i in (0, 1, 3, 4):
        border(ext0, (i,), n0, zeros)
    border(ext0, (2,), n0, ones(1))
    border(packed1, (0,), n1, ones(2))
    border(packed1, (1,), n1, zeros)
    for flag, at in ((gx == 0, 0), (gx == nx - 1, 2)):

        @pl.when(flag)
        def _(at=at):
            coef_blocks[at] = zeros(coef_blocks.shape[1:])
            rhs_blocks[at] = zeros(rhs_blocks.shape[1:])

    wide = n2 * (ny // 4)
    line, head, tail = pl.ds(HALO, wide), pl.ds(0, HALO), pl.ds(HALO + wide, HALO)
    for ref in (coef_cols, rhs_cols):
        for part in (head, tail):
            at = (slice(None),) * (len(ref.shape) - 2) + (part,)
            ref[at] = zeros(ref.shape[:-2] + (HALO, LANES))

    told(0, *along_y)
    tell(1, *along_y)

    def whole_diag(part, bx, by, n, scale):
        rows = part.shape[0]
        row = lax.broadcasted_iota(jnp.int32, part.shape, 0)
        col = lax.broadcasted_iota(jnp.int32, part.shape, 1)
        at_x = jnp.logical_or(row == HALO - 1, row == HALO + n - 1)
        at_y = jnp.logical_or(col == HALO - 1, col == HALO + n - 1)
        bxu = jnp.concatenate([bx[1:rows], jnp.zeros_like(bx[:1])], 0)
        return part + scale * (jnp.where(at_x, bxu, 0.0) + jnp.where(at_y, roll(by, -1, 1), 0.0))

    def sweep(number, first, rows, faces, work, width, finish, clip=None):
        coefs = steps()
        source, target = 6 + number % 2, 7 - number % 2

        def body(i, carry):
            at = first + i * rows[1]
            here = pl.ds(at, rows[1])
            x = work[source, here]
            total = faces[0][here] * work[source, pl.ds(at - 1, rows[1])]
            total = total + faces[0][pl.ds(at + 1, rows[1])] * work[source, pl.ds(at + 1, rows[1])]
            total = total + faces[1][here] * roll(x, 1, 1) + work[2, here] * roll(x, -1, 1)
            total = total + faces[2][here] * roll(x, width, 2) + work[3, here] * roll(x, -width, 2)
            if number == 3:
                finish(at, rows[1], work[4, here], work[1, here] - x, work[0, here], total)
            else:
                a, b = coefs[number]
                scaled = work[1, here] - x + work[0, here] * total
                update = a * (x if number == 0 else work[5, here]) + b * scaled
                x = x + update
                if clip is not None:
                    col = lax.broadcasted_iota(jnp.int32, x.shape, 1)
                    x = jnp.where(jnp.logical_and(col >= HALO, col < HALO + clip), x, 0.0)
                work[5, here] = update
                work[target, here] = x
            return carry

        lax.fori_loop(0, rows[0], body, 0, unroll=True)

    def prepare(faces, work, diag, scale, width):
        inverse = 1.0 / diag
        work[0] = scale * inverse
        work[2] = roll(faces[1][...], -1, 1)
        work[3] = roll(faces[2][...], -width, 2)
        work[4] = diag

    def begin(work, rhs, scale):
        work[1] = work[0] * rhs * (1.0 / scale)
        work[6] = work[1] * (1.0 / THETA)

    arrive(sent0, 0)
    told(0, *along_x)
    tell(1, *along_x)
    told(1, *along_y)
    tell(2, *along_y)
    faces0 = (ext0.at[3], ext0.at[0], ext0.at[4])
    prepare(faces0, work0, whole_diag(ext0[2], ext0[3], ext0[0], n0, 16.0), 16.0, 1)
    begin(work0, ext0[1], 16.0)

    def halve(pairs, first, width):
        def finish(at, resid):
            rows = resid.shape[0] // 2
            summed = resid.reshape((rows, 2) + resid.shape[1:])
            summed = summed[:, 0] + summed[:, 1]
            pairs[pl.ds(lax.div(at - first, 2), rows)] = summed + roll(summed, -width, 2)

        return finish

    down0 = pair0.at[4]
    keep0 = halve(down0, 2, 1)

    def partial(at, rows, diag, gap, scaled, total):
        row = at + lax.broadcasted_iota(jnp.int32, gap.shape, 0)
        col = lax.broadcasted_iota(jnp.int32, gap.shape, 1)
        in_x = jnp.logical_and(row >= HALO, row < HALO + n0)
        in_y = jnp.logical_and(col >= HALO, col < HALO + n0)
        near_y = jnp.logical_and(col >= HALO - 2, col < HALO + n0 + 2)
        mine = jnp.where(jnp.logical_and(in_x, in_y), diag * gap, 0.0)
        keep0(at, mine + jnp.where(jnp.logical_or(in_y, jnp.logical_and(in_x, near_y)), 16.0 * total, 0.0))

    sweep(0, 2, (5, 4), faces0, work0, 1, None)
    sweep(1, 3, (3, 6), faces0, work0, 1, None)
    sweep(2, 4, (4, 4), faces0, work0, 1, None, n0)
    for at in (1, HALO + n0):
        work0[7, pl.ds(at, 3)] = jnp.zeros((3,) + work0.shape[2:], F32)
    sweep(3, 2, (5, 4), faces0, work0, 1, partial)
    count = n1 + HALO
    terms = (down0[:, pl.ds(0, count, stride=2), :] + down0[:, pl.ds(1, count, stride=2), :]) * 0.125
    part1[pl.ds(HALO - 1, n1 + 2), pl.ds(HALO - 2, count), :] = terms
    halved = part1[...].reshape(rhs1.shape)
    even = lane_of(send1.shape) % 2 == 0
    send1[...] = jnp.where(even, halved[:, 0], roll(halved[:, 1], 1, 2))

    def outer(dx, dy):
        half = n1 // 2
        sx, tx = {
            0: (pl.ds(1, half + 2), pl.ds(1, half + 2)),
            1: (pl.ds(half, 3), pl.ds(0, 3)),
            -1: (pl.ds(1, 3), pl.ds(half + 1, 3)),
        }[dx]
        wide = HALO + 1
        sy, ty = {
            0: (pl.ds(HALO - 1, n1 + 2), pl.ds(HALO - 1, n1 + 2)),
            1: (pl.ds(n1 + HALO + 1 - wide, wide), pl.ds(HALO + 1 - wide, wide)),
            -1: (pl.ds(HALO - 1, wide), pl.ds(HALO - 1 + n1, wide)),
        }[dy]
        land = land1.at[2 if dx * dy != 0 else 1 if dx != 0 else 0]
        return send1.at[sx, sy], land.at[tx, ty]

    sent2 = exchange(2, outer)
    start(sent2)

    told(2, *along_y)
    mine = coef_blocks.at[1, gy, :, first4]
    for o in range(1, ny):
        pltpu.make_async_remote_copy(
            mine, mine, line_send.at[0], line_recv.at[0], device_id=peer_y(o), device_id_type=MESH
        ).start()

    own = pl.ds(HALO, n0)
    store = pltpu.make_async_copy(work0.at[7, own, own], fine_ref, out_sem)
    store.start()

    arrive(sent1, 1)
    even = lane_of(packed1.shape[1:]) % 2 == 0
    part = jnp.where(even, packed1[0], 1.0)
    coef1[0] = roll(packed1[0], -1, 2)
    coef1[1] = packed1[1]
    coef1[2] = roll(packed1[1], -1, 2)
    faces1 = (coef1.at[0], coef1.at[1], coef1.at[2])
    prepare(faces1, work1, whole_diag(part, coef1[0], coef1[1], n1, 4.0), 4.0, 2)

    arrive(sent2, 2)
    told(1, *along_x)
    tell(2, *along_x)
    summed = send1[...] + land1[0] + land1[1] + land1[2]
    rhs1[:, 0] = summed
    rhs1[:, 1] = roll(summed, -1, 2)
    begin(work1, rhs1[...].reshape(part1.shape), 4.0)
    down1 = pair1.at[4]
    keep1 = halve(down1, HALO, 2)

    def whole(at, rows, diag, gap, scaled, total):
        keep1(at, diag * (gap + scaled * total))

    for number, rows in enumerate(((2, 7), (2, 6), (2, 5), (2, 4))):
        sweep(number, number + 1, rows, faces1, work1, 2, whole)
    rhs2 = (down1[:, pl.ds(HALO, n2, stride=2), :] + down1[:, pl.ds(HALO + 1, n2, stride=2), :]) * 0.125
    lane = lane_of(rhs2.shape[1:]) % 4
    mixed = rhs2[0]
    for i in range(1, n2):
        mixed = jnp.where(lane == i, roll(rhs2[i], i, 1), mixed)
    rhs_blocks[1, gy, first4] = mixed

    mine = rhs_blocks.at[1, gy, first4]
    for dx in (0, 1, -1):

        def spread(dx=dx):
            for o in sorted(range(1 if dx == 0 else 0, ny), key=lambda o: -min(o, ny - o)):
                pltpu.make_async_remote_copy(
                    mine, rhs_blocks.at[1 - dx, gy, first4], line_send.at[3 + dx], line_recv.at[3 + dx],
                    device_id=(gx + dx, lax.rem(gy + o, ny)), device_id_type=MESH,
                ).start()

        if dx == 0:
            spread()
        else:
            pl.when(has(dx, 0))(spread)

    told(2, *along_x)
    tell(3, *along_x)

    others = pl.ds(0, ny - 1)
    bytes_of(coef_blocks.at[1, others, :, first4], line_recv.at[0]).wait()
    passed = []
    for dx in (1, -1):
        src, dst = coef_blocks.at[1, :, :, first4], coef_blocks.at[1 - dx, :, :, first4]
        passed.append(remote(src, dst, line_send.at[(dx + 1) // 2 * 4 + 1], line_recv.at[(dx + 1) // 2 * 4 + 1], dx, 0))
    start(passed)

    def compacted(value, width, shift=0):
        rows = value.reshape((-1, LANES))
        count = LANES // width
        pick = lax.broadcasted_iota(jnp.int32, (LANES, count), 0) == shift + width * lax.broadcasted_iota(jnp.int32, (LANES, count), 1)
        out = jnp.dot(rows, pick.astype(F32), precision=lax.Precision.HIGHEST, preferred_element_type=F32)
        return out.reshape(value.shape[:-1] + (count,))

    own = pl.ds(HALO, n1)
    one_ref[...] = compacted(work1[7, own, own, :], 2)

    residue = lane_of(basis.shape[2:]) % 4

    def grouped(blocks, shift):
        out = None
        for q in range(4):
            moved = roll(blocks[q], q - shift, 1) if q != shift else blocks[q]
            out = moved if out is None else jnp.where(residue == q, moved, out)
        return out

    def joined(ref):
        side = lane_of((ref.shape[0], HALO, LANES)) % 4
        ref[:, head] = jnp.where(side != 0, roll(ref[:, pl.ds(wide, HALO)], 1, 2), 0.0)
        ref[:, tail] = jnp.where(side != 3, roll(ref[:, pl.ds(HALO, HALO)], -1, 2), 0.0)

    for copy, dx, _, _ in passed:
        pl.when(has(-dx, 0))(copy.wait_recv)
    for s in range(3):
        for b in range(ny):
            q, p = divmod(b, ny // 4)
            for i in range(n2):
                coef_cols[s, i, q, pl.ds(HALO + n2 * p, n2)] = coef_blocks[s, b, i, first4]
    for s in range(3):
        for i in range(n2):
            blocks = [coef_cols[s, i, q] * SHRINK for q in range(4)]
            for a, at in enumerate((0, 1, 2, 4)):
                coef2[at, n2 * s + i] = grouped(blocks, a)
    for at in (0, 1, 2, 4):
        joined(coef2.at[at])
    diag, bx_in, by_in = coef2[0], coef2[1], coef2[2]
    row = lax.broadcasted_iota(jnp.int32, diag.shape, 0)
    col = lax.broadcasted_iota(jnp.int32, diag.shape, 1)
    bxu = jnp.concatenate([bx_in[1:], jnp.zeros_like(bx_in[:1])], 0)
    byu = roll(by_in, -1, 1)
    coef2[0] = diag + jnp.where(row % n2 == n2 - 1, bxu, 0.0) + jnp.where(col % n2 == n2 - 1, byu, 0.0)
    coef2[3] = byu
    coef2[5] = roll(coef2[4], -4, 2)

    bytes_of(rhs_blocks.at[1, others, first4], line_recv.at[3]).wait()
    for s in (1, 0, 2):
        if s != 1:
            arriving = bytes_of(rhs_blocks.at[s, :, first4], line_recv.at[4 - s])
            pl.when(has(s - 1, 0))(arriving.wait)
        for b in range(ny):
            q, p = divmod(b, ny // 4)
            rhs_cols[s, q, pl.ds(HALO + n2 * p, n2)] = rhs_blocks[s, b, first4]
        blocks = [rhs_cols[s, q] for q in range(4)]
        for i in range(n2):
            basis[0, n2 * s + i] = grouped(blocks, i)
    joined(basis.at[0])
    for number in range(4):
        first, last = number + 1, n2 + 2 * HALO - number - 1
        here = pl.ds(first, last - first)
        x = basis[number, here]
        total = coef2[1, here] * basis[number, pl.ds(first - 1, last - first)]
        total = total + coef2[1, pl.ds(first + 1, last - first)] * basis[number, pl.ds(first + 1, last - first)]
        total = total + coef2[2, here] * roll(x, 1, 1) + coef2[3, here] * roll(x, -1, 1)
        total = total + coef2[4, here] * roll(x, 4, 2) + coef2[5, here] * roll(x, -4, 2)
        basis[number + 1, here] = coef2[0, here] * x - total

    own = pl.ds(HALO, n2)
    vectors = [basis[i, own, line, :] for i in range(5)]
    lane = lane_of((1, LANES))
    row = jnp.zeros((1, LANES), F32)
    for k in range(9):
        product = jnp.sum(vectors[k // 2] * vectors[(k + 1) // 2], axis=0)
        moment = jnp.sum(jnp.sum(product, axis=0, keepdims=True), axis=1, keepdims=True)
        row = jnp.where(lane == k, moment, row)

    def all_sum(row, slots, k, peer):
        slots[0] = row
        count = slots.shape[0] - 1
        for o in sorted(range(1, count + 1), key=lambda o: -min(o, count + 1 - o)):
            pltpu.make_async_remote_copy(
                slots.at[0], slots.at[o], row_send.at[k], row_recv.at[k], device_id=peer(o), device_id_type=MESH
            ).start()
        meanwhile()
        others = slots.at[pl.ds(1, count)]
        bytes_of(others, row_recv.at[k]).wait()
        total = slots[...]
        while total.shape[0] > 1:
            half = total.shape[0] // 2
            total = total[:half] + total[half:]
        return total[0], bytes_of(others, row_send.at[k])

    def meanwhile():
        for which, copies in enumerate((sent0, sent1, sent2)):
            leave(copies, which)
        for copy, dx, _, _ in passed:
            pl.when(has(dx, 0))(copy.wait_send)
        for dx in (1, -1):
            pl.when(has(dx, 0))(bytes_of(rhs_blocks.at[1, :, first4], line_send.at[3 + dx]).wait)
        bytes_of(rhs_blocks.at[1, others, first4], line_send.at[3]).wait()
        bytes_of(coef_blocks.at[1, others, :, first4], line_send.at[0]).wait()
        store.wait()

    told(3, *along_x)
    row, sent5 = all_sum(row, gather_x, 0, peer_x)
    moments = [jnp.sum(jnp.where(lane == k, row, 0.0), axis=1, keepdims=True) for k in range(9)]

    def balanced(terms):
        while len(terms) > 1:
            pairs = [a + b for a, b in zip(terms[0::2], terms[1::2])]
            terms = pairs + terms[2 * len(pairs) :]
        return terms[0]

    def inner(u, w):
        return balanced([
            a * balanced([b * moments[i + j] for j, b in enumerate(w) if b is not None])
            for i, a in enumerate(u) if a is not None
        ])

    def plus(u, c, w):
        out = []
        for a, b in zip(u, w):
            term = None if b is None else c * b
            out.append(a if term is None else term if a is None else a + term)
        return out

    def applied(u):
        return [None] + [None if a is None else a * (1.0 / SHRINK) for a in u[:-1]]

    shadow = [jnp.ones((1, 1), F32), None, None, None, None]
    solved = [None] * 5
    resid = direction = shadow
    rho = moments[0]
    for number in range(BICG):
        image = applied(direction)
        step = rho / inner(shadow, image)
        half = plus(resid, -step, image)
        turned = applied(half)
        omega = inner(turned, half) / inner(turned, turned)
        solved = plus(plus(solved, step, direction), omega, half)
        if number + 1 < BICG:
            resid = plus(half, -omega, turned)
            rho_next = inner(shadow, resid)
            factor = (rho_next / rho) * (step / omega)
            direction = plus(resid, factor, plus(direction, -omega, image))
            rho = rho_next

    total = None
    for i, c in enumerate(solved):
        if c is not None:
            term = c * vectors[i]
            total = term if total is None else total + term
    group, place = lax.div(gy, ny // 4), lax.rem(gy, ny // 4)
    mine = compacted(total, 4, group)
    bottom = mine[:, :n2]
    for p in range(1, ny // 4):
        bottom = jnp.where(place == p, mine[:, n2 * p : n2 * (p + 1)], bottom)
    bottom_ref[...] = bottom
    sent5.wait()


def per_device(right_side, alpha_cells, beta_x, beta_y, beta_z):
    nx, ny = lax.axis_size("gx"), lax.axis_size("gy")
    n0, _, nz = right_side.shape
    n1, n2 = n0 // 2, n0 // 4
    e0, e1, e2 = n0 + 2 * HALO, n1 + 2 * HALO, n2 + 2 * HALO
    anywhere = pl.BlockSpec(memory_space=pl.ANY)
    vmem = pl.BlockSpec(memory_space=pltpu.VMEM)

    def body(*refs):
        kernel(nx, ny, *refs)

    return pl.pallas_call(
        body,
        out_shape=(
            pltpu.VMEM((n0, n0, nz), F32),
            pltpu.VMEM((n1, n1, nz // 2), F32),
            pltpu.VMEM((n2, n2, nz // 4), F32),
        ),
        in_specs=[anywhere] * 5,
        out_specs=(vmem,) * 3,
        scratch_shapes=[
            pltpu.VMEM((5, n0, n0, nz), F32),
            pltpu.VMEM((5, e0, e0, nz), F32),
            pltpu.VMEM((8, e0, e0, nz), F32),
            pltpu.VMEM((5, n1 + 2, e0, nz), F32),
            pltpu.VMEM((2, e1, e1, nz), F32),
            pltpu.VMEM((3, e1, e1, nz), F32),
            pltpu.VMEM((8, e1, e1, nz), F32),
            pltpu.VMEM((e1 // 2, 2, e1, nz), F32),
            pltpu.VMEM((e1, e1, nz), F32),
            pltpu.VMEM((e1 // 2, e1, nz), F32),
            pltpu.VMEM((3, e1 // 2, e1, nz), F32),
            pltpu.VMEM((5, n2, e1, nz), F32),
            pltpu.VMEM((3, ny, n2, 8, nz), F32),
            pltpu.VMEM((3, n2, 4, 24, nz), F32),
            pltpu.VMEM((6, e2, 24, nz), F32),
            pltpu.VMEM((3, ny, 8, nz), F32),
            pltpu.VMEM((3, 4, 24, nz), F32),
            pltpu.VMEM((5, e2, 24, nz), F32),
            pltpu.VMEM((nx, 1, nz), F32),
            pltpu.VMEM((1024, nz), F32),
            pltpu.SemaphoreType.DMA,
            pltpu.SemaphoreType.DMA,
            pltpu.SemaphoreType.DMA((3,)),
            pltpu.SemaphoreType.DMA((3,)),
            pltpu.SemaphoreType.DMA((6,)),
            pltpu.SemaphoreType.DMA((6,)),
            pltpu.SemaphoreType.DMA((1,)),
            pltpu.SemaphoreType.DMA((1,)),
            pltpu.SemaphoreType.REGULAR((4,)),
            pltpu.SemaphoreType.REGULAR((4,)),
        ],
        compiler_params=pltpu.CompilerParams(collective_id=0, has_side_effects=True, vmem_limit_bytes=60 * 2**20),
        cost_estimate=pl.CostEstimate(flops=40_000_000, bytes_accessed=800_000, transcendentals=0),
        name="vcycle_down",
    )(right_side, alpha_cells, beta_x, beta_y, beta_z)


def solution(mesh):
    placed = P("gx", "gy", None)
    return jax.shard_map(per_device, mesh=mesh, in_specs=(placed,) * 5, out_specs=(placed,) * 3, check_vma=False)
```

```python
import jax
import jax.numpy as jnp
from jax import lax
from jax.experimental import pallas as pl
from jax.experimental.pallas import tpu as pltpu
from jax.sharding import PartitionSpec as P

MESH = pl.DeviceIdType.MESH
F32 = jnp.float32

BICG = 2
LMAX = 2.0
LMIN = 0.25
THETA = 0.5 * (LMAX + LMIN)
DELTA = 0.5 * (LMAX - LMIN)
SIGMA = THETA / DELTA

HALO = 4
LANES = 128
DIRECTIONS = ((1, 1), (1, -1), (-1, 1), (-1, -1), (0, 1), (0, -1), (1, 0), (-1, 0))
SHRINK = 0.125


def steps():
    rho = 1.0 / SIGMA
    out = []
    for _ in range(3):
        rho_next = 1.0 / (2.0 * SIGMA - rho)
        out.append((rho_next * rho, 2.0 * rho_next / DELTA))
        rho = rho_next
    return out


def lane_of(shape):
    return lax.broadcasted_iota(jnp.int32, shape, len(shape) - 1)


def roll(value, shift, axis):
    extent = value.shape[axis]
    return pltpu.roll(value, shift % extent, axis)


def spans(offset, own, depth=HALO, skip=0):
    if offset == 1:
        return pl.ds(own + HALO - skip - depth, depth), pl.ds(HALO - skip - depth, depth)
    if offset == -1:
        return pl.ds(HALO + skip, depth), pl.ds(own + HALO + skip, depth)
    return pl.ds(HALO, own), pl.ds(HALO, own)


def kernel(
    nx, ny,
    rhs_hbm, alpha_hbm, bx_hbm, by_hbm, bz_hbm,
    fine_ref, one_ref, bottom_ref,
    raw, ext0, work0, pair0,
    packed1, coef1, work1, rhs1, part1, send1, land1, pair1,
    coef_blocks, coef_cols, coef2, rhs_blocks, rhs_cols, basis,
    gather_x, tally,
    load_sem, out_sem, send_sem, recv_sem, line_send, line_recv, row_send, row_recv, known_x, known_y,
):
    gx = lax.axis_index("gx")
    gy = lax.axis_index("gy")
    n0, n1, n2 = raw.shape[1], raw.shape[1] // 2, raw.shape[1] // 4

    for i, src in enumerate((rhs_hbm, alpha_hbm, bx_hbm, by_hbm, bz_hbm)):
        pltpu.make_async_copy(src, raw.at[i], load_sem).start()

    def has(dx, dy):
        ok = None
        for step, at, count in ((dx, gx, nx), (dy, gy, ny)):
            if step != 0:
                this = at < count - 1 if step > 0 else at > 0
                ok = this if ok is None else jnp.logical_and(ok, this)
        return ok

    barrier = pltpu.get_barrier_semaphore()
    greeted = jnp.int32(4)
    for dx, dy in DIRECTIONS[:4]:
        there = has(dx, dy)
        greeted = greeted + there.astype(jnp.int32)

        @pl.when(there)
        def _(dx=dx, dy=dy):
            pl.semaphore_signal(barrier, inc=1, device_id=(gx + dx, gy + dy), device_id_type=MESH)

    def peer_y(o):
        return (gx, lax.rem(gy + o + ny, ny))

    def peer_x(o):
        return (lax.rem(gx + o + nx, nx), gy)

    for o in (1, -1):
        pl.semaphore_signal(barrier, inc=1, device_id=peer_x(o), device_id_type=MESH)
        pl.semaphore_signal(barrier, inc=1, device_id=peer_y(o), device_id_type=MESH)

    def tell(number, sems, peer, count):
        if 2**number < count // 2:
            for o in (2**number, -(2**number)):
                pl.semaphore_signal(sems.at[number], inc=1, device_id=peer(o), device_id_type=MESH)

    def told(number, sems, peer, count):
        if 2**number < count // 2:
            pl.semaphore_wait(sems.at[number], 2)

    along_x, along_y = (known_x, peer_x, nx), (known_y, peer_y, ny)

    def remote(src, dst, ssem, rsem, dx, dy):
        copy = pltpu.make_async_remote_copy(src, dst, ssem, rsem, device_id=(gx + dx, gy + dy), device_id_type=MESH)
        rows = 1
        for extent in dst.shape[:-1]:
            rows *= extent
        return copy, dx, dy, rows

    def exchange(which, part):
        return [remote(*part(dx, dy), send_sem.at[which], recv_sem.at[which], dx, dy) for dx, dy in DIRECTIONS]

    def exchange_fine(ref, own):
        out = []
        deep = HALO - 1

        def add(src, dst, dx, dy):
            out.append(remote(src, dst, send_sem.at[0], recv_sem.at[0], dx, dy))

        for dx, dy in DIRECTIONS[:4]:
            (sx, tx), (sy, ty) = spans(dx, own, deep - 1), spans(dy, own, deep - 1)
            add(ref.at[:, sx, sy], ref.at[:, tx, ty], dx, dy)
            if dy == -1:
                (sx, tx), (sy, ty) = spans(dx, own, 1, deep - 1), spans(dy, own, 1)
                add(ref.at[0, sx, sy], ref.at[0, tx, ty], dx, dy)
            if dx == -1:
                (sx, tx), (sy, ty) = spans(dx, own, 1), spans(dy, own, 1, deep - 1)
                add(ref.at[3, sx, sy], ref.at[3, tx, ty], dx, dy)
        whole = pl.ds(HALO, own)
        for dy in (1, -1):
            sy, ty = spans(dy, own, deep)
            add(ref.at[pl.ds(0, 3), whole, sy], ref.at[pl.ds(0, 3), whole, ty], 0, dy)
            sy, ty = spans(dy, own, deep - 1)
            add(ref.at[pl.ds(3, 2), whole, sy], ref.at[pl.ds(3, 2), whole, ty], 0, dy)
        for dx in (1, -1):
            sx, tx = spans(dx, own, deep)
            add(ref.at[:, sx, whole], ref.at[:, tx, whole], dx, 0)
        return out

    def start(copies):
        for copy, dx, dy, _ in copies:
            pl.when(has(dx, dy))(copy.start)

    def bytes_of(ref, sem):
        return pltpu.make_async_copy(ref, ref, sem)

    def settle(copies, sem, way):
        def waits(ex, ey):
            rows = sum(r for _, dx, dy, r in copies if (ex == 0 or way * dx != ex) and (ey == 0 or way * dy != ey))
            bytes_of(tally.at[pl.ds(0, rows)], sem).wait()

        def where(at, count):
            return {-1: at == 0, 0: jnp.logical_and(at > 0, at < count - 1), 1: at == count - 1}

        at_x, at_y = where(gx, nx), where(gy, ny)
        inside = jnp.logical_and(at_x[0], at_y[0])
        pl.when(inside)(lambda: waits(0, 0))

        @pl.when(jnp.logical_not(inside))
        def _():
            for ex in (-1, 0, 1):
                for ey in (-1, 0, 1):
                    if (ex, ey) != (0, 0):
                        pl.when(jnp.logical_and(at_x[ex], at_y[ey]))(lambda ex=ex, ey=ey: waits(ex, ey))

    def arrive(copies, which):
        settle(copies, recv_sem.at[which], -1)

    def leave(copies, which):
        settle(copies, send_sem.at[which], 1)

    x_inner = jnp.where(gx > 0, 1.0, 0.0).astype(F32)

    def own_coefs(alpha, bx, by, bz, scale, width):
        n = bx.shape[0]
        col = lax.broadcasted_iota(jnp.int32, bx.shape, 1)
        bz_in = jnp.where(lane_of(bx.shape) < width, 0.0, bz)
        bxu = jnp.concatenate([bx[1:], jnp.zeros_like(bx[:1])], 0)
        byu = jnp.where(col == n - 1, 0.0, roll(by, -1, 1))
        diag = alpha + scale * (bx + bxu + by + byu + bz + roll(bz_in, -width, 2))
        by_in = jnp.where(jnp.logical_and(col == 0, gy == 0), 0.0, by)
        bx_in = jnp.concatenate([bx[:1] * x_inner, bx[1:]], 0)
        return diag, bx_in, by_in, bz_in

    for ref in (part1, land1):
        ref[...] = jnp.zeros(ref.shape, F32)

    pltpu.make_async_copy(raw, raw, load_sem).wait()

    own = pl.ds(HALO, n0)
    diag, bx_in, by_in, bz_in = own_coefs(raw[1], raw[2], raw[3], raw[4], 16.0, 1)
    for i, v in enumerate((by_in, raw[0], diag, bx_in, bz_in)):
        ext0[i, own, own, :] = v

    pl.semaphore_wait(barrier, greeted)
    sent0 = exchange_fine(ext0, n0)
    start(sent0)
    tell(0, *along_x)
    tell(0, *along_y)

    def halves(ref, n):
        return ref[pl.ds(0, n), pl.ds(0, n, stride=2), :], ref[pl.ds(0, n), pl.ds(1, n, stride=2), :]

    def coarsen(alpha, bx, by, bz, pairs, width):
        n = bx.shape[0] // 2

        def xs(v):
            w = v.reshape((n, 2) + v.shape[1:])
            return w[:, 0], w[:, 1]

        def zsum(v):
            return v + roll(v, -width, 2)

        pairs[0, pl.ds(0, n), pl.ds(0, 2 * n)] = zsum(sum(xs(alpha)))
        pairs[1, pl.ds(0, n), pl.ds(0, 2 * n)] = zsum(xs(bx)[0])
        pairs[2, pl.ds(0, n), pl.ds(0, 2 * n)] = zsum(sum(xs(by)))
        pairs[3, pl.ds(0, n), pl.ds(0, 2 * n)] = sum(xs(bz))
        a0, a1 = halves(pairs.at[0], n)
        x0, x1 = halves(pairs.at[1], n)
        y0, _ = halves(pairs.at[2], n)
        z0, z1 = halves(pairs.at[3], n)
        return (a0 + a1) * 0.125, (x0 + x1) * 0.25, y0 * 0.25, (z0 + z1) * 0.25

    alpha1, bx1, by1, bz1 = coarsen(raw[1], raw[2], raw[3], raw[4], pair0, 1)
    diag, bx_in, by_in, bz_in = own_coefs(alpha1, bx1, by1, bz1, 4.0, 2)
    own = pl.ds(HALO, n1)
    lane = lane_of(diag.shape)
    packed1[0, own, own, :] = jnp.where(lane % 2 == 0, diag, roll(bx_in, 1, 2))
    packed1[1, own, own, :] = jnp.where(lane % 2 == 0, by_in, roll(bz_in, 1, 2))

    alpha2, bx2, by2, bz2 = coarsen(alpha1, bx1, by1, bz1, pair1, 2)
    diag, bx_in, by_in, bz_in = own_coefs(alpha2, bx2, by2, bz2, 1.0, 4)
    lane = lane_of(diag.shape) % 4
    mixed = jnp.where(lane < 2, jnp.where(lane == 0, diag, roll(bx_in, 1, 2)), jnp.where(lane == 2, roll(by_in, 2, 2), roll(bz_in, 3, 2)))
    first4 = pl.ds(0, n2)
    coef_blocks[1, gy, :, first4] = mixed

    def edges(dx, dy):
        (sx, tx), (sy, ty) = spans(dx, n1), spans(dy, n1)
        return packed1.at[:, sx, sy], packed1.at[:, tx, ty]

    sent1 = exchange(1, edges)
    start(sent1)

    def border(ref, index, n, value):
        for flag, at in ((gx == 0, 0), (gx == nx - 1, n + HALO)):

            @pl.when(flag)
            def _(at=at):
                ref[index + (pl.ds(at, HALO),)] = value((HALO, n + 2 * HALO, LANES))

        for flag, at in ((gy == 0, 0), (gy == ny - 1, n + HALO)):

            @pl.when(flag)
            def _(at=at):
                ref[index + (slice(None), pl.ds(at, HALO))] = value((n + 2 * HALO, HALO, LANES))

    def zeros(shape):
        return jnp.zeros(shape, F32)

    def ones(every):
        return lambda shape: jnp.where(lane_of(shape) % every == 0, 1.0, 0.0).astype(F32)

    for i in (0, 1, 3, 4):
        border(ext0, (i,), n0, zeros)
    border(ext0, (2,), n0, ones(1))
    border(packed1, (0,), n1, ones(2))
    border(packed1, (1,), n1, zeros)
    for flag, at in ((gx == 0, 0), (gx == nx - 1, 2)):

        @pl.when(flag)
        def _(at=at):
            coef_blocks[at] = zeros(coef_blocks.shape[1:])
            rhs_blocks[at] = zeros(rhs_blocks.shape[1:])

    wide = n2 * (ny // 4)
    line, head, tail = pl.ds(HALO, wide), pl.ds(0, HALO), pl.ds(HALO + wide, HALO)
    for ref in (coef_cols, rhs_cols):
        for part in (head, tail):
            at = (slice(None),) * (len(ref.shape) - 2) + (part,)
            ref[at] = zeros(ref.shape[:-2] + (HALO, LANES))

    told(0, *along_y)
    tell(1, *along_y)

    def whole_diag(part, bx, by, n, scale):
        rows = part.shape[0]
        row = lax.broadcasted_iota(jnp.int32, part.shape, 0)
        col = lax.broadcasted_iota(jnp.int32, part.shape, 1)
        at_x = jnp.logical_or(row == HALO - 1, row == HALO + n - 1)
        at_y = jnp.logical_or(col == HALO - 1, col == HALO + n - 1)
        bxu = jnp.concatenate([bx[1:rows], jnp.zeros_like(bx[:1])], 0)
        return part + scale * (jnp.where(at_x, bxu, 0.0) + jnp.where(at_y, roll(by, -1, 1), 0.0))

    def sweep(number, first, rows, faces, work, width, finish, clip=None):
        coefs = steps()
        source, target = 6 + number % 2, 7 - number % 2

        def body(i, carry):
            at = first + i * rows[1]
            here = pl.ds(at, rows[1])
            x = work[source, here]
            total = faces[0][here] * work[source, pl.ds(at - 1, rows[1])]
            total = total + faces[0][pl.ds(at + 1, rows[1])] * work[source, pl.ds(at + 1, rows[1])]
            total = total + faces[1][here] * roll(x, 1, 1) + work[2, here] * roll(x, -1, 1)
            total = total + faces[2][here] * roll(x, width, 2) + work[3, here] * roll(x, -width, 2)
            if number == 3:
                finish(at, rows[1], work[4, here], work[1, here] - x, work[0, here], total)
            else:
                a, b = coefs[number]
                scaled = work[1, here] - x + work[0, here] * total
                update = a * (x if number == 0 else work[5, here]) + b * scaled
                x = x + update
                if clip is not None:
                    col = lax.broadcasted_iota(jnp.int32, x.shape, 1)
                    x = jnp.where(jnp.logical_and(col >= HALO, col < HALO + clip), x, 0.0)
                work[5, here] = update
                work[target, here] = x
            return carry

        lax.fori_loop(0, rows[0], body, 0, unroll=True)

    def prepare(faces, work, diag, scale, width):
        inverse = 1.0 / diag
        work[0] = scale * inverse
        work[2] = roll(faces[1][...], -1, 1)
        work[3] = roll(faces[2][...], -width, 2)
        work[4] = diag

    def begin(work, rhs, scale):
        work[1] = work[0] * rhs * (1.0 / scale)
        work[6] = work[1] * (1.0 / THETA)

    arrive(sent0, 0)
    told(0, *along_x)
    tell(1, *along_x)
    told(1, *along_y)
    tell(2, *along_y)
    faces0 = (ext0.at[3], ext0.at[0], ext0.at[4])
    prepare(faces0, work0, whole_diag(ext0[2], ext0[3], ext0[0], n0, 16.0), 16.0, 1)
    begin(work0, ext0[1], 16.0)

    def halve(pairs, first, width):
        def finish(at, resid):
            rows = resid.shape[0] // 2
            summed = resid.reshape((rows, 2) + resid.shape[1:])
            summed = summed[:, 0] + summed[:, 1]
            pairs[pl.ds(lax.div(at - first, 2), rows)] = summed + roll(summed, -width, 2)

        return finish

    down0 = pair0.at[4]
    keep0 = halve(down0, 2, 1)

    def partial(at, rows, diag, gap, scaled, total):
        row = at + lax.broadcasted_iota(jnp.int32, gap.shape, 0)
        col = lax.broadcasted_iota(jnp.int32, gap.shape, 1)
        in_x = jnp.logical_and(row >= HALO, row < HALO + n0)
        in_y = jnp.logical_and(col >= HALO, col < HALO + n0)
        near_y = jnp.logical_and(col >= HALO - 2, col < HALO + n0 + 2)
        mine = jnp.where(jnp.logical_and(in_x, in_y), diag * gap, 0.0)
        keep0(at, mine + jnp.where(jnp.logical_or(in_y, jnp.logical_and(in_x, near_y)), 16.0 * total, 0.0))

    sweep(0, 2, (5, 4), faces0, work0, 1, None)
    sweep(1, 3, (3, 6), faces0, work0, 1, None)
    sweep(2, 4, (4, 4), faces0, work0, 1, None, n0)
    for at in (1, HALO + n0):
        work0[7, pl.ds(at, 3)] = jnp.zeros((3,) + work0.shape[2:], F32)
    sweep(3, 2, (5, 4), faces0, work0, 1, partial)
    count = n1 + HALO
    terms = (down0[:, pl.ds(0, count, stride=2), :] + down0[:, pl.ds(1, count, stride=2), :]) * 0.125
    part1[pl.ds(HALO - 1, n1 + 2), pl.ds(HALO - 2, count), :] = terms
    halved = part1[...].reshape(rhs1.shape)
    even = lane_of(send1.shape) % 2 == 0
    send1[...] = jnp.where(even, halved[:, 0], roll(halved[:, 1], 1, 2))

    def outer(dx, dy):
        half = n1 // 2
        sx, tx = {
            0: (pl.ds(1, half + 2), pl.ds(1, half + 2)),
            1: (pl.ds(half, 3), pl.ds(0, 3)),
            -1: (pl.ds(1, 3), pl.ds(half + 1, 3)),
        }[dx]
        wide = HALO + 1
        sy, ty = {
            0: (pl.ds(HALO - 1, n1 + 2), pl.ds(HALO - 1, n1 + 2)),
            1: (pl.ds(n1 + HALO + 1 - wide, wide), pl.ds(HALO + 1 - wide, wide)),
            -1: (pl.ds(HALO - 1, wide), pl.ds(HALO - 1 + n1, wide)),
        }[dy]
        land = land1.at[2 if dx * dy != 0 else 1 if dx != 0 else 0]
        return send1.at[sx, sy], land.at[tx, ty]

    sent2 = exchange(2, outer)
    start(sent2)

    told(2, *along_y)
    mine = coef_blocks.at[1, gy, :, first4]
    for o in range(1, ny):
        pltpu.make_async_remote_copy(
            mine, mine, line_send.at[0], line_recv.at[0], device_id=peer_y(o), device_id_type=MESH
        ).start()

    own = pl.ds(HALO, n0)
    store = pltpu.make_async_copy(work0.at[7, own, own], fine_ref, out_sem)
    store.start()

    arrive(sent1, 1)
    even = lane_of(packed1.shape[1:]) % 2 == 0
    part = jnp.where(even, packed1[0], 1.0)
    coef1[0] = roll(packed1[0], -1, 2)
    coef1[1] = packed1[1]
    coef1[2] = roll(packed1[1], -1, 2)
    faces1 = (coef1.at[0], coef1.at[1], coef1.at[2])
    prepare(faces1, work1, whole_diag(part, coef1[0], coef1[1], n1, 4.0), 4.0, 2)

    arrive(sent2, 2)
    told(1, *along_x)
    tell(2, *along_x)
    summed = send1[...] + land1[0] + land1[1] + land1[2]
    rhs1[:, 0] = summed
    rhs1[:, 1] = roll(summed, -1, 2)
    begin(work1, rhs1[...].reshape(part1.shape), 4.0)
    down1 = pair1.at[4]
    keep1 = halve(down1, HALO, 2)

    def whole(at, rows, diag, gap, scaled, total):
        keep1(at, diag * (gap + scaled * total))

    for number, rows in enumerate(((2, 7), (2, 6), (2, 5), (2, 4))):
        sweep(number, number + 1, rows, faces1, work1, 2, whole)
    rhs2 = (down1[:, pl.ds(HALO, n2, stride=2), :] + down1[:, pl.ds(HALO + 1, n2, stride=2), :]) * 0.125
    lane = lane_of(rhs2.shape[1:]) % 4
    mixed = rhs2[0]
    for i in range(1, n2):
        mixed = jnp.where(lane == i, roll(rhs2[i], i, 1), mixed)
    rhs_blocks[1, gy, first4] = mixed

    mine = rhs_blocks.at[1, gy, first4]
    for dx in (0, 1, -1):

        def spread(dx=dx):
            for o in sorted(range(1 if dx == 0 else 0, ny), key=lambda o: -min(o, ny - o)):
                pltpu.make_async_remote_copy(
                    mine, rhs_blocks.at[1 - dx, gy, first4], line_send.at[3 + dx], line_recv.at[3 + dx],
                    device_id=(gx + dx, lax.rem(gy + o, ny)), device_id_type=MESH,
                ).start()

        if dx == 0:
            spread()
        else:
            pl.when(has(dx, 0))(spread)

    told(2, *along_x)
    tell(3, *along_x)

    others = pl.ds(0, ny - 1)
    bytes_of(coef_blocks.at[1, others, :, first4], line_recv.at[0]).wait()
    passed = []
    for dx in (1, -1):
        src, dst = coef_blocks.at[1, :, :, first4], coef_blocks.at[1 - dx, :, :, first4]
        passed.append(remote(src, dst, line_send.at[(dx + 1) // 2 * 4 + 1], line_recv.at[(dx + 1) // 2 * 4 + 1], dx, 0))
    start(passed)

    def compacted(value, width, shift=0):
        rows = value.reshape((-1, LANES))
        count = LANES // width
        pick = lax.broadcasted_iota(jnp.int32, (LANES, count), 0) == shift + width * lax.broadcasted_iota(jnp.int32, (LANES, count), 1)
        out = jnp.dot(rows, pick.astype(F32), precision=lax.Precision.HIGHEST, preferred_element_type=F32)
        return out.reshape(value.shape[:-1] + (count,))

    own = pl.ds(HALO, n1)
    one_ref[...] = compacted(work1[7, own, own, :], 2)

    residue = lane_of(basis.shape[2:]) % 4

    def grouped(blocks, shift):
        out = None
        for q in range(4):
            moved = roll(blocks[q], q - shift, 1) if q != shift else blocks[q]
            out = moved if out is None else jnp.where(residue == q, moved, out)
        return out

    def joined(ref):
        side = lane_of((ref.shape[0], HALO, LANES)) % 4
        ref[:, head] = jnp.where(side != 0, roll(ref[:, pl.ds(wide, HALO)], 1, 2), 0.0)
        ref[:, tail] = jnp.where(side != 3, roll(ref[:, pl.ds(HALO, HALO)], -1, 2), 0.0)

    for copy, dx, _, _ in passed:
        pl.when(has(-dx, 0))(copy.wait_recv)
    for s in range(3):
        for b in range(ny):
            q, p = divmod(b, ny // 4)
            for i in range(n2):
                coef_cols[s, i, q, pl.ds(HALO + n2 * p, n2)] = coef_blocks[s, b, i, first4]
    for s in range(3):
        for i in range(n2):
            blocks = [coef_cols[s, i, q] * SHRINK for q in range(4)]
            for a, at in enumerate((0, 1, 2, 4)):
                coef2[at, n2 * s + i] = grouped(blocks, a)
    for at in (0, 1, 2, 4):
        joined(coef2.at[at])
    diag, bx_in, by_in = coef2[0], coef2[1], coef2[2]
    row = lax.broadcasted_iota(jnp.int32, diag.shape, 0)
    col = lax.broadcasted_iota(jnp.int32, diag.shape, 1)
    bxu = jnp.concatenate([bx_in[1:], jnp.zeros_like(bx_in[:1])], 0)
    byu = roll(by_in, -1, 1)
    coef2[0] = diag + jnp.where(row % n2 == n2 - 1, bxu, 0.0) + jnp.where(col % n2 == n2 - 1, byu, 0.0)
    coef2[3] = byu
    coef2[5] = roll(coef2[4], -4, 2)

    bytes_of(rhs_blocks.at[1, others, first4], line_recv.at[3]).wait()
    for s in (1, 0, 2):
        if s != 1:
            arriving = bytes_of(rhs_blocks.at[s, :, first4], line_recv.at[4 - s])
            pl.when(has(s - 1, 0))(arriving.wait)
        for b in range(ny):
            q, p = divmod(b, ny // 4)
            rhs_cols[s, q, pl.ds(HALO + n2 * p, n2)] = rhs_blocks[s, b, first4]
        blocks = [rhs_cols[s, q] for q in range(4)]
        for i in range(n2):
            basis[0, n2 * s + i] = grouped(blocks, i)
    joined(basis.at[0])
    for number in range(4):
        first, last = number + 1, n2 + 2 * HALO - number - 1
        here = pl.ds(first, last - first)
        x = basis[number, here]
        total = coef2[1, here] * basis[number, pl.ds(first - 1, last - first)]
        total = total + coef2[1, pl.ds(first + 1, last - first)] * basis[number, pl.ds(first + 1, last - first)]
        total = total + coef2[2, here] * roll(x, 1, 1) + coef2[3, here] * roll(x, -1, 1)
        total = total + coef2[4, here] * roll(x, 4, 2) + coef2[5, here] * roll(x, -4, 2)
        basis[number + 1, here] = coef2[0, here] * x - total

    own = pl.ds(HALO, n2)
    vectors = [basis[i, own] for i in range(5)]
    col = lax.broadcasted_iota(jnp.int32, basis.shape[2:], 0)
    inner_cols = jnp.logical_and(col >= HALO, col < HALO + wide)
    lane = lane_of((1, LANES))
    row = jnp.zeros((1, LANES), F32)
    for k in range(9):
        product = jnp.where(inner_cols, jnp.sum(vectors[k // 2] * vectors[(k + 1) // 2], axis=0), 0.0)
        moment = jnp.sum(jnp.sum(product, axis=0, keepdims=True), axis=1, keepdims=True)
        row = jnp.where(lane == k, moment, row)

    def all_sum(row, slots, k, peer):
        slots[0] = row
        count = slots.shape[0] - 1
        for o in sorted(range(1, count + 1), key=lambda o: -min(o, count + 1 - o)):
            pltpu.make_async_remote_copy(
                slots.at[0], slots.at[o], row_send.at[k], row_recv.at[k], device_id=peer(o), device_id_type=MESH
            ).start()
        meanwhile()
        others = slots.at[pl.ds(1, count)]
        bytes_of(others, row_recv.at[k]).wait()
        total = slots[...]
        while total.shape[0] > 1:
            half = total.shape[0] // 2
            total = total[:half] + total[half:]
        return total[0], bytes_of(others, row_send.at[k])

    def meanwhile():
        for which, copies in enumerate((sent0, sent1, sent2)):
            leave(copies, which)
        for copy, dx, _, _ in passed:
            pl.when(has(dx, 0))(copy.wait_send)
        for dx in (1, -1):
            pl.when(has(dx, 0))(bytes_of(rhs_blocks.at[1, :, first4], line_send.at[3 + dx]).wait)
        bytes_of(rhs_blocks.at[1, others, first4], line_send.at[3]).wait()
        bytes_of(coef_blocks.at[1, others, :, first4], line_send.at[0]).wait()
        store.wait()

    told(3, *along_x)
    row, sent5 = all_sum(row, gather_x, 0, peer_x)
    moments = [jnp.sum(jnp.where(lane == k, row, 0.0), axis=1, keepdims=True) for k in range(9)]

    def balanced(terms):
        while len(terms) > 1:
            pairs = [a + b for a, b in zip(terms[0::2], terms[1::2])]
            terms = pairs + terms[2 * len(pairs) :]
        return terms[0]

    def inner(u, w):
        return balanced([
            a * balanced([b * moments[i + j] for j, b in enumerate(w) if b is not None])
            for i, a in enumerate(u) if a is not None
        ])

    def plus(u, c, w):
        out = []
        for a, b in zip(u, w):
            term = None if b is None else c * b
            out.append(a if term is None else term if a is None else a + term)
        return out

    def applied(u):
        return [None] + [None if a is None else a * (1.0 / SHRINK) for a in u[:-1]]

    shadow = [jnp.ones((1, 1), F32), None, None, None, None]
    solved = [None] * 5
    resid = direction = shadow
    rho = moments[0]
    for number in range(BICG):
        image = applied(direction)
        step = rho / inner(shadow, image)
        half = plus(resid, -step, image)
        turned = applied(half)
        omega = inner(turned, half) / inner(turned, turned)
        solved = plus(plus(solved, step, direction), omega, half)
        if number + 1 < BICG:
            resid = plus(half, -omega, turned)
            rho_next = inner(shadow, resid)
            factor = (rho_next / rho) * (step / omega)
            direction = plus(resid, factor, plus(direction, -omega, image))
            rho = rho_next

    total = None
    for i, c in enumerate(solved):
        if c is not None:
            term = c * vectors[i]
            total = term if total is None else total + term
    group, place = lax.div(gy, ny // 4), lax.rem(gy, ny // 4)
    mine = compacted(total, 4, group)[:, HALO:]
    bottom = mine[:, :n2]
    for p in range(1, ny // 4):
        bottom = jnp.where(place == p, mine[:, n2 * p : n2 * (p + 1)], bottom)
    bottom_ref[...] = bottom
    sent5.wait()


def per_device(right_side, alpha_cells, beta_x, beta_y, beta_z):
    nx, ny = lax.axis_size("gx"), lax.axis_size("gy")
    n0, _, nz = right_side.shape
    n1, n2 = n0 // 2, n0 // 4
    e0, e1, e2 = n0 + 2 * HALO, n1 + 2 * HALO, n2 + 2 * HALO
    anywhere = pl.BlockSpec(memory_space=pl.ANY)
    vmem = pl.BlockSpec(memory_space=pltpu.VMEM)

    def body(*refs):
        kernel(nx, ny, *refs)

    return pl.pallas_call(
        body,
        out_shape=(
            pltpu.VMEM((n0, n0, nz), F32),
            pltpu.VMEM((n1, n1, nz // 2), F32),
            pltpu.VMEM((n2, n2, nz // 4), F32),
        ),
        in_specs=[anywhere] * 5,
        out_specs=(vmem,) * 3,
        scratch_shapes=[
            pltpu.VMEM((5, n0, n0, nz), F32),
            pltpu.VMEM((5, e0, e0, nz), F32),
            pltpu.VMEM((8, e0, e0, nz), F32),
            pltpu.VMEM((5, n1 + 2, e0, nz), F32),
            pltpu.VMEM((2, e1, e1, nz), F32),
            pltpu.VMEM((3, e1, e1, nz), F32),
            pltpu.VMEM((8, e1, e1, nz), F32),
            pltpu.VMEM((e1 // 2, 2, e1, nz), F32),
            pltpu.VMEM((e1, e1, nz), F32),
            pltpu.VMEM((e1 // 2, e1, nz), F32),
            pltpu.VMEM((3, e1 // 2, e1, nz), F32),
            pltpu.VMEM((5, n2, e1, nz), F32),
            pltpu.VMEM((3, ny, n2, 8, nz), F32),
            pltpu.VMEM((3, n2, 4, 24, nz), F32),
            pltpu.VMEM((6, e2, 24, nz), F32),
            pltpu.VMEM((3, ny, 8, nz), F32),
            pltpu.VMEM((3, 4, 24, nz), F32),
            pltpu.VMEM((5, e2, 24, nz), F32),
            pltpu.VMEM((nx, 1, nz), F32),
            pltpu.VMEM((1024, nz), F32),
            pltpu.SemaphoreType.DMA,
            pltpu.SemaphoreType.DMA,
            pltpu.SemaphoreType.DMA((3,)),
            pltpu.SemaphoreType.DMA((3,)),
            pltpu.SemaphoreType.DMA((6,)),
            pltpu.SemaphoreType.DMA((6,)),
            pltpu.SemaphoreType.DMA((1,)),
            pltpu.SemaphoreType.DMA((1,)),
            pltpu.SemaphoreType.REGULAR((4,)),
            pltpu.SemaphoreType.REGULAR((4,)),
        ],
        compiler_params=pltpu.CompilerParams(collective_id=0, has_side_effects=True, vmem_limit_bytes=60 * 2**20),
        cost_estimate=pl.CostEstimate(flops=40_000_000, bytes_accessed=800_000, transcendentals=0),
        name="vcycle_down",
    )(right_side, alpha_cells, beta_x, beta_y, beta_z)


def solution(mesh):
    placed = P("gx", "gy", None)
    return jax.shard_map(per_device, mesh=mesh, in_specs=(placed,) * 5, out_specs=(placed,) * 3, check_vma=False)
```
